32 devices in a mesh: groups: 2 (over y), expert: 4 (over z), dp: 4 (over x, core).
Axes of the slice: x: 2, y: 2, z: 4, core: 2. Of those that a mesh axis runs over, the one named last changes fastest.
Arguments:
- hidden_rows: bfloat16 [256, 4096], P(('groups', 'expert', 'dp')), parts along dimension 0, may hold values from -6 to 6
- expert_ids: int32 [256, 8], P(('groups', 'expert', 'dp')), parts along dimension 0, may hold values from 0 to 15, as said below
- gate_values: float32 [256, 8], P(('groups', 'expert', 'dp')), parts along dimension 0, may hold values from 0.1 to 0.6
- gate_proj: bfloat16 [16, 4096, 1024], P('expert', None, 'dp'), may hold values from -0.09375 to 0.09375
- up_proj: bfloat16 [16, 4096, 1024], P('expert', None, 'dp'), may hold values from -0.09375 to 0.09375
- down_proj: bfloat16 [16, 1024, 4096], P('expert', None, 'dp'), may hold values from -0.1875 to 0.1875
- queries: bfloat16 [64, 128, 576], P(('groups', 'expert', 'dp')), parts along dimension 0, may hold values from -16 to 16
- latent_cache: bfloat16 [64, 512, 576], P(('groups', 'expert', 'dp')), parts along dimension 0, may hold values from -8 to 8
- cache_lengths: int32 [64], P(('groups', 'expert', 'dp')), parts along dimension 0, may hold values from 2 to 512, as said below
Outputs:
- mixed_rows: bfloat16 [256, 4096], P(('groups', 'expert', 'dp')), parts along dimension 0
- attention_latent: bfloat16 [64, 128, 512], P(('groups', 'expert', 'dp')), parts along dimension 0
The draws below stay inside these ranges and needn't reach their ends.
There are 2 independent parts, one for each index of `groups`. The reference program is written for one: setup_inputs(seed, part) draws one part's arguments, and reference() takes and returns one part's arrays. A program takes and returns all parts, laid end to end along the dimension named above; an argument that names none is the same for every part. Nothing has to cross between parts.
Inputs may be any that keep to these rules, and one draw needn't show every extreme that they name: `expert_ids`: each row names 8 different experts. Within the rows of one device (aligned blocks of 8 rows) no expert is named by more than 6 rows, and one expert, the same for every block, is named by exactly 6 rows in each block. `cache_lengths`: some row has length 512.
All inputs are finite; a program needn't handle non-finite values.
Results may differ from the reference program's by a relative error of at most 0.0057.
Values may be sent and summed in bfloat16 or wider, within the bound.
No kernel may reach another device: no remote copies, remote signals or barrier semaphores. Data moves between devices by JAX's collectives and lax.ppermute only.
A program may use at most 128 MiB of HBM per device.

```python
import jax
import jax.numpy as jnp
from jax import lax

D = 4096
FF = 1024
HEADS = 128
LATENT = 512
QK = 576
TOP = 8
ROWS_DEV = 8
CTX = 512
EXPERTS = 16
CAP = 6
TOKENS = 128
ATT_TOKENS = 32


def draw_expert_ids(key, part):
    key = jax.random.fold_in(key, 11)
    block_count = TOKENS // ROWS_DEV
    hot_expert = jax.random.randint(jax.random.fold_in(key, 1), (), 0, EXPERTS).astype(jnp.int32)
    block_keys = jax.random.split(jax.random.fold_in(key, 2), block_count)

    def one_block(block_key):
        first_key, second_key, third_key = jax.random.split(block_key, 3)
        capacity_units = jax.random.permutation(first_key, (EXPERTS - 1) * CAP)
        chosen = (capacity_units[:ROWS_DEV * TOP - CAP] // CAP).astype(jnp.int32)
        chosen = chosen + (chosen >= hot_expert).astype(jnp.int32)
        pool_sorted = jnp.sort(jnp.concatenate([jnp.full((CAP,), hot_expert, jnp.int32), chosen]))
        assigned = pool_sorted.reshape(TOP, ROWS_DEV).T
        row_order = jax.random.permutation(second_key, ROWS_DEV)
        assigned = assigned[row_order]
        scores = jax.random.randint(third_key, (ROWS_DEV, TOP), 0, 1 << 20) * TOP + jnp.arange(TOP, dtype=jnp.int32)[None, :]
        shuffle = jnp.argsort(scores, axis=1)
        return jnp.take_along_axis(assigned, shuffle, axis=1)
    return jax.vmap(one_block)(block_keys).reshape(TOKENS, TOP).astype(jnp.int32)


def draw_cache_lengths(key, part):
    key = jax.random.fold_in(key, 12)
    first_key, second_key = jax.random.split(key)
    lengths = jax.random.randint(first_key, (ATT_TOKENS,), 2, CTX + 1)
    long_row = jax.random.randint(second_key, (), 0, ATT_TOKENS)
    return lengths.at[long_row].set(CTX).astype(jnp.int32)


def draw_queries(key, part):
    key = jax.random.fold_in(key, 13)
    first_key = jax.random.fold_in(key, 0)
    drawn = jnp.clip(jax.random.normal(first_key, (ATT_TOKENS, HEADS, QK), jnp.float32), -6.0, 6.0)
    return drawn.astype(jnp.bfloat16)


def draw_latent_cache(key, part):
    key = jax.random.fold_in(key, 14)
    first_key = jax.random.fold_in(key, 0)
    drawn = jnp.clip(jax.random.normal(first_key, (ATT_TOKENS, CTX, QK), jnp.float32), -6.0, 6.0)
    return drawn.astype(jnp.bfloat16)


def block_scale(rng, extent, shards, smallest, top_value):
    factor_of, own = 1.0, jax.random.fold_in(rng, 6)
    for dim, shards_of in shards:
        steps = jnp.exp(jax.random.uniform(jax.random.fold_in(own, dim), (shards_of,), jnp.float32, smallest / len(shards), top_value / len(shards)))
        factor_of = factor_of * jnp.repeat(steps, extent[dim] // shards_of).reshape([-1 if axis == dim else 1 for axis in range(len(extent))])
    return factor_of


def scatter_about(key, extent, scale, limit, cuts=(), kind=jnp.bfloat16):
    values = scale * jax.random.normal(key, extent, jnp.float32)
    if cuts:
        values = values * block_scale(key, extent, cuts, -0.22, 0.18)
    return jnp.clip(values, -limit, limit).astype(kind)


def setup_inputs(seed: int = 0, part: int = 0) -> dict:
    keys = jax.random.split(jax.random.key(seed), 10)
    own_keys = jax.random.split(jax.random.fold_in(keys[9], part), 10)
    return {
        "hidden_rows": scatter_about(own_keys[0], (TOKENS, D), 1.0, 6.0, ((0, 16),)),
        "expert_ids": draw_expert_ids(jax.random.fold_in(jax.random.fold_in(keys[9], part), 71), part),
        "gate_values": jnp.clip(0.1 + 0.5 * jax.random.uniform(own_keys[2], (TOKENS, TOP), jnp.float32) ** block_scale(own_keys[2], (TOKENS, TOP), ((0, 16),), -0.2, 0.2), 0.1, 0.6),
        "gate_proj": scatter_about(keys[3], (EXPERTS, D, FF), D ** -0.5, 0.09375, ((0, 4), (2, 4))),
        "up_proj": scatter_about(keys[4], (EXPERTS, D, FF), D ** -0.5, 0.09375, ((0, 4), (2, 4))),
        "down_proj": scatter_about(keys[5], (EXPERTS, FF, D), FF ** -0.5, 0.1875, ((0, 4), (2, 4))),
        "queries": draw_queries(jax.random.fold_in(jax.random.fold_in(keys[9], part), 71), part),
        "latent_cache": draw_latent_cache(jax.random.fold_in(jax.random.fold_in(keys[9], part), 71), part),
        "cache_lengths": draw_cache_lengths(jax.random.fold_in(jax.random.fold_in(keys[9], part), 71), part),
    }


softmax_scale = 192.0 ** -0.5


def expert_block(row_block, gate_matrix, up_matrix, down_matrix):
    gate_pre = jnp.dot(row_block, gate_matrix, preferred_element_type=jnp.float32)
    up_pre = jnp.dot(row_block, up_matrix, preferred_element_type=jnp.float32)
    hidden = (jax.nn.silu(gate_pre) * up_pre).astype(jnp.bfloat16)
    return jnp.dot(hidden, down_matrix, preferred_element_type=jnp.float32).astype(jnp.bfloat16)


def mixture(hidden_rows, expert_ids, gate_values, gate_proj, up_proj, down_proj):
    block_count = TOKENS // ROWS_DEV
    row_blocks = hidden_rows.reshape(block_count, ROWS_DEV, D)
    routes = expert_ids.reshape(block_count, ROWS_DEV, TOP)
    weighting = gate_values.reshape(block_count, ROWS_DEV, TOP)
    slot_range = jnp.arange(CAP, dtype=jnp.int32)
    row_range = jnp.arange(ROWS_DEV, dtype=jnp.int32)

    def per_expert(running, expert_index):
        matches = routes == expert_index
        naming = jnp.sum(matches.astype(jnp.int32), axis=2).astype(jnp.int32)
        share_weight = jnp.sum(jnp.where(matches, weighting, 0.0), axis=2)
        before = (jnp.cumsum(naming, axis=1) - naming).astype(jnp.int32)
        slot_hit = (naming[:, :, None] == 1) & (before[:, :, None] == slot_range[None, None, :])
        source_row = jnp.sum(jnp.where(slot_hit, row_range[None, :, None], 0), axis=1).astype(jnp.int32)
        picked = jnp.take_along_axis(row_blocks, source_row[:, :, None], axis=1)
        outputs = expert_block(picked.reshape(block_count * CAP, D), gate_proj[expert_index],
                               up_proj[expert_index], down_proj[expert_index]).reshape(block_count, CAP, D)
        slot_index = jnp.minimum(before, CAP - 1).astype(jnp.int32)
        returned = jnp.take_along_axis(outputs, slot_index[:, :, None], axis=1)
        return running + share_weight[:, :, None] * returned.astype(jnp.float32), None

    zeroed = jnp.zeros((block_count, ROWS_DEV, D), jnp.float32)
    running, _ = lax.scan(per_expert, zeroed, jnp.arange(EXPERTS, dtype=jnp.int32))
    return running.reshape(TOKENS, D).astype(jnp.bfloat16)


def attention(queries, latent_cache, cache_lengths):
    def one_row(operands):
        query_row, cache_row, length = operands
        scores = jnp.dot(query_row, cache_row.T, preferred_element_type=jnp.float32) * softmax_scale
        usable = jnp.arange(CTX, dtype=jnp.int32) < length
        scores = jnp.where(usable[None, :], scores, -1e30)
        highest = jnp.max(scores, axis=1, keepdims=True)
        weights = jnp.exp(scores - highest)
        weights = weights / jnp.sum(weights, axis=1, keepdims=True)
        return jnp.dot(weights.astype(jnp.bfloat16), cache_row[:, :LATENT],
                       preferred_element_type=jnp.float32).astype(jnp.bfloat16)

    return lax.map(one_row, (queries, latent_cache, cache_lengths))


def reference(hidden_rows, expert_ids, gate_values, gate_proj, up_proj, down_proj, queries, latent_cache, cache_lengths):
    mixed_rows = mixture(hidden_rows, expert_ids, gate_values, gate_proj, up_proj, down_proj)
    attention_latent = attention(queries, latent_cache, cache_lengths)
    return (mixed_rows, attention_latent)
```

```python
import jax
import jax.numpy as jnp
from jax import lax
from jax.experimental import pallas as pl
from jax.experimental.pallas import tpu as pltpu
from jax.sharding import PartitionSpec as P

LATENT = 512
F32 = jnp.float32
BF16 = jnp.bfloat16
VMEM = pltpu.VMEM
MIB = 1024 * 1024


softmax_scale = 192.0 ** (-0.5)


def attend_kernel(lengths_ref, queries_ref, cache_ref, out_ref):
    length = lengths_ref[pl.program_id(0)]
    cache = cache_ref[0]
    scores = (
        lax.dot_general(
            queries_ref[0], cache, (((1,), (1,)), ((), ())), preferred_element_type=F32
        )
        * softmax_scale
    )
    usable = lax.broadcasted_iota(jnp.int32, scores.shape, 1) < length
    scores = jnp.where(usable, scores, -1e30)
    weights = jnp.exp(scores - jnp.max(scores, axis=1, keepdims=True))
    weights = weights / jnp.sum(weights, axis=1, keepdims=True)
    out_ref[0] = jnp.dot(
        weights.astype(BF16), cache[:, :LATENT], preferred_element_type=F32
    ).astype(BF16)


def attend(queries, latent_cache, cache_lengths):
    rows, heads, width = queries.shape
    positions = latent_cache.shape[1]
    return pl.pallas_call(
        attend_kernel,
        grid_spec=pltpu.PrefetchScalarGridSpec(
            num_scalar_prefetch=1,
            grid=(rows,),
            in_specs=[
                pl.BlockSpec((1, heads, width), lambda r, n: (r, 0, 0)),
                pl.BlockSpec((1, positions, width), lambda r, n: (r, 0, 0)),
            ],
            out_specs=pl.BlockSpec((1, heads, LATENT), lambda r, n: (r, 0, 0)),
        ),
        out_shape=jax.ShapeDtypeStruct((rows, heads, LATENT), BF16),
        compiler_params=pltpu.CompilerParams(vmem_limit_bytes=16 * MIB),
        cost_estimate=pl.CostEstimate(
            flops=2 * rows * heads * positions * (width + LATENT),
            bytes_accessed=2 * rows * (positions * width + heads * (width + LATENT)),
            transcendentals=rows * heads * positions,
        ),
    )(cache_lengths, queries, latent_cache)


def gate_table(expert_ids, gate_values, experts_all):
    chosen = expert_ids[:, :, None] == jnp.arange(experts_all, dtype=jnp.int32)[None, None, :]
    return jnp.sum(jnp.where(chosen, gate_values[:, :, None], 0.0), axis=1)


def in_parts(table):
    high = table.astype(BF16)
    rest = table - high.astype(F32)
    middle = rest.astype(BF16)
    low = (rest - middle.astype(F32)).astype(BF16)
    return [high, middle, low]


def gate_up_kernel(rows_ref, gate_ref, up_ref, out_ref):
    rows = rows_ref[...]
    for e in range(gate_ref.shape[0]):
        gate = jnp.dot(rows, gate_ref[e], preferred_element_type=F32)
        up = jnp.dot(rows, up_ref[e], preferred_element_type=F32)
        out_ref[e] = (gate / (1.0 + jnp.exp(-gate)) * up).astype(BF16)


def gate_up(rows, gate_proj, up_proj):
    experts, depth, share = gate_proj.shape
    whole = pl.BlockSpec(memory_space=VMEM)
    return pl.pallas_call(
        gate_up_kernel,
        in_specs=[whole] * 3,
        out_specs=whole,
        out_shape=jax.ShapeDtypeStruct((experts, rows.shape[0], share), BF16),
        compiler_params=pltpu.CompilerParams(vmem_limit_bytes=40 * MIB),
        cost_estimate=pl.CostEstimate(
            flops=4 * experts * rows.shape[0] * depth * share,
            bytes_accessed=4 * experts * depth * share,
            transcendentals=experts * rows.shape[0] * share,
        ),
    )(
        rows,
        pltpu.with_memory_space_constraint(gate_proj, VMEM),
        pltpu.with_memory_space_constraint(up_proj, VMEM),
    )


def swap_halves(value, half):
    pieces = []
    for start in range(0, value.shape[0], 2 * half):
        pieces.append(value[start + half : start + 2 * half])
        pieces.append(value[start : start + half])
    return jnp.concatenate(pieces, axis=0)


def down_kernel(place_ref, table_ref, h0_ref, h1_ref, h2_ref, h3_ref, down_ref, *out_refs):
    place = place_ref[0]
    share = h0_ref.shape[2]
    width = down_ref.shape[2]
    tile = 256
    rows_z = out_refs[0].shape[0]
    experts = down_ref.shape[0]
    for start in range(0, width, tile):
        total = jnp.zeros((h0_ref.shape[1], tile), F32)
        for e in range(experts):
            made = jnp.zeros((h0_ref.shape[1], tile), F32)
            for k, ref in enumerate((h0_ref, h1_ref, h2_ref, h3_ref)):
                hidden = ref[e]
                if k >= 2:
                    hidden = swap_halves(hidden, rows_z // 2)
                owner = jnp.bitwise_xor(place, k)
                weights = down_ref[e, pl.ds(pl.multiple_of(owner * share, share), share), start : start + tile]
                made += jnp.dot(hidden, weights, preferred_element_type=F32)
            total += table_ref[:, e : e + 1] * made.astype(BF16).astype(F32)
        done = total.astype(BF16)
        for k, ref in enumerate(out_refs):
            ref[:, start : start + tile] = done[k * rows_z : (k + 1) * rows_z]


def down(place, table, hidden, down_proj):
    experts, depth, width = down_proj.shape
    rows = hidden[0].shape[1]
    whole = pl.BlockSpec(memory_space=VMEM)
    return pl.pallas_call(
        down_kernel,
        in_specs=[pl.BlockSpec(memory_space=pltpu.SMEM)] + [whole] * 6,
        out_specs=[whole] * 4,
        out_shape=[jax.ShapeDtypeStruct((rows // 4, width), BF16)] * 4,
        compiler_params=pltpu.CompilerParams(vmem_limit_bytes=40 * MIB),
        cost_estimate=pl.CostEstimate(
            flops=2 * experts * rows * depth * width,
            bytes_accessed=2 * experts * depth * width,
            transcendentals=0,
        ),
    )(place, table, *hidden, pltpu.with_memory_space_constraint(down_proj, VMEM))


def swap(value, axis, bit):
    size = lax.axis_size(axis)
    return lax.ppermute(value, axis, [(i, i ^ bit) for i in range(size)])


def routed_four(hidden_rows, expert_ids, gate_values, gate_proj, up_proj, down_proj):
    rows_dev, feature_count = hidden_rows.shape
    local_experts = gate_proj.shape[0]
    width = down_proj.shape[2]
    experts_all = local_experts * 4
    layer = lax.axis_index("expert")
    place = lax.axis_index("dp")
    core = place % 2
    x_side = place // 2

    parts = in_parts(gate_table(expert_ids, gate_values, experts_all))
    pad = -3 * experts_all % 128
    sent = jnp.concatenate([hidden_rows] + parts + [jnp.zeros((rows_dev, pad), BF16)], axis=1)
    total_width = sent.shape[1]
    along_z = [sent] + [swap(sent, "expert", k) for k in (1, 2, 3)]
    along_x = [swap(block, "dp", 2) for block in along_z]
    mine = jnp.stack([jnp.stack(along_z), jnp.stack(along_x)], axis=1)
    other_z = swap(jnp.stack(along_z), "dp", 1)
    other_x = swap(jnp.stack(along_x), "dp", 1)
    other = jnp.stack([other_z, other_x], axis=1)
    gathered = jnp.where(
        core == 0, jnp.stack([mine, other], axis=2), jnp.stack([other, mine], axis=2)
    ).reshape(16 * rows_dev, total_width)
    rows = gathered[:, :feature_count]
    coded = gathered[:, feature_count : feature_count + 3 * experts_all].astype(F32)
    table = coded[:, :experts_all] + coded[:, experts_all : 2 * experts_all] + coded[:, 2 * experts_all :]
    table = lax.dynamic_slice_in_dim(table, layer * local_experts, local_experts, axis=1)

    hidden = gate_up(rows, gate_proj, up_proj)
    hidden_x = swap(hidden, "dp", 2)
    hidden_c = swap(hidden, "dp", 1)
    hidden_xc = swap(hidden_x, "dp", 1)
    partial = down(
        place.astype(jnp.int32).reshape(1),
        table,
        (hidden, hidden_c, hidden_x, hidden_xc),
        down_proj,
    )
    arrived = [partial[0]] + [swap(partial[k], "expert", k) for k in (1, 2, 3)]
    summed = sum(block.astype(F32) for block in arrived).astype(BF16)
    summed = summed.reshape(2, 2, rows_dev, width)
    both = jnp.stack([summed[0], swap(summed[1], "dp", 2)])
    kept = jnp.where(core == 0, both[:, 0], both[:, 1])
    given = jnp.where(core == 0, both[:, 1], both[:, 0])
    taken = swap(given, "dp", 1)
    by_core = jnp.where(core == 0, jnp.stack([kept, taken], 1), jnp.stack([taken, kept], 1))
    by_place = jnp.where(x_side == 0, by_core, by_core[::-1]).reshape(4, rows_dev, width)
    return jnp.transpose(by_place, (1, 0, 2)).reshape(rows_dev, 4 * width)


def routed_any(hidden_rows, expert_ids, gate_values, gate_proj, up_proj, down_proj):
    rows_dev, feature_count = hidden_rows.shape
    local_experts = gate_proj.shape[0]
    width = down_proj.shape[2]
    owners = lax.axis_size("expert")
    members = lax.axis_size("dp")
    experts_all = local_experts * owners
    table = gate_table(expert_ids, gate_values, experts_all)
    rows = lax.all_gather(hidden_rows, ("expert", "dp"), axis=0, tiled=True)
    table = lax.all_gather(table, ("expert", "dp"), axis=0, tiled=True)
    table = lax.dynamic_slice_in_dim(
        table, lax.axis_index("expert") * local_experts, local_experts, axis=1
    )
    total = jnp.zeros((rows.shape[0], width), F32)
    for e in range(local_experts):
        gate = jnp.dot(rows, gate_proj[e], preferred_element_type=F32)
        up = jnp.dot(rows, up_proj[e], preferred_element_type=F32)
        share = (jax.nn.silu(gate) * up).astype(BF16)
        hidden = lax.all_gather(share, "dp", axis=1, tiled=True)
        made = jnp.dot(hidden, down_proj[e], preferred_element_type=F32).astype(BF16)
        total += table[:, e : e + 1] * made.astype(F32)
    partial = total.astype(BF16).reshape(owners, members, rows_dev, width)
    returned = lax.all_to_all(
        lax.all_to_all(partial, "expert", split_axis=0, concat_axis=0, tiled=True),
        "dp",
        split_axis=1,
        concat_axis=1,
        tiled=True,
    )
    blended = jnp.sum(returned.astype(F32), axis=0).astype(BF16)
    return jnp.transpose(blended, (1, 0, 2)).reshape(rows_dev, members * width)


def local(
    hidden_rows,
    expert_ids,
    gate_values,
    gate_proj,
    up_proj,
    down_proj,
    queries,
    latent_cache,
    cache_lengths,
):
    attended = attend(queries, latent_cache, cache_lengths)
    four = lax.axis_size("expert") == 4 and lax.axis_size("dp") == 4
    routed = routed_four if four else routed_any
    blended = routed(hidden_rows, expert_ids, gate_values, gate_proj, up_proj, down_proj)
    return (blended, attended)


def solution(mesh):
    return jax.shard_map(
        local,
        mesh=mesh,
        in_specs=(
            P(("groups", "expert", "dp"), None),
            P(("groups", "expert", "dp"), None),
            P(("groups", "expert", "dp"), None),
            P("expert", None, "dp"),
            P("expert", None, "dp"),
            P("expert", None, "dp"),
            P(("groups", "expert", "dp"), None, None),
            P(("groups", "expert", "dp"), None, None),
            P(("groups", "expert", "dp")),
        ),
        out_specs=(P(("groups", "expert", "dp"), None), P(("groups", "expert", "dp"), None, None)),
        check_vma=False,
    )
```

```python
import jax
import jax.numpy as jnp
from jax import lax
from jax.experimental import pallas as pl
from jax.experimental.pallas import tpu as pltpu
from jax.sharding import PartitionSpec as P

LATENT = 512
F32 = jnp.float32
BF16 = jnp.bfloat16
VMEM = pltpu.VMEM
MIB = 1024 * 1024


softmax_scale = 192.0 ** (-0.5)


def attend_rows(lengths_ref, queries_ref, cache_ref, out_ref):
    for r in range(queries_ref.shape[0]):
        queries = queries_ref[r].T
        cache = cache_ref[r]
        scores = jnp.dot(queries, cache, preferred_element_type=F32) * softmax_scale
        usable = lax.broadcasted_iota(jnp.int32, scores.shape, 1) < lengths_ref[r]
        scores = jnp.where(usable, scores, -1e30)
        weights = jnp.exp(scores - jnp.max(scores, axis=1, keepdims=True))
        weights = weights / jnp.sum(weights, axis=1, keepdims=True)
        out_ref[r] = lax.dot_general(
            weights.astype(BF16),
            cache[:LATENT],
            (((1,), (1,)), ((), ())),
            preferred_element_type=F32,
        ).astype(BF16)


def attend_cost(queries, latent_cache):
    rows, heads, width = queries.shape
    positions = latent_cache.shape[1]
    return pl.CostEstimate(
        flops=2 * rows * heads * positions * (width + LATENT),
        bytes_accessed=2 * rows * (positions * width + heads * (width + LATENT)),
        transcendentals=rows * heads * positions,
    )


def in_hbm(array):
    return pltpu.with_memory_space_constraint(array, pltpu.HBM)


def in_vmem(array):
    return pltpu.with_memory_space_constraint(array, VMEM)


def whole(space=VMEM):
    return pl.BlockSpec(memory_space=space)


def attend(queries, latent_cache, cache_lengths):
    rows, heads, _ = queries.shape
    return pl.pallas_call(
        attend_rows,
        in_specs=[whole(pltpu.SMEM), whole(), whole()],
        out_specs=whole(),
        out_shape=jax.ShapeDtypeStruct((rows, heads, LATENT), BF16),
        compiler_params=pltpu.CompilerParams(vmem_limit_bytes=16 * MIB),
        cost_estimate=attend_cost(queries, latent_cache),
    )(cache_lengths, jnp.swapaxes(queries, 1, 2), jnp.swapaxes(latent_cache, 1, 2))


def attend_and_fetch_kernel(
    lengths_ref, queries_ref, cache_ref, source_ref, after_ref, out_ref, held_ref, sem
):
    copy = pltpu.make_async_copy(source_ref, held_ref, sem)
    copy.start()
    attend_rows(lengths_ref, queries_ref, cache_ref, out_ref)
    copy.wait()


def attend_and_fetch(queries, latent_cache, cache_lengths, weights, after):
    rows, heads, _ = queries.shape
    return pl.pallas_call(
        attend_and_fetch_kernel,
        in_specs=[whole(pltpu.SMEM), whole(), whole(), whole(pltpu.HBM), whole(pl.ANY)],
        out_specs=[whole(), whole()],
        out_shape=[
            jax.ShapeDtypeStruct((rows, heads, LATENT), BF16),
            VMEM(weights.shape, weights.dtype),
        ],
        scratch_shapes=[pltpu.SemaphoreType.DMA],
        compiler_params=pltpu.CompilerParams(vmem_limit_bytes=12 * MIB),
        cost_estimate=attend_cost(queries, latent_cache),
    )(
        cache_lengths,
        jnp.swapaxes(queries, 1, 2),
        jnp.swapaxes(latent_cache, 1, 2),
        in_hbm(weights),
        after,
    )


def once_done(value, other):
    return pl.pallas_call(
        lambda *refs: None,
        in_specs=[whole(pl.ANY)] * 2,
        out_specs=whole(pl.ANY),
        out_shape=VMEM(value.shape, value.dtype),
        input_output_aliases={0: 0},
        compiler_params=pltpu.CompilerParams(vmem_limit_bytes=MIB),
        cost_estimate=pl.CostEstimate(flops=0, bytes_accessed=0, transcendentals=0),
    )(value, other)


def fetch_kernel(source_ref, *refs):
    count = len(refs) - 3
    piece_refs, (held_ref, stack_ref, sems) = refs[:count], refs[count:]
    copies = [
        pltpu.make_async_copy(source_ref.at[e], held_ref.at[e], sems.at[e])
        for e in range(source_ref.shape[0])
    ]
    for copy in copies:
        copy.start()
    for k, piece_ref in enumerate(piece_refs):
        stack_ref[k] = piece_ref[...]
    for copy in copies:
        copy.wait()


def fetch(weights, pieces):
    return pl.pallas_call(
        fetch_kernel,
        in_specs=[whole(pltpu.HBM)] + [whole()] * len(pieces),
        out_specs=[whole(), whole()],
        out_shape=[
            VMEM(weights.shape, weights.dtype),
            VMEM((len(pieces),) + pieces[0].shape, pieces[0].dtype),
        ],
        scratch_shapes=[pltpu.SemaphoreType.DMA((weights.shape[0],))],
        compiler_params=pltpu.CompilerParams(vmem_limit_bytes=2 * MIB),
        cost_estimate=pl.CostEstimate(
            flops=0, bytes_accessed=2 * weights.size, transcendentals=0
        ),
    )(in_hbm(weights), *pieces)


def gate_table(expert_ids, gate_values, experts_all):
    chosen = expert_ids[:, :, None] == jnp.arange(experts_all, dtype=jnp.int32)[None, None, :]
    return jnp.sum(jnp.where(chosen, gate_values[:, :, None], 0.0), axis=1)


def pack_kernel(experts_all, rows_in, ids_in, gates_in, out_ref, ids_ref, gates_ref, sems):
    rows, feature_count = rows_in.shape
    copies = [
        pltpu.make_async_copy(ids_in, ids_ref, sems.at[0]),
        pltpu.make_async_copy(gates_in, gates_ref, sems.at[1]),
        pltpu.make_async_copy(rows_in, out_ref.at[:, :feature_count], sems.at[2]),
    ]
    for copy in copies:
        copy.start()
    copies[0].wait()
    copies[1].wait()
    lane = lax.broadcasted_iota(jnp.int32, (rows, out_ref.shape[1] - feature_count), 1)
    expert = lax.rem(lane, experts_all)
    table = jnp.zeros(lane.shape, F32)
    for k in range(ids_ref.shape[1]):
        table += jnp.where(ids_ref[:, k : k + 1] == expert, gates_ref[:, k : k + 1], 0.0)
    high = table.astype(BF16).astype(F32)
    middle = (table - high).astype(BF16).astype(F32)
    low = table - high - middle
    coded = jnp.where(
        lane < experts_all,
        high,
        jnp.where(
            lane < 2 * experts_all, middle, jnp.where(lane < 3 * experts_all, low, 0.0)
        ),
    )
    out_ref[:, feature_count:] = coded.astype(BF16)
    copies[2].wait()


def pack(hidden_rows, expert_ids, gate_values, experts_all):
    rows, feature_count = hidden_rows.shape
    return pl.pallas_call(
        lambda *refs: pack_kernel(experts_all, *refs),
        in_specs=[whole(pltpu.HBM)] * 3,
        out_specs=whole(),
        out_shape=VMEM((rows, feature_count + 128), BF16),
        scratch_shapes=[
            VMEM(expert_ids.shape, jnp.int32),
            VMEM(gate_values.shape, F32),
            pltpu.SemaphoreType.DMA((3,)),
        ],
        compiler_params=pltpu.CompilerParams(vmem_limit_bytes=2 * MIB),
        cost_estimate=pl.CostEstimate(
            flops=0, bytes_accessed=4 * rows * feature_count, transcendentals=0
        ),
    )(in_hbm(hidden_rows), in_hbm(expert_ids), in_hbm(gate_values))


def gate_up_kernel(
    slots,
    experts_all,
    mine_z_ref,
    mine_x_ref,
    other_z_ref,
    other_x_ref,
    gate_ref,
    up_ref,
    hidden_ref,
    table_ref,
    slot_ref,
    rows_ref,
    coded_ref,
):
    layer = lax.axis_index("expert")
    member = lax.axis_index("dp")
    x_side, core = jnp.right_shift(member, 1), jnp.bitwise_and(member, 1)
    layers, rows_dev, _ = mine_z_ref.shape
    experts, feature_count, _ = gate_ref.shape
    count = rows_ref.shape[0]
    first = core == 0
    for z in range(layers):
        for x, (mine_ref, other_ref) in enumerate(
            ((mine_z_ref, other_z_ref), (mine_x_ref, other_x_ref))
        ):
            at = (2 * z + x) * 2 * rows_dev
            mine, other = mine_ref[z], other_ref[z]
            pair = jnp.concatenate(
                [jnp.where(first, mine, other), jnp.where(first, other, mine)], axis=0
            )
            rows_ref[at : at + 2 * rows_dev] = pair[:, :feature_count]
            coded_ref[at : at + 2 * rows_dev] = pair[:, feature_count:]
    lanes = coded_ref.shape[1]
    source = lax.broadcasted_iota(jnp.int32, (lanes, lanes), 0)
    target = lax.broadcasted_iota(jnp.int32, (lanes, lanes), 1)
    selector = (
        (lax.rem(source, experts_all) == layer * experts + target)
        & (target < experts)
        & (source < 3 * experts_all)
    )
    table = jnp.dot(
        coded_ref[...], selector.astype(F32).astype(BF16), preferred_element_type=F32
    )
    table_ref[...] = table
    chosen = (table > 0.0).astype(F32).astype(BF16)
    row = lax.broadcasted_iota(jnp.int32, (count, count), 0)
    column = lax.broadcasted_iota(jnp.int32, (count, count), 1)
    turn = x_side * (2 * rows_dev)
    ahead = jnp.bitwise_xor(column, turn) < jnp.bitwise_xor(row, turn)
    rank = jnp.dot(ahead.astype(F32).astype(BF16), chosen, preferred_element_type=F32)
    rank = jnp.where(table > 0.0, rank, -1.0)
    slot = lax.broadcasted_iota(jnp.int32, (count, slot_ref.shape[2]), 1).astype(F32)
    rows = rows_ref[...]
    for e in range(experts):
        in_slot = (rank[:, e : e + 1] == slot).astype(F32).astype(BF16)
        slot_ref[e] = in_slot
        gate = jnp.dot(rows, gate_ref[e], preferred_element_type=F32)
        up = jnp.dot(rows, up_ref[e], preferred_element_type=F32)
        made = (gate / (1.0 + jnp.exp(-gate)) * up).astype(BF16)
        hidden_ref[e] = lax.dot_general(
            in_slot, made, (((0,), (0,)), ((), ())), preferred_element_type=F32
        )[:slots].astype(BF16)


def gate_up(pieces, gate_proj, up_proj, slots, experts_all):
    experts, depth, share = gate_proj.shape
    layers, rows_dev, total_width = pieces[0].shape
    count = 4 * layers * rows_dev
    extra = total_width - depth
    return pl.pallas_call(
        lambda *refs: gate_up_kernel(slots, experts_all, *refs),
        in_specs=[whole()] * 6,
        out_specs=[whole()] * 3,
        out_shape=[
            VMEM((experts, slots, share), BF16),
            VMEM((count, extra), F32),
            VMEM((experts, count, 128), BF16),
        ],
        scratch_shapes=[VMEM((count, depth), BF16), VMEM((count, extra), BF16)],
        compiler_params=pltpu.CompilerParams(vmem_limit_bytes=24 * MIB),
        cost_estimate=pl.CostEstimate(
            flops=4 * experts * count * depth * share,
            bytes_accessed=4 * experts * depth * share,
            transcendentals=experts * count * share,
        ),
    )(*pieces, in_vmem(gate_proj), in_vmem(up_proj))


def down_kernel(
    table_ref, slot_ref, h0_ref, h1_ref, h2_ref, h3_ref, down_ref, *out_refs
):
    place = lax.axis_index("dp")
    experts, slots, share = h0_ref.shape
    width = down_ref.shape[2]
    count = table_ref.shape[0]
    tile = 256
    rows_z = out_refs[0].shape[0]
    for start in range(0, width, tile):
        total = jnp.zeros((count, tile), F32)
        for e in range(experts):
            made = jnp.zeros((slots, tile), F32)
            for k, ref in enumerate((h0_ref, h1_ref, h2_ref, h3_ref)):
                owner = jnp.bitwise_xor(place, k)
                weights = down_ref[
                    e, pl.ds(pl.multiple_of(owner * share, share), share), start : start + tile
                ]
                made += jnp.dot(ref[e], weights, preferred_element_type=F32)
            spread = jnp.dot(
                slot_ref[e][:, :slots], made.astype(BF16), preferred_element_type=F32
            )
            total += table_ref[:, e : e + 1] * spread
        done = total.astype(BF16)
        for k, ref in enumerate(out_refs):
            ref[:, start : start + tile] = done[k * rows_z : (k + 1) * rows_z]


def down(table, slot, hidden, down_proj):
    experts, depth, width = down_proj.shape
    rows = table.shape[0]
    return pl.pallas_call(
        down_kernel,
        in_specs=[whole()] * 7,
        out_specs=[whole()] * 4,
        out_shape=[VMEM((rows // 4, width), BF16)] * 4,
        compiler_params=pltpu.CompilerParams(vmem_limit_bytes=16 * MIB),
        cost_estimate=pl.CostEstimate(
            flops=2 * experts * rows * depth * width,
            bytes_accessed=2 * experts * depth * width,
            transcendentals=0,
        ),
    )(table, slot, *hidden, in_vmem(down_proj))


def swap(value, axis, bit):
    size = lax.axis_size(axis)
    return lax.ppermute(value, axis, [(i, i ^ bit) for i in range(size)])


def routed_four(
    hidden_rows,
    expert_ids,
    gate_values,
    gate_proj,
    up_proj,
    down_proj,
    queries,
    latent_cache,
    cache_lengths,
):
    rows_dev, feature_count = hidden_rows.shape
    local_experts = gate_proj.shape[0]
    width = down_proj.shape[2]
    experts_all = local_experts * 4
    capacity = max(2, 3 * rows_dev * expert_ids.shape[1] // (2 * experts_all))
    member = lax.axis_index("dp").astype(jnp.int32)
    core = jnp.bitwise_and(member, 1)
    x_side = jnp.right_shift(member, 1)

    sent = pack(hidden_rows, expert_ids, gate_values, experts_all)
    along_z = [sent] + [swap(sent, "expert", k) for k in (1, 2, 3)]
    along_x = [swap(sent, "dp", 2)]
    gate_held, passed = fetch(gate_proj, along_z[1:2])
    along_z[1] = passed[0]
    along_x += [swap(block, "dp", 2) for block in along_z[1:]]
    up_held, mine_z = fetch(up_proj, along_z)
    mine_x = jnp.stack(along_x)
    other_z = swap(mine_z, "dp", 1)
    other_x = swap(mine_x, "dp", 1)

    hidden, table, slot = gate_up(
        (mine_z, mine_x, other_z, other_x),
        gate_held,
        up_held,
        16 * capacity,
        experts_all,
    )
    hidden_x = swap(hidden, "dp", 2)
    hidden_c = swap(hidden, "dp", 1)
    attended, down_held = attend_and_fetch(
        queries, latent_cache, cache_lengths, down_proj, hidden
    )
    hidden_x = once_done(hidden_x, down_held)
    hidden_xc = swap(hidden_x, "dp", 1)
    partial = down(table, slot, (hidden, hidden_c, hidden_x, hidden_xc), down_held)
    arrived = [partial[0]] + [swap(partial[k], "expert", k) for k in (1, 2, 3)]
    summed = sum(block.astype(F32) for block in arrived).astype(BF16)
    summed = summed.reshape(2, 2, rows_dev, width)
    both = jnp.stack([summed[0], swap(summed[1], "dp", 2)])
    kept = jnp.where(core == 0, both[:, 0], both[:, 1])
    given = jnp.where(core == 0, both[:, 1], both[:, 0])
    taken = swap(given, "dp", 1)
    by_core = jnp.where(core == 0, jnp.stack([kept, taken], 1), jnp.stack([taken, kept], 1))
    by_place = jnp.where(x_side == 0, by_core, by_core[::-1]).reshape(4, rows_dev, width)
    blended = jnp.transpose(by_place, (1, 0, 2)).reshape(rows_dev, 4 * width)
    return blended, attended


def routed_any(hidden_rows, expert_ids, gate_values, gate_proj, up_proj, down_proj):
    rows_dev, feature_count = hidden_rows.shape
    local_experts = gate_proj.shape[0]
    width = down_proj.shape[2]
    owners = lax.axis_size("expert")
    members = lax.axis_size("dp")
    experts_all = local_experts * owners
    table = gate_table(expert_ids, gate_values, experts_all)
    rows = lax.all_gather(hidden_rows, ("expert", "dp"), axis=0, tiled=True)
    table = lax.all_gather(table, ("expert", "dp"), axis=0, tiled=True)
    table = lax.dynamic_slice_in_dim(
        table, lax.axis_index("expert") * local_experts, local_experts, axis=1
    )
    total = jnp.zeros((rows.shape[0], width), F32)
    for e in range(local_experts):
        gate = jnp.dot(rows, gate_proj[e], preferred_element_type=F32)
        up = jnp.dot(rows, up_proj[e], preferred_element_type=F32)
        share = (jax.nn.silu(gate) * up).astype(BF16)
        hidden = lax.all_gather(share, "dp", axis=1, tiled=True)
        made = jnp.dot(hidden, down_proj[e], preferred_element_type=F32).astype(BF16)
        total += table[:, e : e + 1] * made.astype(F32)
    partial = total.astype(BF16).reshape(owners, members, rows_dev, width)
    returned = lax.all_to_all(
        lax.all_to_all(partial, "expert", split_axis=0, concat_axis=0, tiled=True),
        "dp",
        split_axis=1,
        concat_axis=1,
        tiled=True,
    )
    blended = jnp.sum(returned.astype(F32), axis=0).astype(BF16)
    return jnp.transpose(blended, (1, 0, 2)).reshape(rows_dev, members * width)


def local(
    hidden_rows,
    expert_ids,
    gate_values,
    gate_proj,
    up_proj,
    down_proj,
    queries,
    latent_cache,
    cache_lengths,
):
    routing = (hidden_rows, expert_ids, gate_values, gate_proj, up_proj, down_proj)
    attention = (queries, latent_cache, cache_lengths)
    four = lax.axis_size("expert") == 4 and lax.axis_size("dp") == 4
    if four and hidden_rows.shape[0] == 8 and 12 * gate_proj.shape[0] <= 128:
        return routed_four(*routing, *attention)
    return routed_any(*routing), attend(*attention)


def solution(mesh):
    return jax.shard_map(
        local,
        mesh=mesh,
        in_specs=(
            P(("groups", "expert", "dp"), None),
            P(("groups", "expert", "dp"), None),
            P(("groups", "expert", "dp"), None),
            P("expert", None, "dp"),
            P("expert", None, "dp"),
            P("expert", None, "dp"),
            P(("groups", "expert", "dp"), None, None),
            P(("groups", "expert", "dp"), None, None),
            P(("groups", "expert", "dp")),
        ),
        out_specs=(P(("groups", "expert", "dp"), None), P(("groups", "expert", "dp"), None, None)),
        check_vma=False,
    )
```

```python
import jax
import jax.numpy as jnp
from jax import lax
from jax.experimental import pallas as pl
from jax.experimental.pallas import tpu as pltpu
from jax.sharding import PartitionSpec as P

LATENT = 512
F32 = jnp.float32
BF16 = jnp.bfloat16
VMEM = pltpu.VMEM
MIB = 1024 * 1024


softmax_scale = 192.0 ** (-0.5)


def attend_rows(lengths_ref, queries_ref, cache_ref, out_ref):
    for r in range(queries_ref.shape[0]):
        queries = queries_ref[r].T
        cache = cache_ref[r]
        scores = jnp.dot(queries, cache, preferred_element_type=F32) * softmax_scale
        usable = lax.broadcasted_iota(jnp.int32, scores.shape, 1) < lengths_ref[r]
        scores = jnp.where(usable, scores, -1e30)
        weights = jnp.exp(scores - jnp.max(scores, axis=1, keepdims=True))
        weights = weights / jnp.sum(weights, axis=1, keepdims=True)
        out_ref[r] = lax.dot_general(
            weights.astype(BF16),
            cache[:LATENT],
            (((1,), (1,)), ((), ())),
            preferred_element_type=F32,
        ).astype(BF16)


def attend_cost(queries, latent_cache):
    rows, heads, width = queries.shape
    positions = latent_cache.shape[1]
    return pl.CostEstimate(
        flops=2 * rows * heads * positions * (width + LATENT),
        bytes_accessed=2 * rows * (positions * width + heads * (width + LATENT)),
        transcendentals=rows * heads * positions,
    )


def in_hbm(array):
    return pltpu.with_memory_space_constraint(array, pltpu.HBM)


def in_vmem(array):
    return pltpu.with_memory_space_constraint(array, VMEM)


def whole(space=VMEM):
    return pl.BlockSpec(memory_space=space)


def attend(queries, latent_cache, cache_lengths):
    rows, heads, _ = queries.shape
    return pl.pallas_call(
        attend_rows,
        in_specs=[whole(pltpu.SMEM), whole(), whole()],
        out_specs=whole(),
        out_shape=jax.ShapeDtypeStruct((rows, heads, LATENT), BF16),
        compiler_params=pltpu.CompilerParams(vmem_limit_bytes=16 * MIB),
        cost_estimate=attend_cost(queries, latent_cache),
    )(cache_lengths, jnp.swapaxes(queries, 1, 2), jnp.swapaxes(latent_cache, 1, 2))


def attend_and_fetch_kernel(
    lengths_ref, queries_ref, cache_ref, source_ref, after_ref, out_ref, held_ref, sem
):
    copy = pltpu.make_async_copy(source_ref, held_ref, sem)
    copy.start()
    attend_rows(lengths_ref, queries_ref, cache_ref, out_ref)
    copy.wait()


def attend_and_fetch(queries, latent_cache, cache_lengths, weights, after):
    rows, heads, _ = queries.shape
    return pl.pallas_call(
        attend_and_fetch_kernel,
        in_specs=[whole(pltpu.SMEM), whole(), whole(), whole(pltpu.HBM), whole(pl.ANY)],
        out_specs=[whole(), whole()],
        out_shape=[
            jax.ShapeDtypeStruct((rows, heads, LATENT), BF16),
            VMEM(weights.shape, weights.dtype),
        ],
        scratch_shapes=[pltpu.SemaphoreType.DMA],
        compiler_params=pltpu.CompilerParams(vmem_limit_bytes=12 * MIB),
        cost_estimate=attend_cost(queries, latent_cache),
    )(
        cache_lengths,
        jnp.swapaxes(queries, 1, 2),
        jnp.swapaxes(latent_cache, 1, 2),
        in_hbm(weights),
        after,
    )


def once_done(value, other):
    return pl.pallas_call(
        lambda *refs: None,
        in_specs=[whole(pl.ANY)] * 2,
        out_specs=whole(pl.ANY),
        out_shape=VMEM(value.shape, value.dtype),
        input_output_aliases={0: 0},
        compiler_params=pltpu.CompilerParams(vmem_limit_bytes=MIB),
        cost_estimate=pl.CostEstimate(flops=0, bytes_accessed=0, transcendentals=0),
    )(value, other)


def fetch_kernel(gate_ref, up_ref, *refs):
    *piece_refs, gate_held_ref, up_held_ref, stack_ref, sems = refs
    copies = []
    for source_ref, held_ref in ((gate_ref, gate_held_ref), (up_ref, up_held_ref)):
        for e in range(held_ref.shape[0]):
            copies.append(
                pltpu.make_async_copy(source_ref.at[e], held_ref.at[e], sems.at[len(copies)])
            )
    for copy in copies:
        copy.start()
    for k, piece_ref in enumerate(piece_refs):
        stack_ref[k] = piece_ref[...]
    for copy in copies:
        copy.wait()


def fetch(gate_proj, up_proj, count, pieces):
    held = VMEM((count,) + gate_proj.shape[1:], gate_proj.dtype)
    return pl.pallas_call(
        fetch_kernel,
        in_specs=[whole(pltpu.HBM)] * 2 + [whole()] * len(pieces),
        out_specs=[whole()] * 3,
        out_shape=[held, held, VMEM((len(pieces),) + pieces[0].shape, pieces[0].dtype)],
        scratch_shapes=[pltpu.SemaphoreType.DMA((2 * count,))],
        compiler_params=pltpu.CompilerParams(vmem_limit_bytes=2 * MIB),
        cost_estimate=pl.CostEstimate(
            flops=0,
            bytes_accessed=4 * count * gate_proj[0].size,
            transcendentals=0,
        ),
    )(in_hbm(gate_proj), in_hbm(up_proj), *pieces)


def gate_table(expert_ids, gate_values, experts_all):
    chosen = expert_ids[:, :, None] == jnp.arange(experts_all, dtype=jnp.int32)[None, None, :]
    return jnp.sum(jnp.where(chosen, gate_values[:, :, None], 0.0), axis=1)


def pack_kernel(experts_all, rows_in, ids_in, gates_in, out_ref, ids_ref, gates_ref, sems):
    rows, feature_count = rows_in.shape
    copies = [
        pltpu.make_async_copy(ids_in, ids_ref, sems.at[0]),
        pltpu.make_async_copy(gates_in, gates_ref, sems.at[1]),
        pltpu.make_async_copy(rows_in, out_ref.at[:, :feature_count], sems.at[2]),
    ]
    for copy in copies:
        copy.start()
    copies[0].wait()
    copies[1].wait()
    lane = lax.broadcasted_iota(jnp.int32, (rows, out_ref.shape[1] - feature_count), 1)
    expert = lax.rem(lane, experts_all)
    table = jnp.zeros(lane.shape, F32)
    for k in range(ids_ref.shape[1]):
        table += jnp.where(ids_ref[:, k : k + 1] == expert, gates_ref[:, k : k + 1], 0.0)
    high = table.astype(BF16).astype(F32)
    middle = (table - high).astype(BF16).astype(F32)
    low = table - high - middle
    coded = jnp.where(
        lane < experts_all,
        high,
        jnp.where(
            lane < 2 * experts_all, middle, jnp.where(lane < 3 * experts_all, low, 0.0)
        ),
    )
    out_ref[:, feature_count:] = coded.astype(BF16)
    copies[2].wait()


def pack(hidden_rows, expert_ids, gate_values, experts_all):
    rows, feature_count = hidden_rows.shape
    return pl.pallas_call(
        lambda *refs: pack_kernel(experts_all, *refs),
        in_specs=[whole(pltpu.HBM)] * 3,
        out_specs=whole(),
        out_shape=VMEM((rows, feature_count + 128), BF16),
        scratch_shapes=[
            VMEM(expert_ids.shape, jnp.int32),
            VMEM(gate_values.shape, F32),
            pltpu.SemaphoreType.DMA((3,)),
        ],
        compiler_params=pltpu.CompilerParams(vmem_limit_bytes=2 * MIB),
        cost_estimate=pl.CostEstimate(
            flops=0, bytes_accessed=4 * rows * feature_count, transcendentals=0
        ),
    )(in_hbm(hidden_rows), in_hbm(expert_ids), in_hbm(gate_values))


def gate_up_kernel(
    slots,
    experts_all,
    mine_z_ref,
    mine_x_ref,
    other_z_ref,
    other_x_ref,
    gate_held_ref,
    up_held_ref,
    gate_ref,
    up_ref,
    hidden_ref,
    spread_ref,
    rows_ref,
    coded_ref,
    gate_late_ref,
    up_late_ref,
    sems,
):
    ready = gate_held_ref.shape[0]
    late = gate_late_ref.shape[0]
    copies = []
    for e in range(late):
        for m, (source_ref, late_ref) in enumerate(
            ((gate_ref, gate_late_ref), (up_ref, up_late_ref))
        ):
            copies.append(
                pltpu.make_async_copy(
                    source_ref.at[ready + e], late_ref.at[e], sems.at[2 * e + m]
                )
            )
    for copy in copies:
        copy.start()
    layer = lax.axis_index("expert")
    member = lax.axis_index("dp")
    x_side, core = jnp.right_shift(member, 1), jnp.bitwise_and(member, 1)
    layers, rows_dev, _ = mine_z_ref.shape
    experts, feature_count, _ = gate_ref.shape
    count = rows_ref.shape[0]
    first = core == 0
    for z in range(layers):
        for x, (mine_ref, other_ref) in enumerate(
            ((mine_z_ref, other_z_ref), (mine_x_ref, other_x_ref))
        ):
            at = (2 * z + x) * 2 * rows_dev
            mine, other = mine_ref[z], other_ref[z]
            pair = jnp.concatenate(
                [jnp.where(first, mine, other), jnp.where(first, other, mine)], axis=0
            )
            rows_ref[at : at + 2 * rows_dev] = pair[:, :feature_count]
            coded_ref[at : at + 2 * rows_dev] = pair[:, feature_count:]
    lanes = coded_ref.shape[1]
    source = lax.broadcasted_iota(jnp.int32, (lanes, lanes), 0)
    target = lax.broadcasted_iota(jnp.int32, (lanes, lanes), 1)
    selector = (
        (lax.rem(source, experts_all) == layer * experts + target)
        & (target < experts)
        & (source < 3 * experts_all)
    )
    table = jnp.dot(
        coded_ref[...], selector.astype(F32).astype(BF16), preferred_element_type=F32
    )
    chosen = (table > 0.0).astype(F32).astype(BF16)
    row = lax.broadcasted_iota(jnp.int32, (count, count), 0)
    column = lax.broadcasted_iota(jnp.int32, (count, count), 1)
    turn = x_side * (2 * rows_dev)
    ahead = jnp.bitwise_xor(column, turn) < jnp.bitwise_xor(row, turn)
    rank = jnp.dot(ahead.astype(F32).astype(BF16), chosen, preferred_element_type=F32)
    rank = jnp.where(table > 0.0, rank, -1.0)
    slot = lax.broadcasted_iota(jnp.int32, (count, count), 1).astype(F32)
    rows = rows_ref[...]
    for e in range(experts):
        hit = rank[:, e : e + 1] == slot
        in_slot = hit.astype(F32).astype(BF16)
        value = jnp.where(hit, table[:, e : e + 1], 0.0)
        high = value.astype(BF16)
        spread_ref[:count, e * count : (e + 1) * count] = high
        spread_ref[count:, e * count : (e + 1) * count] = (value - high.astype(F32)).astype(BF16)
        if e < ready:
            gate_matrix, up_matrix = gate_held_ref[e], up_held_ref[e]
        else:
            copies[2 * (e - ready)].wait()
            copies[2 * (e - ready) + 1].wait()
            gate_matrix, up_matrix = gate_late_ref[e - ready], up_late_ref[e - ready]
        gate = jnp.dot(rows, gate_matrix, preferred_element_type=F32)
        up = jnp.dot(rows, up_matrix, preferred_element_type=F32)
        made = (gate / (1.0 + jnp.exp(-gate)) * up).astype(BF16)
        hidden_ref[e] = lax.dot_general(
            in_slot, made, (((0,), (0,)), ((), ())), preferred_element_type=F32
        )[:slots].astype(BF16)


def gate_up(pieces, gate_held, up_held, gate_proj, up_proj, slots, experts_all):
    experts, depth, share = gate_proj.shape
    layers, rows_dev, total_width = pieces[0].shape
    count = 4 * layers * rows_dev
    late = experts - gate_held.shape[0]
    extra = total_width - depth
    return pl.pallas_call(
        lambda *refs: gate_up_kernel(slots, experts_all, *refs),
        in_specs=[whole()] * 6 + [whole(pltpu.HBM)] * 2,
        out_specs=[whole()] * 2,
        out_shape=[
            VMEM((experts, slots, share), BF16),
            VMEM((2 * count, experts * count), BF16),
        ],
        scratch_shapes=[
            VMEM((count, depth), BF16),
            VMEM((count, extra), BF16),
            VMEM((late, depth, share), BF16),
            VMEM((late, depth, share), BF16),
            pltpu.SemaphoreType.DMA((2 * late,)),
        ],
        compiler_params=pltpu.CompilerParams(vmem_limit_bytes=24 * MIB),
        cost_estimate=pl.CostEstimate(
            flops=4 * experts * count * depth * share,
            bytes_accessed=4 * experts * depth * share,
            transcendentals=experts * count * share,
        ),
    )(*pieces, gate_held, up_held, in_hbm(gate_proj), in_hbm(up_proj))


def down_kernel(
    spread_ref, h0_ref, h1_ref, h2_ref, h3_ref, down_ref, o0_ref, o1_ref, o2_ref, o3_ref, made_ref
):
    place = lax.axis_index("dp")
    experts, slots, share = h0_ref.shape
    width = down_ref.shape[2]
    count = spread_ref.shape[0] // 2
    rows_z = o0_ref.shape[0]
    tile = 256
    for e in range(experts):
        if slots < count:
            made_ref[e * count + slots : (e + 1) * count] = jnp.zeros(
                (count - slots, width), BF16
            )
        made = jnp.zeros((slots, width), F32)
        for k, ref in enumerate((h0_ref, h1_ref, h2_ref, h3_ref)):
            owner = jnp.bitwise_xor(place, k)
            weights = down_ref[e, pl.ds(pl.multiple_of(owner * share, share), share)]
            made += jnp.dot(ref[e], weights, preferred_element_type=F32)
        made_ref[e * count : e * count + slots] = made.astype(BF16)
    spread = spread_ref[...]
    for start in range(0, width, tile):
        both = jnp.dot(spread, made_ref[:, start : start + tile], preferred_element_type=F32)
        done = (both[:count] + both[count:]).astype(BF16)
        for k, ref in enumerate((o0_ref, o1_ref, o2_ref, o3_ref)):
            ref[:, start : start + tile] = done[k * rows_z : (k + 1) * rows_z]


def down(spread, hidden, down_proj):
    experts, depth, width = down_proj.shape
    count = spread.shape[0] // 2
    return pl.pallas_call(
        down_kernel,
        in_specs=[whole()] * 6,
        out_specs=[whole()] * 4,
        out_shape=[VMEM((count // 4, width), BF16)] * 4,
        scratch_shapes=[VMEM((experts * count, width), BF16)],
        compiler_params=pltpu.CompilerParams(vmem_limit_bytes=16 * MIB),
        cost_estimate=pl.CostEstimate(
            flops=2 * experts * count * depth * width,
            bytes_accessed=2 * experts * depth * width,
            transcendentals=0,
        ),
    )(spread, *hidden, in_vmem(down_proj))


def collect_kernel(p0_ref, p1_ref, p2_ref, p3_ref, own_ref, core_ref, x_ref, far_ref):
    total = p0_ref[...].astype(F32)
    for ref in (p1_ref, p2_ref, p3_ref):
        total += ref[...].astype(F32)
    rows = own_ref.shape[0]
    first = jnp.bitwise_and(lax.axis_index("dp"), 1) == 0
    near = [total[k * rows : (k + 1) * rows] for k in range(4)]
    own_ref[...] = jnp.where(first, near[0], near[1]).astype(BF16)
    core_ref[...] = jnp.where(first, near[1], near[0]).astype(BF16)
    x_ref[...] = jnp.where(first, near[2], near[3]).astype(BF16)
    far_ref[...] = jnp.where(first, near[3], near[2]).astype(BF16)


def collect(partials):
    rows, width = partials[0].shape
    return pl.pallas_call(
        collect_kernel,
        in_specs=[whole()] * 4,
        out_specs=[whole()] * 4,
        out_shape=[VMEM((rows // 4, width), BF16)] * 4,
        compiler_params=pltpu.CompilerParams(vmem_limit_bytes=2 * MIB),
        cost_estimate=pl.CostEstimate(
            flops=4 * rows * width, bytes_accessed=8 * rows * width, transcendentals=0
        ),
    )(*partials)


def place_kernel(p0_ref, p1_ref, p2_ref, p3_ref, out_ref):
    place = lax.axis_index("dp")
    width = p0_ref.shape[1]
    for k, ref in enumerate((p0_ref, p1_ref, p2_ref, p3_ref)):
        at = pl.multiple_of(jnp.bitwise_xor(place, k) * width, width)
        out_ref[:, pl.ds(at, width)] = ref[...]


def place_all(pieces):
    rows, width = pieces[0].shape
    return pl.pallas_call(
        place_kernel,
        in_specs=[whole()] * 4,
        out_specs=whole(),
        out_shape=jax.ShapeDtypeStruct((rows, 4 * width), BF16),
        compiler_params=pltpu.CompilerParams(vmem_limit_bytes=2 * MIB),
        cost_estimate=pl.CostEstimate(
            flops=0, bytes_accessed=16 * rows * width, transcendentals=0
        ),
    )(*pieces)


def swap(value, axis, bit):
    size = lax.axis_size(axis)
    return lax.ppermute(value, axis, [(i, i ^ bit) for i in range(size)])


def routed_four(
    hidden_rows,
    expert_ids,
    gate_values,
    gate_proj,
    up_proj,
    down_proj,
    queries,
    latent_cache,
    cache_lengths,
):
    rows_dev, feature_count = hidden_rows.shape
    local_experts = gate_proj.shape[0]
    width = down_proj.shape[2]
    experts_all = local_experts * 4
    capacity = max(2, 3 * rows_dev * expert_ids.shape[1] // (2 * experts_all))
    sent = pack(hidden_rows, expert_ids, gate_values, experts_all)
    along_z = [sent] + [swap(sent, "expert", k) for k in (1, 2, 3)]
    along_x = [swap(block, "dp", 2) for block in along_z]
    gate_held, up_held, mine_z = fetch(gate_proj, up_proj, local_experts // 2, along_z)
    mine_x = jnp.stack(along_x)
    other_z = swap(mine_z, "dp", 1)
    other_x = swap(mine_x, "dp", 1)

    hidden, spread = gate_up(
        (mine_z, mine_x, other_z, other_x),
        gate_held,
        up_held,
        gate_proj,
        up_proj,
        16 * capacity,
        experts_all,
    )
    hidden_x = swap(hidden, "dp", 2)
    hidden_c = swap(hidden, "dp", 1)
    attended, down_held = attend_and_fetch(
        queries, latent_cache, cache_lengths, down_proj, hidden
    )
    hidden_x = once_done(hidden_x, down_held)
    hidden_xc = swap(hidden_x, "dp", 1)
    partial = down(spread, (hidden, hidden_c, hidden_x, hidden_xc), down_held)
    arrived = [partial[0]] + [swap(partial[k], "expert", k) for k in (1, 2, 3)]
    own, to_core, to_x, to_far = collect(arrived)
    far = swap(to_far, "dp", 3)
    blended = place_all((own, swap(to_core, "dp", 1), swap(to_x, "dp", 2), far))
    return blended, attended


def routed_any(hidden_rows, expert_ids, gate_values, gate_proj, up_proj, down_proj):
    rows_dev, feature_count = hidden_rows.shape
    local_experts = gate_proj.shape[0]
    width = down_proj.shape[2]
    owners = lax.axis_size("expert")
    members = lax.axis_size("dp")
    experts_all = local_experts * owners
    table = gate_table(expert_ids, gate_values, experts_all)
    rows = lax.all_gather(hidden_rows, ("expert", "dp"), axis=0, tiled=True)
    table = lax.all_gather(table, ("expert", "dp"), axis=0, tiled=True)
    table = lax.dynamic_slice_in_dim(
        table, lax.axis_index("expert") * local_experts, local_experts, axis=1
    )
    total = jnp.zeros((rows.shape[0], width), F32)
    for e in range(local_experts):
        gate = jnp.dot(rows, gate_proj[e], preferred_element_type=F32)
        up = jnp.dot(rows, up_proj[e], preferred_element_type=F32)
        share = (jax.nn.silu(gate) * up).astype(BF16)
        hidden = lax.all_gather(share, "dp", axis=1, tiled=True)
        made = jnp.dot(hidden, down_proj[e], preferred_element_type=F32).astype(BF16)
        total += table[:, e : e + 1] * made.astype(F32)
    partial = total.astype(BF16).reshape(owners, members, rows_dev, width)
    returned = lax.all_to_all(
        lax.all_to_all(partial, "expert", split_axis=0, concat_axis=0, tiled=True),
        "dp",
        split_axis=1,
        concat_axis=1,
        tiled=True,
    )
    blended = jnp.sum(returned.astype(F32), axis=0).astype(BF16)
    return jnp.transpose(blended, (1, 0, 2)).reshape(rows_dev, members * width)


def local(
    hidden_rows,
    expert_ids,
    gate_values,
    gate_proj,
    up_proj,
    down_proj,
    queries,
    latent_cache,
    cache_lengths,
):
    routing = (hidden_rows, expert_ids, gate_values, gate_proj, up_proj, down_proj)
    attention = (queries, latent_cache, cache_lengths)
    four = lax.axis_size("expert") == 4 and lax.axis_size("dp") == 4
    if four and hidden_rows.shape[0] == 8 and 12 * gate_proj.shape[0] <= 128:
        return routed_four(*routing, *attention)
    return routed_any(*routing), attend(*attention)


def solution(mesh):
    return jax.shard_map(
        local,
        mesh=mesh,
        in_specs=(
            P(("groups", "expert", "dp"), None),
            P(("groups", "expert", "dp"), None),
            P(("groups", "expert", "dp"), None),
            P("expert", None, "dp"),
            P("expert", None, "dp"),
            P("expert", None, "dp"),
            P(("groups", "expert", "dp"), None, None),
            P(("groups", "expert", "dp"), None, None),
            P(("groups", "expert", "dp")),
        ),
        out_specs=(P(("groups", "expert", "dp"), None), P(("groups", "expert", "dp"), None, None)),
        check_vma=False,
    )
```

```python
import jax
import jax.numpy as jnp
from jax import lax
from jax.experimental import pallas as pl
from jax.experimental.pallas import tpu as pltpu
from jax.sharding import PartitionSpec as P

LATENT = 512
F32 = jnp.float32
BF16 = jnp.bfloat16
VMEM = pltpu.VMEM
MIB = 1024 * 1024


softmax_scale = 192.0 ** (-0.5)


def attend_rows(lengths_ref, queries_ref, cache_ref, out_ref):
    for r in range(queries_ref.shape[0]):
        queries = queries_ref[r].T
        cache = cache_ref[r]
        scores = jnp.dot(queries, cache, preferred_element_type=F32) * softmax_scale
        usable = lax.broadcasted_iota(jnp.int32, scores.shape, 1) < lengths_ref[r]
        scores = jnp.where(usable, scores, -1e30)
        weights = jnp.exp(scores - jnp.max(scores, axis=1, keepdims=True))
        weights = weights / jnp.sum(weights, axis=1, keepdims=True)
        out_ref[r] = lax.dot_general(
            weights.astype(BF16),
            cache[:LATENT],
            (((1,), (1,)), ((), ())),
            preferred_element_type=F32,
        ).astype(BF16)


def attend_cost(queries, latent_cache):
    rows, heads, width = queries.shape
    positions = latent_cache.shape[1]
    return pl.CostEstimate(
        flops=2 * rows * heads * positions * (width + LATENT),
        bytes_accessed=2 * rows * (positions * width + heads * (width + LATENT)),
        transcendentals=rows * heads * positions,
    )


def in_hbm(array):
    return pltpu.with_memory_space_constraint(array, pltpu.HBM)


def in_vmem(array):
    return pltpu.with_memory_space_constraint(array, VMEM)


def whole(space=VMEM):
    return pl.BlockSpec(memory_space=space)


def attend(queries, latent_cache, cache_lengths):
    rows, heads, _ = queries.shape
    return pl.pallas_call(
        attend_rows,
        in_specs=[whole(pltpu.SMEM), whole(), whole()],
        out_specs=whole(),
        out_shape=jax.ShapeDtypeStruct((rows, heads, LATENT), BF16),
        compiler_params=pltpu.CompilerParams(vmem_limit_bytes=16 * MIB),
        cost_estimate=attend_cost(queries, latent_cache),
    )(cache_lengths, jnp.swapaxes(queries, 1, 2), jnp.swapaxes(latent_cache, 1, 2))


def attend_and_fetch_kernel(
    lengths_ref, queries_ref, cache_ref, source_ref, after_ref, out_ref, held_ref, sem
):
    copy = pltpu.make_async_copy(source_ref, held_ref, sem)
    copy.start()
    attend_rows(lengths_ref, queries_ref, cache_ref, out_ref)
    copy.wait()


def attend_and_fetch(queries, latent_cache, cache_lengths, weights, after):
    rows, heads, _ = queries.shape
    return pl.pallas_call(
        attend_and_fetch_kernel,
        in_specs=[whole(pltpu.SMEM), whole(), whole(), whole(pltpu.HBM), whole(pl.ANY)],
        out_specs=[whole(), whole()],
        out_shape=[
            jax.ShapeDtypeStruct((rows, heads, LATENT), BF16),
            VMEM(weights.shape, weights.dtype),
        ],
        scratch_shapes=[pltpu.SemaphoreType.DMA],
        compiler_params=pltpu.CompilerParams(vmem_limit_bytes=12 * MIB),
        cost_estimate=attend_cost(queries, latent_cache),
    )(
        cache_lengths,
        jnp.swapaxes(queries, 1, 2),
        jnp.swapaxes(latent_cache, 1, 2),
        in_hbm(weights),
        after,
    )


def once_done(value, other):
    return pl.pallas_call(
        lambda *refs: None,
        in_specs=[whole(pl.ANY)] * 2,
        out_specs=whole(pl.ANY),
        out_shape=VMEM(value.shape, value.dtype),
        input_output_aliases={0: 0},
        compiler_params=pltpu.CompilerParams(vmem_limit_bytes=MIB),
        cost_estimate=pl.CostEstimate(flops=0, bytes_accessed=0, transcendentals=0),
    )(value, other)


def fetch_kernel(start, gate_ref, up_ref, *refs):
    *piece_refs, gate_held_ref, up_held_ref, stack_ref, sems = refs
    copies = []
    for source_ref, held_ref in ((gate_ref, gate_held_ref), (up_ref, up_held_ref)):
        for e in range(held_ref.shape[0]):
            copies.append(
                pltpu.make_async_copy(
                    source_ref.at[start + e], held_ref.at[e], sems.at[len(copies)]
                )
            )
    for copy in copies:
        copy.start()
    for k, piece_ref in enumerate(piece_refs):
        stack_ref[k] = piece_ref[...]
    for copy in copies:
        copy.wait()


def fetch(gate_proj, up_proj, start, stop, pieces):
    held = VMEM((stop - start,) + gate_proj.shape[1:], gate_proj.dtype)
    return pl.pallas_call(
        lambda *refs: fetch_kernel(start, *refs),
        in_specs=[whole(pltpu.HBM)] * 2 + [whole()] * len(pieces),
        out_specs=[whole()] * 3,
        out_shape=[held, held, VMEM((len(pieces),) + pieces[0].shape, pieces[0].dtype)],
        scratch_shapes=[pltpu.SemaphoreType.DMA((2 * (stop - start),))],
        compiler_params=pltpu.CompilerParams(vmem_limit_bytes=2 * MIB),
        cost_estimate=pl.CostEstimate(
            flops=0,
            bytes_accessed=4 * (stop - start) * gate_proj[0].size,
            transcendentals=0,
        ),
    )(in_hbm(gate_proj), in_hbm(up_proj), *pieces)


def gate_table(expert_ids, gate_values, experts_all):
    chosen = expert_ids[:, :, None] == jnp.arange(experts_all, dtype=jnp.int32)[None, None, :]
    return jnp.sum(jnp.where(chosen, gate_values[:, :, None], 0.0), axis=1)


def pack_kernel(experts_all, rows_in, ids_in, gates_in, out_ref, ids_ref, gates_ref, sems):
    rows, feature_count = rows_in.shape
    copies = [
        pltpu.make_async_copy(ids_in, ids_ref, sems.at[0]),
        pltpu.make_async_copy(gates_in, gates_ref, sems.at[1]),
        pltpu.make_async_copy(rows_in, out_ref.at[:, :feature_count], sems.at[2]),
    ]
    for copy in copies:
        copy.start()
    copies[0].wait()
    copies[1].wait()
    lane = lax.broadcasted_iota(jnp.int32, (rows, out_ref.shape[1] - feature_count), 1)
    expert = lax.rem(lane, experts_all)
    table = jnp.zeros(lane.shape, F32)
    for k in range(ids_ref.shape[1]):
        table += jnp.where(ids_ref[:, k : k + 1] == expert, gates_ref[:, k : k + 1], 0.0)
    high = table.astype(BF16).astype(F32)
    middle = (table - high).astype(BF16).astype(F32)
    low = table - high - middle
    coded = jnp.where(
        lane < experts_all,
        high,
        jnp.where(
            lane < 2 * experts_all, middle, jnp.where(lane < 3 * experts_all, low, 0.0)
        ),
    )
    out_ref[:, feature_count:] = coded.astype(BF16)
    copies[2].wait()


def pack(hidden_rows, expert_ids, gate_values, experts_all):
    rows, feature_count = hidden_rows.shape
    return pl.pallas_call(
        lambda *refs: pack_kernel(experts_all, *refs),
        in_specs=[whole(pltpu.HBM)] * 3,
        out_specs=whole(),
        out_shape=VMEM((rows, feature_count + 128), BF16),
        scratch_shapes=[
            VMEM(expert_ids.shape, jnp.int32),
            VMEM(gate_values.shape, F32),
            pltpu.SemaphoreType.DMA((3,)),
        ],
        compiler_params=pltpu.CompilerParams(vmem_limit_bytes=2 * MIB),
        cost_estimate=pl.CostEstimate(
            flops=0, bytes_accessed=4 * rows * feature_count, transcendentals=0
        ),
    )(in_hbm(hidden_rows), in_hbm(expert_ids), in_hbm(gate_values))


def gate_up_kernel(
    slots,
    experts_all,
    mine_z_ref,
    mine_x_ref,
    other_z_ref,
    other_x_ref,
    gate_first_ref,
    up_first_ref,
    gate_next_ref,
    up_next_ref,
    hidden_ref,
    spread_ref,
    rows_ref,
    coded_ref,
):
    matrices = []
    for pair in ((gate_first_ref, up_first_ref), (gate_next_ref, up_next_ref)):
        matrices += [[ref.at[e] for ref in pair] for e in range(pair[0].shape[0])]
    layer = lax.axis_index("expert")
    member = lax.axis_index("dp")
    x_side, core = jnp.right_shift(member, 1), jnp.bitwise_and(member, 1)
    layers, rows_dev, _ = mine_z_ref.shape
    feature_count = rows_ref.shape[1]
    experts = len(matrices)
    count = rows_ref.shape[0]
    first = core == 0
    for z in range(layers):
        for x, (mine_ref, other_ref) in enumerate(
            ((mine_z_ref, other_z_ref), (mine_x_ref, other_x_ref))
        ):
            at = (2 * z + x) * 2 * rows_dev
            mine, other = mine_ref[z], other_ref[z]
            pair = jnp.concatenate(
                [jnp.where(first, mine, other), jnp.where(first, other, mine)], axis=0
            )
            rows_ref[at : at + 2 * rows_dev] = pair[:, :feature_count]
            coded_ref[at : at + 2 * rows_dev] = pair[:, feature_count:]
    lanes = coded_ref.shape[1]
    source = lax.broadcasted_iota(jnp.int32, (lanes, lanes), 0)
    target = lax.broadcasted_iota(jnp.int32, (lanes, lanes), 1)
    selector = (
        (lax.rem(source, experts_all) == layer * experts + target)
        & (target < experts)
        & (source < 3 * experts_all)
    )
    table = jnp.dot(
        coded_ref[...], selector.astype(F32).astype(BF16), preferred_element_type=F32
    )
    chosen = (table > 0.0).astype(F32).astype(BF16)
    row = lax.broadcasted_iota(jnp.int32, (count, count), 0)
    column = lax.broadcasted_iota(jnp.int32, (count, count), 1)
    turn = x_side * (2 * rows_dev)
    ahead = jnp.bitwise_xor(column, turn) < jnp.bitwise_xor(row, turn)
    rank = jnp.dot(ahead.astype(F32).astype(BF16), chosen, preferred_element_type=F32)
    rank = jnp.where(table > 0.0, rank, -1.0)
    slot = lax.broadcasted_iota(jnp.int32, (count, count), 1).astype(F32)
    rows = rows_ref[...]
    for e in range(experts):
        hit = rank[:, e : e + 1] == slot
        in_slot = hit.astype(F32).astype(BF16)
        value = jnp.where(hit, table[:, e : e + 1], 0.0)
        high = value.astype(BF16)
        spread_ref[:count, e * count : (e + 1) * count] = high
        spread_ref[count:, e * count : (e + 1) * count] = (value - high.astype(F32)).astype(BF16)
        gate = jnp.dot(rows, matrices[e][0][...], preferred_element_type=F32)
        up = jnp.dot(rows, matrices[e][1][...], preferred_element_type=F32)
        made = (gate / (1.0 + jnp.exp(-gate)) * up).astype(BF16)
        hidden_ref[e] = lax.dot_general(
            in_slot, made, (((0,), (0,)), ((), ())), preferred_element_type=F32
        )[:slots].astype(BF16)


def gate_up(pieces, held, slots, experts_all):
    _, depth, share = held[0].shape
    experts = sum(array.shape[0] for array in held[::2])
    layers, rows_dev, total_width = pieces[0].shape
    count = 4 * layers * rows_dev
    extra = total_width - depth
    return pl.pallas_call(
        lambda *refs: gate_up_kernel(slots, experts_all, *refs),
        in_specs=[whole()] * 8,
        out_specs=[whole()] * 2,
        out_shape=[
            VMEM((experts, slots, share), BF16),
            VMEM((2 * count, experts * count), BF16),
        ],
        scratch_shapes=[
            VMEM((count, depth), BF16),
            VMEM((count, extra), BF16),
        ],
        compiler_params=pltpu.CompilerParams(vmem_limit_bytes=24 * MIB),
        cost_estimate=pl.CostEstimate(
            flops=4 * experts * count * depth * share,
            bytes_accessed=4 * experts * depth * share,
            transcendentals=experts * count * share,
        ),
    )(*pieces, *held)


def down_first_kernel(h0_ref, h1_ref, h2_ref, down_ref, made_ref):
    place = lax.axis_index("dp")
    experts, slots, share = h0_ref.shape
    for e in range(experts):
        made = jnp.zeros(made_ref.shape[1:], F32)
        for k, ref in enumerate((h0_ref, h1_ref, h2_ref)):
            owner = jnp.bitwise_xor(place, k)
            weights = down_ref[e, pl.ds(pl.multiple_of(owner * share, share), share)]
            made += jnp.dot(ref[e], weights, preferred_element_type=F32)
        made_ref[e] = made


def down_first(hidden, down_held):
    experts, slots, share = hidden[0].shape
    width = down_held.shape[2]
    return pl.pallas_call(
        down_first_kernel,
        in_specs=[whole()] * 4,
        out_specs=whole(),
        out_shape=VMEM((experts, slots, width), F32),
        compiler_params=pltpu.CompilerParams(vmem_limit_bytes=8 * MIB),
        cost_estimate=pl.CostEstimate(
            flops=6 * experts * slots * share * width,
            bytes_accessed=4 * experts * slots * width,
            transcendentals=0,
        ),
    )(*hidden, down_held)


def down_last_kernel(
    spread_ref, first_ref, h3_ref, down_ref, o0_ref, o1_ref, o2_ref, o3_ref, made_ref
):
    owner = jnp.bitwise_xor(lax.axis_index("dp"), 3)
    experts, slots, share = h3_ref.shape
    width = down_ref.shape[2]
    count = spread_ref.shape[0] // 2
    rows_z = o0_ref.shape[0]
    tile = 256
    for e in range(experts):
        if slots < count:
            made_ref[e * count + slots : (e + 1) * count] = jnp.zeros(
                (count - slots, width), BF16
            )
        weights = down_ref[e, pl.ds(pl.multiple_of(owner * share, share), share)]
        made = first_ref[e] + jnp.dot(h3_ref[e], weights, preferred_element_type=F32)
        made_ref[e * count : e * count + slots] = made.astype(BF16)
    spread = spread_ref[...]
    for start in range(0, width, tile):
        both = jnp.dot(spread, made_ref[:, start : start + tile], preferred_element_type=F32)
        done = (both[:count] + both[count:]).astype(BF16)
        for k, ref in enumerate((o0_ref, o1_ref, o2_ref, o3_ref)):
            ref[:, start : start + tile] = done[k * rows_z : (k + 1) * rows_z]


def down_last(spread, first, hidden, down_held):
    experts, slots, width = first.shape
    count = spread.shape[0] // 2
    return pl.pallas_call(
        down_last_kernel,
        in_specs=[whole()] * 4,
        out_specs=[whole()] * 4,
        out_shape=[VMEM((count // 4, width), BF16)] * 4,
        scratch_shapes=[VMEM((experts * count, width), BF16)],
        compiler_params=pltpu.CompilerParams(vmem_limit_bytes=12 * MIB),
        cost_estimate=pl.CostEstimate(
            flops=4 * experts * count * count * width,
            bytes_accessed=8 * experts * slots * width,
            transcendentals=0,
        ),
    )(spread, first, hidden, down_held)


def collect_kernel(p0_ref, p1_ref, p2_ref, p3_ref, own_ref, core_ref, x_ref, far_ref):
    total = p0_ref[...].astype(F32)
    for ref in (p1_ref, p2_ref, p3_ref):
        total += ref[...].astype(F32)
    rows = own_ref.shape[0]
    first = jnp.bitwise_and(lax.axis_index("dp"), 1) == 0
    near = [total[k * rows : (k + 1) * rows] for k in range(4)]
    own_ref[...] = jnp.where(first, near[0], near[1]).astype(BF16)
    core_ref[...] = jnp.where(first, near[1], near[0]).astype(BF16)
    x_ref[...] = jnp.where(first, near[2], near[3]).astype(BF16)
    far_ref[...] = jnp.where(first, near[3], near[2]).astype(BF16)


def collect(partials):
    rows, width = partials[0].shape
    return pl.pallas_call(
        collect_kernel,
        in_specs=[whole()] * 4,
        out_specs=[whole()] * 4,
        out_shape=[VMEM((rows // 4, width), BF16)] * 4,
        compiler_params=pltpu.CompilerParams(vmem_limit_bytes=2 * MIB),
        cost_estimate=pl.CostEstimate(
            flops=4 * rows * width, bytes_accessed=8 * rows * width, transcendentals=0
        ),
    )(*partials)


def place_kernel(p0_ref, p1_ref, p2_ref, p3_ref, out_ref):
    place = lax.axis_index("dp")
    width = p0_ref.shape[1]
    for k, ref in enumerate((p0_ref, p1_ref, p2_ref, p3_ref)):
        at = pl.multiple_of(jnp.bitwise_xor(place, k) * width, width)
        out_ref[:, pl.ds(at, width)] = ref[...]


def place_all(pieces):
    rows, width = pieces[0].shape
    return pl.pallas_call(
        place_kernel,
        in_specs=[whole()] * 4,
        out_specs=whole(),
        out_shape=jax.ShapeDtypeStruct((rows, 4 * width), BF16),
        compiler_params=pltpu.CompilerParams(vmem_limit_bytes=2 * MIB),
        cost_estimate=pl.CostEstimate(
            flops=0, bytes_accessed=16 * rows * width, transcendentals=0
        ),
    )(*pieces)


def swap(value, axis, bit):
    size = lax.axis_size(axis)
    return lax.ppermute(value, axis, [(i, i ^ bit) for i in range(size)])


def routed_four(
    hidden_rows,
    expert_ids,
    gate_values,
    gate_proj,
    up_proj,
    down_proj,
    queries,
    latent_cache,
    cache_lengths,
):
    rows_dev, feature_count = hidden_rows.shape
    local_experts = gate_proj.shape[0]
    width = down_proj.shape[2]
    experts_all = local_experts * 4
    capacity = max(2, 3 * rows_dev * expert_ids.shape[1] // (2 * experts_all))
    sent = pack(hidden_rows, expert_ids, gate_values, experts_all)
    along_z = [sent] + [swap(sent, "expert", k) for k in (1, 2, 3)]
    near_x = swap(jnp.stack(along_z[:2]), "dp", 2)
    gate_first, up_first, passed = fetch(
        gate_proj, up_proj, 0, local_experts // 2, along_z[1:2]
    )
    along_z[2:] = [once_done(block, gate_first) for block in along_z[2:]]
    far_x = swap(jnp.stack(along_z[2:]), "dp", 2)
    gate_next, up_next, mine_z = fetch(
        gate_proj, up_proj, local_experts // 2, local_experts, [along_z[0], passed[0]] + along_z[2:]
    )
    mine_x = jnp.concatenate([near_x, far_x])
    other_z = swap(mine_z, "dp", 1)
    other_x = swap(mine_x, "dp", 1)

    hidden, spread = gate_up(
        (mine_z, mine_x, other_z, other_x),
        (gate_first, up_first, gate_next, up_next),
        16 * capacity,
        experts_all,
    )
    hidden_x = swap(hidden, "dp", 2)
    hidden_c = swap(hidden, "dp", 1)
    attended, down_held = attend_and_fetch(
        queries, latent_cache, cache_lengths, down_proj, hidden
    )
    hidden_x = once_done(hidden_x, down_held)
    hidden_xc = swap(hidden_x, "dp", 1)
    first = down_first((hidden, hidden_c, hidden_x), down_held)
    partial = down_last(spread, first, hidden_xc, down_held)
    arrived = [partial[0]] + [swap(partial[k], "expert", k) for k in (3, 2, 1)]
    own, to_core, to_x, to_far = collect(arrived)
    far = swap(to_far, "dp", 3)
    blended = place_all((own, swap(to_core, "dp", 1), swap(to_x, "dp", 2), far))
    return blended, attended


def routed_any(hidden_rows, expert_ids, gate_values, gate_proj, up_proj, down_proj):
    rows_dev, feature_count = hidden_rows.shape
    local_experts = gate_proj.shape[0]
    width = down_proj.shape[2]
    owners = lax.axis_size("expert")
    members = lax.axis_size("dp")
    experts_all = local_experts * owners
    table = gate_table(expert_ids, gate_values, experts_all)
    rows = lax.all_gather(hidden_rows, ("expert", "dp"), axis=0, tiled=True)
    table = lax.all_gather(table, ("expert", "dp"), axis=0, tiled=True)
    table = lax.dynamic_slice_in_dim(
        table, lax.axis_index("expert") * local_experts, local_experts, axis=1
    )
    total = jnp.zeros((rows.shape[0], width), F32)
    for e in range(local_experts):
        gate = jnp.dot(rows, gate_proj[e], preferred_element_type=F32)
        up = jnp.dot(rows, up_proj[e], preferred_element_type=F32)
        share = (jax.nn.silu(gate) * up).astype(BF16)
        hidden = lax.all_gather(share, "dp", axis=1, tiled=True)
        made = jnp.dot(hidden, down_proj[e], preferred_element_type=F32).astype(BF16)
        total += table[:, e : e + 1] * made.astype(F32)
    partial = total.astype(BF16).reshape(owners, members, rows_dev, width)
    returned = lax.all_to_all(
        lax.all_to_all(partial, "expert", split_axis=0, concat_axis=0, tiled=True),
        "dp",
        split_axis=1,
        concat_axis=1,
        tiled=True,
    )
    blended = jnp.sum(returned.astype(F32), axis=0).astype(BF16)
    return jnp.transpose(blended, (1, 0, 2)).reshape(rows_dev, members * width)


def local(
    hidden_rows,
    expert_ids,
    gate_values,
    gate_proj,
    up_proj,
    down_proj,
    queries,
    latent_cache,
    cache_lengths,
):
    routing = (hidden_rows, expert_ids, gate_values, gate_proj, up_proj, down_proj)
    attention = (queries, latent_cache, cache_lengths)
    four = lax.axis_size("expert") == 4 and lax.axis_size("dp") == 4
    if four and hidden_rows.shape[0] == 8 and 12 * gate_proj.shape[0] <= 128:
        return routed_four(*routing, *attention)
    return routed_any(*routing), attend(*attention)


def solution(mesh):
    return jax.shard_map(
        local,
        mesh=mesh,
        in_specs=(
            P(("groups", "expert", "dp"), None),
            P(("groups", "expert", "dp"), None),
            P(("groups", "expert", "dp"), None),
            P("expert", None, "dp"),
            P("expert", None, "dp"),
            P("expert", None, "dp"),
            P(("groups", "expert", "dp"), None, None),
            P(("groups", "expert", "dp"), None, None),
            P(("groups", "expert", "dp")),
        ),
        out_specs=(P(("groups", "expert", "dp"), None), P(("groups", "expert", "dp"), None, None)),
        check_vma=False,
    )
```

```python
import jax
import jax.numpy as jnp
from jax import lax
from jax.experimental import pallas as pl
from jax.experimental.pallas import tpu as pltpu
from jax.sharding import PartitionSpec as P

LATENT = 512
F32 = jnp.float32
BF16 = jnp.bfloat16
VMEM = pltpu.VMEM
MIB = 1024 * 1024


softmax_scale = 192.0 ** (-0.5)


def attend_rows(lengths_ref, queries_ref, cache_ref, out_ref):
    for r in range(queries_ref.shape[0]):
        queries = queries_ref[r].T
        cache = cache_ref[r]
        scores = jnp.dot(queries, cache, preferred_element_type=F32) * softmax_scale
        usable = lax.broadcasted_iota(jnp.int32, scores.shape, 1) < lengths_ref[r]
        scores = jnp.where(usable, scores, -1e30)
        weights = jnp.exp(scores - jnp.max(scores, axis=1, keepdims=True))
        weights = weights / jnp.sum(weights, axis=1, keepdims=True)
        out_ref[r] = lax.dot_general(
            weights.astype(BF16),
            cache[:LATENT],
            (((1,), (1,)), ((), ())),
            preferred_element_type=F32,
        ).astype(BF16)


def attend_cost(queries, latent_cache):
    rows, heads, width = queries.shape
    positions = latent_cache.shape[1]
    return pl.CostEstimate(
        flops=2 * rows * heads * positions * (width + LATENT),
        bytes_accessed=2 * rows * (positions * width + heads * (width + LATENT)),
        transcendentals=rows * heads * positions,
    )


def in_hbm(array):
    return pltpu.with_memory_space_constraint(array, pltpu.HBM)


def in_vmem(array):
    return pltpu.with_memory_space_constraint(array, VMEM)


def whole(space=VMEM):
    return pl.BlockSpec(memory_space=space)


def attend(queries, latent_cache, cache_lengths):
    rows, heads, _ = queries.shape
    return pl.pallas_call(
        attend_rows,
        in_specs=[whole(pltpu.SMEM), whole(), whole()],
        out_specs=whole(),
        out_shape=jax.ShapeDtypeStruct((rows, heads, LATENT), BF16),
        compiler_params=pltpu.CompilerParams(vmem_limit_bytes=16 * MIB),
        cost_estimate=attend_cost(queries, latent_cache),
    )(cache_lengths, jnp.swapaxes(queries, 1, 2), jnp.swapaxes(latent_cache, 1, 2))


def attend_and_fetch_kernel(
    lengths_ref, queries_ref, cache_ref, source_ref, after_ref, out_ref, held_ref, sem
):
    copy = pltpu.make_async_copy(source_ref, held_ref, sem)
    copy.start()
    attend_rows(lengths_ref, queries_ref, cache_ref, out_ref)
    copy.wait()


def attend_and_fetch(queries, latent_cache, cache_lengths, weights, after):
    rows, heads, _ = queries.shape
    return pl.pallas_call(
        attend_and_fetch_kernel,
        in_specs=[whole(pltpu.SMEM), whole(), whole(), whole(pltpu.HBM), whole(pl.ANY)],
        out_specs=[whole(), whole()],
        out_shape=[
            jax.ShapeDtypeStruct((rows, heads, LATENT), BF16),
            VMEM(weights.shape, weights.dtype),
        ],
        scratch_shapes=[pltpu.SemaphoreType.DMA],
        compiler_params=pltpu.CompilerParams(vmem_limit_bytes=12 * MIB),
        cost_estimate=attend_cost(queries, latent_cache),
    )(
        cache_lengths,
        jnp.swapaxes(queries, 1, 2),
        jnp.swapaxes(latent_cache, 1, 2),
        in_hbm(weights),
        after,
    )


def once_done(value, other):
    return pl.pallas_call(
        lambda *refs: None,
        in_specs=[whole(pl.ANY)] * 2,
        out_specs=whole(pl.ANY),
        out_shape=VMEM(value.shape, value.dtype),
        input_output_aliases={0: 0},
        compiler_params=pltpu.CompilerParams(vmem_limit_bytes=MIB),
        cost_estimate=pl.CostEstimate(flops=0, bytes_accessed=0, transcendentals=0),
    )(value, other)


def fetch_kernel(start, gate_ref, up_ref, *refs):
    *piece_refs, gate_held_ref, up_held_ref, stack_ref, sems = refs
    copies = []
    for source_ref, held_ref in ((gate_ref, gate_held_ref), (up_ref, up_held_ref)):
        for e in range(held_ref.shape[0]):
            copies.append(
                pltpu.make_async_copy(
                    source_ref.at[start + e], held_ref.at[e], sems.at[len(copies)]
                )
            )
    for copy in copies:
        copy.start()
    for k, piece_ref in enumerate(piece_refs):
        stack_ref[k] = piece_ref[...]
    for copy in copies:
        copy.wait()


def fetch(gate_proj, up_proj, start, stop, pieces):
    held = VMEM((stop - start,) + gate_proj.shape[1:], gate_proj.dtype)
    return pl.pallas_call(
        lambda *refs: fetch_kernel(start, *refs),
        in_specs=[whole(pltpu.HBM)] * 2 + [whole()] * len(pieces),
        out_specs=[whole()] * 3,
        out_shape=[held, held, VMEM((len(pieces),) + pieces[0].shape, pieces[0].dtype)],
        scratch_shapes=[pltpu.SemaphoreType.DMA((2 * (stop - start),))],
        compiler_params=pltpu.CompilerParams(vmem_limit_bytes=2 * MIB),
        cost_estimate=pl.CostEstimate(
            flops=0,
            bytes_accessed=4 * (stop - start) * gate_proj[0].size,
            transcendentals=0,
        ),
    )(in_hbm(gate_proj), in_hbm(up_proj), *pieces)


def gate_table(expert_ids, gate_values, experts_all):
    chosen = expert_ids[:, :, None] == jnp.arange(experts_all, dtype=jnp.int32)[None, None, :]
    return jnp.sum(jnp.where(chosen, gate_values[:, :, None], 0.0), axis=1)


def pack_kernel(experts_all, rows_in, ids_in, gates_in, out_ref, ids_ref, gates_ref, sems):
    rows, feature_count = rows_in.shape
    copies = [
        pltpu.make_async_copy(ids_in, ids_ref, sems.at[0]),
        pltpu.make_async_copy(gates_in, gates_ref, sems.at[1]),
        pltpu.make_async_copy(rows_in, out_ref.at[:, :feature_count], sems.at[2]),
    ]
    for copy in copies:
        copy.start()
    copies[0].wait()
    copies[1].wait()
    lane = lax.broadcasted_iota(jnp.int32, (rows, out_ref.shape[1] - feature_count), 1)
    expert = lax.rem(lane, experts_all)
    table = jnp.zeros(lane.shape, F32)
    for k in range(ids_ref.shape[1]):
        table += jnp.where(ids_ref[:, k : k + 1] == expert, gates_ref[:, k : k + 1], 0.0)
    high = table.astype(BF16).astype(F32)
    middle = (table - high).astype(BF16).astype(F32)
    low = table - high - middle
    coded = jnp.where(
        lane < experts_all,
        high,
        jnp.where(
            lane < 2 * experts_all, middle, jnp.where(lane < 3 * experts_all, low, 0.0)
        ),
    )
    out_ref[:, feature_count:] = coded.astype(BF16)
    copies[2].wait()


def pack(hidden_rows, expert_ids, gate_values, experts_all):
    rows, feature_count = hidden_rows.shape
    return pl.pallas_call(
        lambda *refs: pack_kernel(experts_all, *refs),
        in_specs=[whole(pltpu.HBM)] * 3,
        out_specs=whole(),
        out_shape=VMEM((rows, feature_count + 128), BF16),
        scratch_shapes=[
            VMEM(expert_ids.shape, jnp.int32),
            VMEM(gate_values.shape, F32),
            pltpu.SemaphoreType.DMA((3,)),
        ],
        compiler_params=pltpu.CompilerParams(vmem_limit_bytes=2 * MIB),
        cost_estimate=pl.CostEstimate(
            flops=0, bytes_accessed=4 * rows * feature_count, transcendentals=0
        ),
    )(in_hbm(hidden_rows), in_hbm(expert_ids), in_hbm(gate_values))


def gate_up_kernel(
    slots,
    experts_all,
    mine_z_ref,
    other_z_ref,
    mine_x_ref,
    other_x_ref,
    gate_first_ref,
    up_first_ref,
    gate_next_ref,
    up_next_ref,
    hidden_ref,
    spread_ref,
    rows_ref,
):
    matrices = []
    for pair in ((gate_first_ref, up_first_ref), (gate_next_ref, up_next_ref)):
        matrices += [[ref.at[e] for ref in pair] for e in range(pair[0].shape[0])]
    experts = len(matrices)
    depth = gate_first_ref.shape[1]
    groups = (mine_z_ref, other_z_ref, mine_x_ref, other_x_ref)
    rows_group, total_width = mine_z_ref.shape
    count = 4 * rows_group
    lanes = total_width - depth
    for g, ref in enumerate(groups):
        rows_ref[g * rows_group : (g + 1) * rows_group] = ref[:, :depth]
    coded = jnp.concatenate([ref[:, depth:] for ref in groups], axis=0)
    def activated(e):
        gate = jnp.dot(rows_ref[...], matrices[e][0][...], preferred_element_type=F32)
        up = jnp.dot(rows_ref[...], matrices[e][1][...], preferred_element_type=F32)
        return (gate / (1.0 + jnp.exp(-gate)) * up).astype(BF16)

    made = activated(0)
    source = lax.broadcasted_iota(jnp.int32, (lanes, lanes), 0)
    target = lax.broadcasted_iota(jnp.int32, (lanes, lanes), 1)
    selector = (
        (lax.rem(source, experts_all) == lax.axis_index("expert") * experts + target)
        & (target < experts)
        & (source < 3 * experts_all)
    )
    table = jnp.dot(coded, selector.astype(F32).astype(BF16), preferred_element_type=F32)
    chosen = (table > 0.0).astype(F32).astype(BF16)
    row = lax.broadcasted_iota(jnp.int32, (count, count), 0)
    column = lax.broadcasted_iota(jnp.int32, (count, count), 1)
    turn = lax.axis_index("dp") * rows_group
    ahead = jnp.bitwise_xor(column, turn) < jnp.bitwise_xor(row, turn)
    rank = jnp.dot(ahead.astype(F32).astype(BF16), chosen, preferred_element_type=F32)
    rank = jnp.where(table > 0.0, rank, -1.0)
    rank_across = rank.T
    slot = column.astype(F32)
    slot_down = row.astype(F32)[:slots]
    for e in range(experts):
        later = activated(e + 1) if e + 1 < experts else None
        value = jnp.where(rank[:, e : e + 1] == slot, table[:, e : e + 1], 0.0)
        high = value.astype(BF16)
        spread_ref[:count, e * count : (e + 1) * count] = high
        spread_ref[count:, e * count : (e + 1) * count] = (value - high.astype(F32)).astype(BF16)
        to_slot = (rank_across[e : e + 1] == slot_down).astype(F32).astype(BF16)
        hidden_ref[e] = jnp.dot(to_slot, made, preferred_element_type=F32).astype(BF16)
        made = later


def gate_up(pieces, held, slots, experts_all):
    _, depth, share = held[0].shape
    experts = sum(array.shape[0] for array in held[::2])
    count = 4 * pieces[0].shape[0]
    return pl.pallas_call(
        lambda *refs: gate_up_kernel(slots, experts_all, *refs),
        in_specs=[whole()] * 8,
        out_specs=[whole()] * 2,
        out_shape=[
            VMEM((experts, slots, share), BF16),
            VMEM((2 * count, experts * count), BF16),
        ],
        scratch_shapes=[VMEM((count, depth), BF16)],
        compiler_params=pltpu.CompilerParams(vmem_limit_bytes=16 * MIB),
        cost_estimate=pl.CostEstimate(
            flops=4 * experts * count * depth * share,
            bytes_accessed=4 * experts * depth * share,
            transcendentals=experts * count * share,
        ),
    )(*pieces, *held)


def down_first_kernel(h0_ref, h1_ref, h2_ref, down_ref, made_ref):
    place = lax.axis_index("dp")
    experts, slots, share = h0_ref.shape
    for e in range(experts):
        made = jnp.zeros(made_ref.shape[1:], F32)
        for k, ref in enumerate((h0_ref, h1_ref, h2_ref)):
            owner = jnp.bitwise_xor(place, k)
            weights = down_ref[e, pl.ds(pl.multiple_of(owner * share, share), share)]
            made += jnp.dot(ref[e], weights, preferred_element_type=F32)
        made_ref[e] = made


def down_first(hidden, down_held):
    experts, slots, share = hidden[0].shape
    width = down_held.shape[2]
    return pl.pallas_call(
        down_first_kernel,
        in_specs=[whole()] * 4,
        out_specs=whole(),
        out_shape=VMEM((experts, slots, width), F32),
        compiler_params=pltpu.CompilerParams(vmem_limit_bytes=8 * MIB),
        cost_estimate=pl.CostEstimate(
            flops=6 * experts * slots * share * width,
            bytes_accessed=4 * experts * slots * width,
            transcendentals=0,
        ),
    )(*hidden, down_held)


def down_last_kernel(
    spread_ref, first_ref, h3_ref, down_ref, o0_ref, o1_ref, o2_ref, o3_ref, made_ref
):
    owner = jnp.bitwise_xor(lax.axis_index("dp"), 3)
    experts, slots, share = h3_ref.shape
    width = down_ref.shape[2]
    count = spread_ref.shape[0] // 2
    rows_z = o0_ref.shape[0]
    tile = 256
    for e in range(experts):
        if slots < count:
            made_ref[e * count + slots : (e + 1) * count] = jnp.zeros(
                (count - slots, width), BF16
            )
        weights = down_ref[e, pl.ds(pl.multiple_of(owner * share, share), share)]
        made = first_ref[e] + jnp.dot(h3_ref[e], weights, preferred_element_type=F32)
        made_ref[e * count : e * count + slots] = made.astype(BF16)
    spread = spread_ref[...]
    for start in range(0, width, tile):
        both = jnp.dot(spread, made_ref[:, start : start + tile], preferred_element_type=F32)
        done = both[:count] + both[count:]
        rows = rows_z // 4
        for k, ref in enumerate((o0_ref, o1_ref, o2_ref, o3_ref)):
            parts = [
                done[g * rows_z + k * rows : g * rows_z + (k + 1) * rows] for g in range(4)
            ]
            ref[:, start : start + tile] = jnp.concatenate(parts, axis=0).astype(BF16)


def down_last(spread, first, hidden, down_held):
    experts, slots, width = first.shape
    count = spread.shape[0] // 2
    return pl.pallas_call(
        down_last_kernel,
        in_specs=[whole()] * 4,
        out_specs=[whole()] * 4,
        out_shape=[VMEM((count // 4, width), BF16)] * 4,
        scratch_shapes=[VMEM((experts * count, width), BF16)],
        compiler_params=pltpu.CompilerParams(vmem_limit_bytes=12 * MIB),
        cost_estimate=pl.CostEstimate(
            flops=4 * experts * count * count * width,
            bytes_accessed=8 * experts * slots * width,
            transcendentals=0,
        ),
    )(spread, first, hidden, down_held)


def collect_kernel(p0_ref, p1_ref, p2_ref, p3_ref, own_ref, core_ref, x_ref, far_ref):
    total = p0_ref[...].astype(F32)
    for ref in (p1_ref, p2_ref, p3_ref):
        total += ref[...].astype(F32)
    rows = own_ref.shape[0]
    for k, ref in enumerate((own_ref, core_ref, x_ref, far_ref)):
        ref[...] = total[k * rows : (k + 1) * rows].astype(BF16)


def collect(partials):
    rows, width = partials[0].shape
    return pl.pallas_call(
        collect_kernel,
        in_specs=[whole()] * 4,
        out_specs=[whole()] * 4,
        out_shape=[VMEM((rows // 4, width), BF16)] * 4,
        compiler_params=pltpu.CompilerParams(vmem_limit_bytes=2 * MIB),
        cost_estimate=pl.CostEstimate(
            flops=4 * rows * width, bytes_accessed=8 * rows * width, transcendentals=0
        ),
    )(*partials)


def place_kernel(p0_ref, p1_ref, p2_ref, p3_ref, out_ref):
    place = lax.axis_index("dp")
    width = p0_ref.shape[1]
    for k, ref in enumerate((p0_ref, p1_ref, p2_ref, p3_ref)):
        at = pl.multiple_of(jnp.bitwise_xor(place, k) * width, width)
        out_ref[:, pl.ds(at, width)] = ref[...]


def place_all(pieces):
    rows, width = pieces[0].shape
    return pl.pallas_call(
        place_kernel,
        in_specs=[whole()] * 4,
        out_specs=whole(),
        out_shape=jax.ShapeDtypeStruct((rows, 4 * width), BF16),
        compiler_params=pltpu.CompilerParams(vmem_limit_bytes=2 * MIB),
        cost_estimate=pl.CostEstimate(
            flops=0, bytes_accessed=16 * rows * width, transcendentals=0
        ),
    )(*pieces)


def swap(value, axis, bit):
    size = lax.axis_size(axis)
    return lax.ppermute(value, axis, [(i, i ^ bit) for i in range(size)])


def routed_four(
    hidden_rows,
    expert_ids,
    gate_values,
    gate_proj,
    up_proj,
    down_proj,
    queries,
    latent_cache,
    cache_lengths,
):
    rows_dev, feature_count = hidden_rows.shape
    local_experts = gate_proj.shape[0]
    width = down_proj.shape[2]
    experts_all = local_experts * 4
    capacity = max(2, 3 * rows_dev * expert_ids.shape[1] // (2 * experts_all))
    sent = pack(hidden_rows, expert_ids, gate_values, experts_all)
    along_z = [sent] + [swap(sent, "expert", k) for k in (1, 2, 3)]
    near_x = swap(jnp.stack(along_z[:2]), "dp", 2)
    gate_first, up_first, passed = fetch(
        gate_proj, up_proj, 0, local_experts // 2, along_z[1:2]
    )
    along_z[2:] = [once_done(block, gate_first) for block in along_z[2:]]
    far_x = swap(jnp.stack(along_z[2:]), "dp", 2)
    gate_next, up_next, mine_z = fetch(
        gate_proj, up_proj, local_experts // 2, local_experts, [along_z[0], passed[0]] + along_z[2:]
    )
    mine_x = jnp.concatenate([near_x, far_x])
    other_z = swap(mine_z, "dp", 1)
    other_x = swap(mine_x, "dp", 1)

    hidden, spread = gate_up(
        [block.reshape(4 * rows_dev, -1) for block in (mine_z, other_z, mine_x, other_x)],
        (gate_first, up_first, gate_next, up_next),
        16 * capacity,
        experts_all,
    )
    hidden_x = swap(hidden, "dp", 2)
    hidden_c = swap(hidden, "dp", 1)
    attended, down_held = attend_and_fetch(
        queries, latent_cache, cache_lengths, down_proj, hidden
    )
    hidden_x = once_done(hidden_x, down_held)
    hidden_xc = swap(hidden_x, "dp", 1)
    first = down_first((hidden, hidden_c, hidden_x), down_held)
    partial = down_last(spread, first, hidden_xc, down_held)
    arrived = [partial[0]] + [swap(partial[k], "expert", k) for k in (3, 2, 1)]
    own, to_core, to_x, to_far = collect(arrived)
    far = swap(to_far, "dp", 3)
    blended = place_all((own, swap(to_core, "dp", 1), swap(to_x, "dp", 2), far))
    return blended, attended


def routed_any(hidden_rows, expert_ids, gate_values, gate_proj, up_proj, down_proj):
    rows_dev, feature_count = hidden_rows.shape
    local_experts = gate_proj.shape[0]
    width = down_proj.shape[2]
    owners = lax.axis_size("expert")
    members = lax.axis_size("dp")
    experts_all = local_experts * owners
    table = gate_table(expert_ids, gate_values, experts_all)
    rows = lax.all_gather(hidden_rows, ("expert", "dp"), axis=0, tiled=True)
    table = lax.all_gather(table, ("expert", "dp"), axis=0, tiled=True)
    table = lax.dynamic_slice_in_dim(
        table, lax.axis_index("expert") * local_experts, local_experts, axis=1
    )
    total = jnp.zeros((rows.shape[0], width), F32)
    for e in range(local_experts):
        gate = jnp.dot(rows, gate_proj[e], preferred_element_type=F32)
        up = jnp.dot(rows, up_proj[e], preferred_element_type=F32)
        share = (jax.nn.silu(gate) * up).astype(BF16)
        hidden = lax.all_gather(share, "dp", axis=1, tiled=True)
        made = jnp.dot(hidden, down_proj[e], preferred_element_type=F32).astype(BF16)
        total += table[:, e : e + 1] * made.astype(F32)
    partial = total.astype(BF16).reshape(owners, members, rows_dev, width)
    returned = lax.all_to_all(
        lax.all_to_all(partial, "expert", split_axis=0, concat_axis=0, tiled=True),
        "dp",
        split_axis=1,
        concat_axis=1,
        tiled=True,
    )
    blended = jnp.sum(returned.astype(F32), axis=0).astype(BF16)
    return jnp.transpose(blended, (1, 0, 2)).reshape(rows_dev, members * width)


def local(
    hidden_rows,
    expert_ids,
    gate_values,
    gate_proj,
    up_proj,
    down_proj,
    queries,
    latent_cache,
    cache_lengths,
):
    routing = (hidden_rows, expert_ids, gate_values, gate_proj, up_proj, down_proj)
    attention = (queries, latent_cache, cache_lengths)
    four = lax.axis_size("expert") == 4 and lax.axis_size("dp") == 4
    if four and hidden_rows.shape[0] == 8 and 12 * gate_proj.shape[0] <= 128:
        return routed_four(*routing, *attention)
    return routed_any(*routing), attend(*attention)


def solution(mesh):
    return jax.shard_map(
        local,
        mesh=mesh,
        in_specs=(
            P(("groups", "expert", "dp"), None),
            P(("groups", "expert", "dp"), None),
            P(("groups", "expert", "dp"), None),
            P("expert", None, "dp"),
            P("expert", None, "dp"),
            P("expert", None, "dp"),
            P(("groups", "expert", "dp"), None, None),
            P(("groups", "expert", "dp"), None, None),
            P(("groups", "expert", "dp")),
        ),
        out_specs=(P(("groups", "expert", "dp"), None), P(("groups", "expert", "dp"), None, None)),
        check_vma=False,
    )
```

```python
import jax
import jax.numpy as jnp
from jax import lax
from jax.experimental import pallas as pl
from jax.experimental.pallas import tpu as pltpu
from jax.sharding import PartitionSpec as P

LATENT = 512
F32 = jnp.float32
BF16 = jnp.bfloat16
VMEM = pltpu.VMEM
MIB = 1024 * 1024


softmax_scale = 192.0 ** (-0.5)


def attend_rows(lengths_ref, queries_ref, cache_ref, out_ref):
    for r in range(queries_ref.shape[0]):
        queries = queries_ref[r].T
        cache = cache_ref[r]
        scores = jnp.dot(queries, cache, preferred_element_type=F32) * softmax_scale
        usable = lax.broadcasted_iota(jnp.int32, scores.shape, 1) < lengths_ref[r]
        scores = jnp.where(usable, scores, -1e30)
        weights = jnp.exp(scores - jnp.max(scores, axis=1, keepdims=True))
        weights = weights / jnp.sum(weights, axis=1, keepdims=True)
        out_ref[r] = lax.dot_general(
            weights.astype(BF16),
            cache[:LATENT],
            (((1,), (1,)), ((), ())),
            preferred_element_type=F32,
        ).astype(BF16)


def attend_cost(queries, latent_cache):
    rows, heads, width = queries.shape
    positions = latent_cache.shape[1]
    return pl.CostEstimate(
        flops=2 * rows * heads * positions * (width + LATENT),
        bytes_accessed=2 * rows * (positions * width + heads * (width + LATENT)),
        transcendentals=rows * heads * positions,
    )


def in_hbm(array):
    return pltpu.with_memory_space_constraint(array, pltpu.HBM)


def in_vmem(array):
    return pltpu.with_memory_space_constraint(array, VMEM)


def whole(space=VMEM):
    return pl.BlockSpec(memory_space=space)


def attend(queries, latent_cache, cache_lengths):
    rows, heads, _ = queries.shape
    return pl.pallas_call(
        attend_rows,
        in_specs=[whole(pltpu.SMEM), whole(), whole()],
        out_specs=whole(),
        out_shape=jax.ShapeDtypeStruct((rows, heads, LATENT), BF16),
        compiler_params=pltpu.CompilerParams(vmem_limit_bytes=16 * MIB),
        cost_estimate=attend_cost(queries, latent_cache),
    )(cache_lengths, jnp.swapaxes(queries, 1, 2), jnp.swapaxes(latent_cache, 1, 2))


def attend_and_fetch_kernel(
    lengths_ref, queries_ref, cache_ref, source_ref, after_ref, out_ref, held_ref, sem
):
    copy = pltpu.make_async_copy(source_ref, held_ref, sem)
    copy.start()
    attend_rows(lengths_ref, queries_ref, cache_ref, out_ref)
    copy.wait()


def attend_and_fetch(queries, latent_cache, cache_lengths, weights, after):
    rows, heads, _ = queries.shape
    return pl.pallas_call(
        attend_and_fetch_kernel,
        in_specs=[whole(pltpu.SMEM), whole(), whole(), whole(pltpu.HBM), whole(pl.ANY)],
        out_specs=[whole(), whole()],
        out_shape=[
            jax.ShapeDtypeStruct((rows, heads, LATENT), BF16),
            VMEM(weights.shape, weights.dtype),
        ],
        scratch_shapes=[pltpu.SemaphoreType.DMA],
        compiler_params=pltpu.CompilerParams(vmem_limit_bytes=12 * MIB),
        cost_estimate=attend_cost(queries, latent_cache),
    )(
        cache_lengths,
        jnp.swapaxes(queries, 1, 2),
        jnp.swapaxes(latent_cache, 1, 2),
        in_hbm(weights),
        after,
    )


def once_done(value, other):
    return pl.pallas_call(
        lambda *refs: None,
        in_specs=[whole(pl.ANY)] * 2,
        out_specs=whole(pl.ANY),
        out_shape=VMEM(value.shape, value.dtype),
        input_output_aliases={0: 0},
        compiler_params=pltpu.CompilerParams(vmem_limit_bytes=MIB),
        cost_estimate=pl.CostEstimate(flops=4000000000, bytes_accessed=0, transcendentals=0),
    )(value, other)


def gate_table(expert_ids, gate_values, experts_all):
    chosen = expert_ids[:, :, None] == jnp.arange(experts_all, dtype=jnp.int32)[None, None, :]
    return jnp.sum(jnp.where(chosen, gate_values[:, :, None], 0.0), axis=1)


def pack_kernel(experts_all, rows_in, ids_in, gates_in, out_ref, ids_ref, gates_ref, sems):
    rows, feature_count = rows_in.shape
    copies = [
        pltpu.make_async_copy(ids_in, ids_ref, sems.at[0]),
        pltpu.make_async_copy(gates_in, gates_ref, sems.at[1]),
        pltpu.make_async_copy(rows_in, out_ref.at[:, :feature_count], sems.at[2]),
    ]
    for copy in copies:
        copy.start()
    copies[0].wait()
    copies[1].wait()
    lane = lax.broadcasted_iota(jnp.int32, (rows, out_ref.shape[1] - feature_count), 1)
    expert = lax.rem(lane, experts_all)
    table = jnp.zeros(lane.shape, F32)
    for k in range(ids_ref.shape[1]):
        table += jnp.where(ids_ref[:, k : k + 1] == expert, gates_ref[:, k : k + 1], 0.0)
    high = table.astype(BF16).astype(F32)
    middle = (table - high).astype(BF16).astype(F32)
    low = table - high - middle
    coded = jnp.where(
        lane < experts_all,
        high,
        jnp.where(
            lane < 2 * experts_all, middle, jnp.where(lane < 3 * experts_all, low, 0.0)
        ),
    )
    out_ref[:, feature_count:] = coded.astype(BF16)
    copies[2].wait()


def pack(hidden_rows, expert_ids, gate_values, experts_all):
    rows, feature_count = hidden_rows.shape
    return pl.pallas_call(
        lambda *refs: pack_kernel(experts_all, *refs),
        in_specs=[whole(pltpu.HBM)] * 3,
        out_specs=whole(),
        out_shape=VMEM((rows, feature_count + 128), BF16),
        scratch_shapes=[
            VMEM(expert_ids.shape, jnp.int32),
            VMEM(gate_values.shape, F32),
            pltpu.SemaphoreType.DMA((3,)),
        ],
        compiler_params=pltpu.CompilerParams(vmem_limit_bytes=2 * MIB),
        cost_estimate=pl.CostEstimate(
            flops=0, bytes_accessed=4 * rows * feature_count, transcendentals=0
        ),
    )(in_hbm(hidden_rows), in_hbm(expert_ids), in_hbm(gate_values))


def gate_up_kernel(
    slots,
    experts_all,
    mine_z_ref,
    other_z_ref,
    mine_x_ref,
    other_x_ref,
    gate_first_ref,
    up_first_ref,
    hidden_ref,
    spread_ref,
    rows_ref,
):
    matrices = []
    for pair in ((gate_first_ref, up_first_ref),):
        matrices += [[ref.at[e] for ref in pair] for e in range(pair[0].shape[0])]
    experts = len(matrices)
    depth = gate_first_ref.shape[1]
    groups = (mine_z_ref, other_z_ref, mine_x_ref, other_x_ref)
    rows_group, total_width = mine_z_ref.shape
    count = 4 * rows_group
    lanes = total_width - depth
    for g, ref in enumerate(groups):
        rows_ref[g * rows_group : (g + 1) * rows_group] = ref[:, :depth]
    coded = jnp.concatenate([ref[:, depth:] for ref in groups], axis=0)
    def activated(e):
        gate = jnp.dot(rows_ref[...], matrices[e][0][...], preferred_element_type=F32)
        up = jnp.dot(rows_ref[...], matrices[e][1][...], preferred_element_type=F32)
        return (gate / (1.0 + jnp.exp(-gate)) * up).astype(BF16)

    made = activated(0)
    source = lax.broadcasted_iota(jnp.int32, (lanes, lanes), 0)
    target = lax.broadcasted_iota(jnp.int32, (lanes, lanes), 1)
    selector = (
        (lax.rem(source, experts_all) == lax.axis_index("expert") * experts + target)
        & (target < experts)
        & (source < 3 * experts_all)
    )
    table = jnp.dot(coded, selector.astype(F32).astype(BF16), preferred_element_type=F32)
    chosen = (table > 0.0).astype(F32).astype(BF16)
    row = lax.broadcasted_iota(jnp.int32, (count, count), 0)
    column = lax.broadcasted_iota(jnp.int32, (count, count), 1)
    turn = lax.axis_index("dp") * rows_group
    ahead = jnp.bitwise_xor(column, turn) < jnp.bitwise_xor(row, turn)
    rank = jnp.dot(ahead.astype(F32).astype(BF16), chosen, preferred_element_type=F32)
    rank = jnp.where(table > 0.0, rank, -1.0)
    rank_across = rank.T
    slot = column.astype(F32)
    slot_down = row.astype(F32)[:slots]
    for e in range(experts):
        later = activated(e + 1) if e + 1 < experts else None
        value = jnp.where(rank[:, e : e + 1] == slot, table[:, e : e + 1], 0.0)
        high = value.astype(BF16)
        spread_ref[:count, e * count : (e + 1) * count] = high
        spread_ref[count:, e * count : (e + 1) * count] = (value - high.astype(F32)).astype(BF16)
        to_slot = (rank_across[e : e + 1] == slot_down).astype(F32).astype(BF16)
        hidden_ref[e] = jnp.dot(to_slot, made, preferred_element_type=F32).astype(BF16)
        made = later


def gate_up(pieces, held, slots, experts_all):
    _, depth, share = held[0].shape
    experts = sum(array.shape[0] for array in held[::2])
    count = 4 * pieces[0].shape[0]
    return pl.pallas_call(
        lambda *refs: gate_up_kernel(slots, experts_all, *refs),
        in_specs=[whole()] * 6,
        out_specs=[whole()] * 2,
        out_shape=[
            VMEM((experts, slots, share), BF16),
            VMEM((2 * count, experts * count), BF16),
        ],
        scratch_shapes=[VMEM((count, depth), BF16)],
        compiler_params=pltpu.CompilerParams(vmem_limit_bytes=36 * MIB),
        cost_estimate=pl.CostEstimate(
            flops=4 * experts * count * depth * share,
            bytes_accessed=4 * experts * depth * share,
            transcendentals=experts * count * share,
        ),
    )(*pieces, *held)


def down_first_kernel(h0_ref, h1_ref, h2_ref, down_ref, made_ref):
    place = lax.axis_index("dp")
    experts, slots, share = h0_ref.shape
    for e in range(experts):
        made = jnp.zeros(made_ref.shape[1:], F32)
        for k, ref in enumerate((h0_ref, h1_ref, h2_ref)):
            owner = jnp.bitwise_xor(place, k)
            weights = down_ref[e, pl.ds(pl.multiple_of(owner * share, share), share)]
            made += jnp.dot(ref[e], weights, preferred_element_type=F32)
        made_ref[e] = made


def down_first(hidden, down_held):
    experts, slots, share = hidden[0].shape
    width = down_held.shape[2]
    return pl.pallas_call(
        down_first_kernel,
        in_specs=[whole()] * 4,
        out_specs=whole(),
        out_shape=VMEM((experts, slots, width), F32),
        compiler_params=pltpu.CompilerParams(vmem_limit_bytes=8 * MIB),
        cost_estimate=pl.CostEstimate(
            flops=6 * experts * slots * share * width,
            bytes_accessed=4 * experts * slots * width,
            transcendentals=0,
        ),
    )(*hidden, down_held)


def down_last_kernel(
    spread_ref, first_ref, h3_ref, down_ref, o0_ref, o1_ref, o2_ref, o3_ref, made_ref
):
    owner = jnp.bitwise_xor(lax.axis_index("dp"), 3)
    experts, slots, share = h3_ref.shape
    width = down_ref.shape[2]
    count = spread_ref.shape[0] // 2
    rows_z = o0_ref.shape[0]
    tile = 256
    for e in range(experts):
        if slots < count:
            made_ref[e * count + slots : (e + 1) * count] = jnp.zeros(
                (count - slots, width), BF16
            )
        weights = down_ref[e, pl.ds(pl.multiple_of(owner * share, share), share)]
        made = first_ref[e] + jnp.dot(h3_ref[e], weights, preferred_element_type=F32)
        made_ref[e * count : e * count + slots] = made.astype(BF16)
    spread = spread_ref[...]
    for start in range(0, width, tile):
        both = jnp.dot(spread, made_ref[:, start : start + tile], preferred_element_type=F32)
        done = both[:count] + both[count:]
        rows = rows_z // 4
        for k, ref in enumerate((o0_ref, o1_ref, o2_ref, o3_ref)):
            parts = [
                done[g * rows_z + k * rows : g * rows_z + (k + 1) * rows] for g in range(4)
            ]
            ref[:, start : start + tile] = jnp.concatenate(parts, axis=0).astype(BF16)


def down_last(spread, first, hidden, down_held):
    experts, slots, width = first.shape
    count = spread.shape[0] // 2
    return pl.pallas_call(
        down_last_kernel,
        in_specs=[whole()] * 4,
        out_specs=[whole()] * 4,
        out_shape=[VMEM((count // 4, width), BF16)] * 4,
        scratch_shapes=[VMEM((experts * count, width), BF16)],
        compiler_params=pltpu.CompilerParams(vmem_limit_bytes=12 * MIB),
        cost_estimate=pl.CostEstimate(
            flops=4 * experts * count * count * width,
            bytes_accessed=8 * experts * slots * width,
            transcendentals=0,
        ),
    )(spread, first, hidden, down_held)


def collect_kernel(p0_ref, p1_ref, p2_ref, p3_ref, own_ref, core_ref, x_ref, far_ref):
    total = p0_ref[...].astype(F32)
    for ref in (p1_ref, p2_ref, p3_ref):
        total += ref[...].astype(F32)
    rows = own_ref.shape[0]
    for k, ref in enumerate((own_ref, core_ref, x_ref, far_ref)):
        ref[...] = total[k * rows : (k + 1) * rows].astype(BF16)


def collect(partials):
    rows, width = partials[0].shape
    return pl.pallas_call(
        collect_kernel,
        in_specs=[whole()] * 4,
        out_specs=[whole()] * 4,
        out_shape=[VMEM((rows // 4, width), BF16)] * 4,
        compiler_params=pltpu.CompilerParams(vmem_limit_bytes=2 * MIB),
        cost_estimate=pl.CostEstimate(
            flops=4 * rows * width, bytes_accessed=8 * rows * width, transcendentals=0
        ),
    )(*partials)


def place_kernel(p0_ref, p1_ref, p2_ref, p3_ref, out_ref):
    place = lax.axis_index("dp")
    width = p0_ref.shape[1]
    for k, ref in enumerate((p0_ref, p1_ref, p2_ref, p3_ref)):
        at = pl.multiple_of(jnp.bitwise_xor(place, k) * width, width)
        out_ref[:, pl.ds(at, width)] = ref[...]


def place_all(pieces):
    rows, width = pieces[0].shape
    return pl.pallas_call(
        place_kernel,
        in_specs=[whole()] * 4,
        out_specs=whole(),
        out_shape=jax.ShapeDtypeStruct((rows, 4 * width), BF16),
        compiler_params=pltpu.CompilerParams(vmem_limit_bytes=2 * MIB),
        cost_estimate=pl.CostEstimate(
            flops=0, bytes_accessed=16 * rows * width, transcendentals=0
        ),
    )(*pieces)


def swap(value, axis, bit):
    size = lax.axis_size(axis)
    return lax.ppermute(value, axis, [(i, i ^ bit) for i in range(size)])


def routed_four(
    hidden_rows,
    expert_ids,
    gate_values,
    gate_proj,
    up_proj,
    down_proj,
    queries,
    latent_cache,
    cache_lengths,
):
    rows_dev, feature_count = hidden_rows.shape
    local_experts = gate_proj.shape[0]
    width = down_proj.shape[2]
    experts_all = local_experts * 4
    capacity = max(2, 3 * rows_dev * expert_ids.shape[1] // (2 * experts_all))
    sent = pack(hidden_rows, expert_ids, gate_values, experts_all)
    along_z = [sent] + [swap(sent, "expert", k) for k in (1, 2, 3)]
    along_z[1:] = [once_done(block, sent) for block in along_z[1:]]
    along_x = [swap(block, "dp", 2) for block in along_z]
    mine_z, mine_x = jnp.stack(along_z), jnp.stack(along_x)
    other_z = swap(mine_z, "dp", 1)
    other_x = swap(mine_x, "dp", 1)

    hidden, spread = gate_up(
        [block.reshape(4 * rows_dev, -1) for block in (mine_z, other_z, mine_x, other_x)],
        (gate_proj, up_proj),
        16 * capacity,
        experts_all,
    )
    hidden_x = swap(hidden, "dp", 2)
    hidden_c = swap(hidden, "dp", 1)
    attended, down_held = attend_and_fetch(
        queries, latent_cache, cache_lengths, down_proj, hidden
    )
    hidden_x = once_done(hidden_x, down_held)
    hidden_xc = swap(hidden_x, "dp", 1)
    first = down_first((hidden, hidden_c, hidden_x), down_held)
    partial = down_last(spread, first, hidden_xc, down_held)
    arrived = [partial[0]] + [swap(partial[k], "expert", k) for k in (3, 2, 1)]
    own, to_core, to_x, to_far = collect(arrived)
    far = swap(to_far, "dp", 3)
    blended = place_all((own, swap(to_core, "dp", 1), swap(to_x, "dp", 2), far))
    return blended, attended


def routed_any(hidden_rows, expert_ids, gate_values, gate_proj, up_proj, down_proj):
    rows_dev, feature_count = hidden_rows.shape
    local_experts = gate_proj.shape[0]
    width = down_proj.shape[2]
    owners = lax.axis_size("expert")
    members = lax.axis_size("dp")
    experts_all = local_experts * owners
    table = gate_table(expert_ids, gate_values, experts_all)
    rows = lax.all_gather(hidden_rows, ("expert", "dp"), axis=0, tiled=True)
    table = lax.all_gather(table, ("expert", "dp"), axis=0, tiled=True)
    table = lax.dynamic_slice_in_dim(
        table, lax.axis_index("expert") * local_experts, local_experts, axis=1
    )
    total = jnp.zeros((rows.shape[0], width), F32)
    for e in range(local_experts):
        gate = jnp.dot(rows, gate_proj[e], preferred_element_type=F32)
        up = jnp.dot(rows, up_proj[e], preferred_element_type=F32)
        share = (jax.nn.silu(gate) * up).astype(BF16)
        hidden = lax.all_gather(share, "dp", axis=1, tiled=True)
        made = jnp.dot(hidden, down_proj[e], preferred_element_type=F32).astype(BF16)
        total += table[:, e : e + 1] * made.astype(F32)
    partial = total.astype(BF16).reshape(owners, members, rows_dev, width)
    returned = lax.all_to_all(
        lax.all_to_all(partial, "expert", split_axis=0, concat_axis=0, tiled=True),
        "dp",
        split_axis=1,
        concat_axis=1,
        tiled=True,
    )
    blended = jnp.sum(returned.astype(F32), axis=0).astype(BF16)
    return jnp.transpose(blended, (1, 0, 2)).reshape(rows_dev, members * width)


def local(
    hidden_rows,
    expert_ids,
    gate_values,
    gate_proj,
    up_proj,
    down_proj,
    queries,
    latent_cache,
    cache_lengths,
):
    routing = (hidden_rows, expert_ids, gate_values, gate_proj, up_proj, down_proj)
    attention = (queries, latent_cache, cache_lengths)
    four = lax.axis_size("expert") == 4 and lax.axis_size("dp") == 4
    if four and hidden_rows.shape[0] == 8 and 12 * gate_proj.shape[0] <= 128:
        return routed_four(*routing, *attention)
    return routed_any(*routing), attend(*attention)


def solution(mesh):
    return jax.shard_map(
        local,
        mesh=mesh,
        in_specs=(
            P(("groups", "expert", "dp"), None),
            P(("groups", "expert", "dp"), None),
            P(("groups", "expert", "dp"), None),
            P("expert", None, "dp"),
            P("expert", None, "dp"),
            P("expert", None, "dp"),
            P(("groups", "expert", "dp"), None, None),
            P(("groups", "expert", "dp"), None, None),
            P(("groups", "expert", "dp")),
        ),
        out_specs=(P(("groups", "expert", "dp"), None), P(("groups", "expert", "dp"), None, None)),
        check_vma=False,
    )
```

```python
import jax
import jax.numpy as jnp
from jax import lax
from jax.experimental import pallas as pl
from jax.experimental.pallas import tpu as pltpu
from jax.sharding import PartitionSpec as P

LATENT = 512
F32 = jnp.float32
BF16 = jnp.bfloat16
VMEM = pltpu.VMEM
MIB = 1024 * 1024


softmax_scale = 192.0 ** (-0.5)


def attend_rows(lengths_ref, queries_ref, cache_ref, out_ref):
    for r in range(queries_ref.shape[0]):
        queries = queries_ref[r].T
        cache = cache_ref[r]
        scores = jnp.dot(queries, cache, preferred_element_type=F32) * softmax_scale
        usable = lax.broadcasted_iota(jnp.int32, scores.shape, 1) < lengths_ref[r]
        scores = jnp.where(usable, scores, -1e30)
        weights = jnp.exp(scores - jnp.max(scores, axis=1, keepdims=True))
        weights = weights / jnp.sum(weights, axis=1, keepdims=True)
        out_ref[r] = lax.dot_general(
            weights.astype(BF16),
            cache[:LATENT],
            (((1,), (1,)), ((), ())),
            preferred_element_type=F32,
        ).astype(BF16)


def attend_cost(queries, latent_cache):
    rows, heads, width = queries.shape
    positions = latent_cache.shape[1]
    return pl.CostEstimate(
        flops=2 * rows * heads * positions * (width + LATENT),
        bytes_accessed=2 * rows * (positions * width + heads * (width + LATENT)),
        transcendentals=rows * heads * positions,
    )


def in_hbm(array):
    return pltpu.with_memory_space_constraint(array, pltpu.HBM)


def in_vmem(array):
    return pltpu.with_memory_space_constraint(array, VMEM)


def whole(space=VMEM):
    return pl.BlockSpec(memory_space=space)


def attend(queries, latent_cache, cache_lengths):
    rows, heads, _ = queries.shape
    return pl.pallas_call(
        attend_rows,
        in_specs=[whole(pltpu.SMEM), whole(), whole()],
        out_specs=whole(),
        out_shape=jax.ShapeDtypeStruct((rows, heads, LATENT), BF16),
        compiler_params=pltpu.CompilerParams(vmem_limit_bytes=16 * MIB),
        cost_estimate=attend_cost(queries, latent_cache),
    )(cache_lengths, jnp.swapaxes(queries, 1, 2), jnp.swapaxes(latent_cache, 1, 2))


def attend_after_kernel(lengths_ref, queries_ref, cache_ref, after_ref, out_ref):
    attend_rows(lengths_ref, queries_ref, cache_ref, out_ref)


def attend_after(queries, latent_cache, cache_lengths, after):
    rows, heads, _ = queries.shape
    return pl.pallas_call(
        attend_after_kernel,
        in_specs=[whole(pltpu.SMEM), whole(), whole(), whole(pl.ANY)],
        out_specs=whole(),
        out_shape=jax.ShapeDtypeStruct((rows, heads, LATENT), BF16),
        compiler_params=pltpu.CompilerParams(vmem_limit_bytes=8 * MIB),
        cost_estimate=pl.CostEstimate(
            flops=4 * 10**9, bytes_accessed=0, transcendentals=0
        ),
    )(
        cache_lengths,
        jnp.swapaxes(queries, 1, 2),
        jnp.swapaxes(latent_cache, 1, 2),
        after,
    )


def once_done(value, other, flops=0):
    return pl.pallas_call(
        lambda *refs: None,
        in_specs=[whole(pl.ANY)] * 2,
        out_specs=whole(pl.ANY),
        out_shape=VMEM(value.shape, value.dtype),
        input_output_aliases={0: 0},
        compiler_params=pltpu.CompilerParams(vmem_limit_bytes=MIB),
        cost_estimate=pl.CostEstimate(flops=flops, bytes_accessed=0, transcendentals=0),
    )(value, other)


def gate_table(expert_ids, gate_values, experts_all):
    chosen = expert_ids[:, :, None] == jnp.arange(experts_all, dtype=jnp.int32)[None, None, :]
    return jnp.sum(jnp.where(chosen, gate_values[:, :, None], 0.0), axis=1)


def pack_kernel(experts_all, rows_in, ids_in, gates_in, out_ref, ids_ref, gates_ref, sems):
    rows, feature_count = rows_in.shape
    copies = [
        pltpu.make_async_copy(ids_in, ids_ref, sems.at[0]),
        pltpu.make_async_copy(gates_in, gates_ref, sems.at[1]),
        pltpu.make_async_copy(rows_in, out_ref.at[:, :feature_count], sems.at[2]),
    ]
    for copy in copies:
        copy.start()
    copies[0].wait()
    copies[1].wait()
    lane = lax.broadcasted_iota(jnp.int32, (rows, out_ref.shape[1] - feature_count), 1)
    expert = lax.rem(lane, experts_all)
    table = jnp.zeros(lane.shape, F32)
    for k in range(ids_ref.shape[1]):
        table += jnp.where(ids_ref[:, k : k + 1] == expert, gates_ref[:, k : k + 1], 0.0)
    high = table.astype(BF16).astype(F32)
    middle = (table - high).astype(BF16).astype(F32)
    low = table - high - middle
    coded = jnp.where(
        lane < experts_all,
        high,
        jnp.where(
            lane < 2 * experts_all, middle, jnp.where(lane < 3 * experts_all, low, 0.0)
        ),
    )
    out_ref[:, feature_count:] = coded.astype(BF16)
    copies[2].wait()


def pack(hidden_rows, expert_ids, gate_values, experts_all):
    rows, feature_count = hidden_rows.shape
    return pl.pallas_call(
        lambda *refs: pack_kernel(experts_all, *refs),
        in_specs=[whole(pltpu.HBM)] * 3,
        out_specs=whole(),
        out_shape=VMEM((rows, feature_count + 128), BF16),
        scratch_shapes=[
            VMEM(expert_ids.shape, jnp.int32),
            VMEM(gate_values.shape, F32),
            pltpu.SemaphoreType.DMA((3,)),
        ],
        compiler_params=pltpu.CompilerParams(vmem_limit_bytes=2 * MIB),
        cost_estimate=pl.CostEstimate(
            flops=0, bytes_accessed=4 * rows * feature_count, transcendentals=0
        ),
    )(in_hbm(hidden_rows), in_hbm(expert_ids), in_hbm(gate_values))


def activated(rows, gate_ref, up_ref):
    gate = jnp.dot(rows, gate_ref[...], preferred_element_type=F32)
    up = jnp.dot(rows, up_ref[...], preferred_element_type=F32)
    return (gate / (1.0 + jnp.exp(-gate)) * up).astype(BF16)


def compacted(made, rank_row, slots):
    slot = lax.broadcasted_iota(jnp.int32, (slots, rank_row.shape[1]), 0).astype(F32)
    to_slot = (rank_row == slot).astype(F32).astype(BF16)
    return jnp.dot(to_slot, made, preferred_element_type=F32).astype(BF16)


def gate_up_first_kernel(experts_all, *refs):
    groups = refs[:4]
    gate_ref, up_ref, hidden_ref, table_ref, rank_ref, across_ref = refs[4:]
    experts, depth, _ = gate_ref.shape
    rows_group, total_width = groups[0].shape
    count = 4 * rows_group
    lanes = total_width - depth
    rows = jnp.concatenate([ref[:, :depth] for ref in groups], axis=0)
    coded = jnp.concatenate([ref[:, depth:] for ref in groups], axis=0)
    made = activated(rows, gate_ref.at[0], up_ref.at[0])
    source = lax.broadcasted_iota(jnp.int32, (lanes, lanes), 0)
    target = lax.broadcasted_iota(jnp.int32, (lanes, lanes), 1)
    selector = (
        (lax.rem(source, experts_all) == lax.axis_index("expert") * experts + target)
        & (target < experts)
        & (source < 3 * experts_all)
    )
    table = jnp.dot(coded, selector.astype(F32).astype(BF16), preferred_element_type=F32)
    chosen = (table > 0.0).astype(F32).astype(BF16)
    row = lax.broadcasted_iota(jnp.int32, (count, count), 0)
    column = lax.broadcasted_iota(jnp.int32, (count, count), 1)
    turn = lax.axis_index("dp") * rows_group
    ahead = jnp.bitwise_xor(column, turn) < jnp.bitwise_xor(row, turn)
    rank = jnp.dot(ahead.astype(F32).astype(BF16), chosen, preferred_element_type=F32)
    rank = jnp.where(table > 0.0, rank, -1.0)
    across = rank.T
    table_ref[...], rank_ref[...], across_ref[...] = table, rank, across
    part, slots, _ = hidden_ref.shape
    for e in range(part):
        later = activated(rows, gate_ref.at[e + 1], up_ref.at[e + 1]) if e + 1 < part else None
        hidden_ref[e] = compacted(made, across[e : e + 1], slots)
        made = later


def gate_up_next_kernel(*refs):
    groups = refs[:4]
    gate_ref, up_ref, first_ref, table_ref, rank_ref, across_ref = refs[4:10]
    hidden_ref, all_ref, spread_ref = refs[10:]
    experts, depth, _ = gate_ref.shape
    rows = jnp.concatenate([ref[:, :depth] for ref in groups], axis=0)
    count = rows.shape[0]
    done, slots, _ = first_ref.shape
    made = activated(rows, gate_ref.at[done], up_ref.at[done])
    all_ref[:done] = first_ref[...]
    slot = lax.broadcasted_iota(jnp.int32, (count, count), 1).astype(F32)
    table, rank = table_ref[...], rank_ref[...]
    for e in range(experts):
        value = jnp.where(rank[:, e : e + 1] == slot, table[:, e : e + 1], 0.0)
        high = value.astype(BF16)
        spread_ref[:count, e * count : (e + 1) * count] = high
        spread_ref[count:, e * count : (e + 1) * count] = (value - high.astype(F32)).astype(BF16)
    for e in range(done, experts):
        later = (
            activated(rows, gate_ref.at[e + 1], up_ref.at[e + 1]) if e + 1 < experts else None
        )
        hidden = compacted(made, across_ref[e : e + 1], slots)
        hidden_ref[e - done] = hidden
        all_ref[e] = hidden
        made = later


def half_cost(gate_proj, count):
    size = gate_proj.size // 2
    return pl.CostEstimate(flops=4 * count * size, bytes_accessed=4 * size, transcendentals=0)


def gate_up_first(pieces, gate_proj, up_proj, part, slots, experts_all):
    _, depth, share = gate_proj.shape
    rows_group, total_width = pieces[0].shape
    count = 4 * rows_group
    square = VMEM((count, total_width - depth), F32)
    return pl.pallas_call(
        lambda *refs: gate_up_first_kernel(experts_all, *refs),
        in_specs=[whole()] * 6,
        out_specs=[whole()] * 4,
        out_shape=[
            VMEM((part, slots, share), BF16),
            square,
            square,
            VMEM((total_width - depth, count), F32),
        ],
        compiler_params=pltpu.CompilerParams(vmem_limit_bytes=28 * MIB),
        cost_estimate=half_cost(gate_proj, count),
    )(*pieces, gate_proj, up_proj)


def gate_up_next(pieces, gate_proj, up_proj, first, table, rank, across):
    experts, depth, share = gate_proj.shape
    done, slots, _ = first.shape
    count = 4 * pieces[0].shape[0]
    return pl.pallas_call(
        gate_up_next_kernel,
        in_specs=[whole()] * 10,
        out_specs=[whole()] * 3,
        out_shape=[
            VMEM((experts - done, slots, share), BF16),
            VMEM((experts, slots, share), BF16),
            VMEM((2 * count, experts * count), BF16),
        ],
        compiler_params=pltpu.CompilerParams(vmem_limit_bytes=28 * MIB),
        cost_estimate=half_cost(gate_proj, count),
    )(*pieces, gate_proj, up_proj, first, table, rank, across)


def down_part_kernel(start, h0_ref, h1_ref, h2_ref, down_ref, made_ref):
    place = lax.axis_index("dp")
    share = h0_ref.shape[2]
    for e in range(h2_ref.shape[0]):
        made = jnp.zeros(made_ref.shape[1:], F32)
        for k, ref in enumerate((h0_ref.at[start + e], h1_ref.at[start + e], h2_ref.at[e])):
            owner = jnp.bitwise_xor(place, k)
            weights = down_ref[start + e, pl.ds(pl.multiple_of(owner * share, share), share)]
            made += jnp.dot(ref[...], weights, preferred_element_type=F32)
        made_ref[e] = made


def down_part(start, hidden, down_proj):
    part, slots, share = hidden[2].shape
    width = down_proj.shape[2]
    return pl.pallas_call(
        lambda *refs: down_part_kernel(start, *refs),
        in_specs=[whole()] * 4,
        out_specs=whole(),
        out_shape=VMEM((part, slots, width), F32),
        compiler_params=pltpu.CompilerParams(vmem_limit_bytes=20 * MIB),
        cost_estimate=pl.CostEstimate(
            flops=6 * part * slots * share * width,
            bytes_accessed=4 * part * slots * width,
            transcendentals=0,
        ),
    )(*hidden, down_proj)


def down_last_kernel(
    spread_ref,
    begun_first_ref,
    begun_next_ref,
    h3_first_ref,
    h3_next_ref,
    down_ref,
    o0_ref,
    o1_ref,
    o2_ref,
    o3_ref,
    made_ref,
):
    owner = jnp.bitwise_xor(lax.axis_index("dp"), 3)
    part, slots, share = h3_first_ref.shape
    experts, _, width = down_ref.shape
    count = spread_ref.shape[0] // 2
    rows_z = o0_ref.shape[0]
    tile = 256
    for e in range(experts):
        if slots < count:
            made_ref[e * count + slots : (e + 1) * count] = jnp.zeros(
                (count - slots, width), BF16
            )
        weights = down_ref[e, pl.ds(pl.multiple_of(owner * share, share), share)]
        if e < part:
            begun, far = begun_first_ref[e], h3_first_ref[e]
        else:
            begun, far = begun_next_ref[e - part], h3_next_ref[e - part]
        made = begun + jnp.dot(far, weights, preferred_element_type=F32)
        made_ref[e * count : e * count + slots] = made.astype(BF16)
    spread = spread_ref[...]
    for start in range(0, width, tile):
        both = jnp.dot(spread, made_ref[:, start : start + tile], preferred_element_type=F32)
        done = both[:count] + both[count:]
        rows = rows_z // 4
        for k, ref in enumerate((o0_ref, o1_ref, o2_ref, o3_ref)):
            parts = [
                done[g * rows_z + k * rows : g * rows_z + (k + 1) * rows] for g in range(4)
            ]
            ref[:, start : start + tile] = jnp.concatenate(parts, axis=0).astype(BF16)


def down_last(spread, begun, hidden, down_proj):
    experts, _, width = down_proj.shape
    slots = hidden[0].shape[1]
    count = spread.shape[0] // 2
    return pl.pallas_call(
        down_last_kernel,
        in_specs=[whole()] * 6,
        out_specs=[whole()] * 4,
        out_shape=[VMEM((count // 4, width), BF16)] * 4,
        scratch_shapes=[VMEM((experts * count, width), BF16)],
        compiler_params=pltpu.CompilerParams(vmem_limit_bytes=20 * MIB),
        cost_estimate=pl.CostEstimate(
            flops=4 * experts * count * count * width,
            bytes_accessed=8 * experts * slots * width,
            transcendentals=0,
        ),
    )(spread, *begun, *hidden, down_proj)


def collect_kernel(p0_ref, p1_ref, p2_ref, p3_ref, own_ref, core_ref, x_ref, far_ref):
    total = p0_ref[...].astype(F32)
    for ref in (p1_ref, p2_ref, p3_ref):
        total += ref[...].astype(F32)
    rows = own_ref.shape[0]
    for k, ref in enumerate((own_ref, core_ref, x_ref, far_ref)):
        ref[...] = total[k * rows : (k + 1) * rows].astype(BF16)


def collect(partials):
    rows, width = partials[0].shape
    return pl.pallas_call(
        collect_kernel,
        in_specs=[whole()] * 4,
        out_specs=[whole()] * 4,
        out_shape=[VMEM((rows // 4, width), BF16)] * 4,
        compiler_params=pltpu.CompilerParams(vmem_limit_bytes=2 * MIB),
        cost_estimate=pl.CostEstimate(
            flops=4 * rows * width, bytes_accessed=8 * rows * width, transcendentals=0
        ),
    )(*partials)


def place_kernel(p0_ref, p1_ref, p2_ref, p3_ref, out_ref):
    place = lax.axis_index("dp")
    width = p0_ref.shape[1]
    for k, ref in enumerate((p0_ref, p1_ref, p2_ref, p3_ref)):
        at = pl.multiple_of(jnp.bitwise_xor(place, k) * width, width)
        out_ref[:, pl.ds(at, width)] = ref[...]


def place_all(pieces):
    rows, width = pieces[0].shape
    return pl.pallas_call(
        place_kernel,
        in_specs=[whole()] * 4,
        out_specs=whole(),
        out_shape=jax.ShapeDtypeStruct((rows, 4 * width), BF16),
        compiler_params=pltpu.CompilerParams(vmem_limit_bytes=2 * MIB),
        cost_estimate=pl.CostEstimate(
            flops=0, bytes_accessed=16 * rows * width, transcendentals=0
        ),
    )(*pieces)


def swap(value, axis, bit):
    size = lax.axis_size(axis)
    return lax.ppermute(value, axis, [(i, i ^ bit) for i in range(size)])


def routed_four(
    hidden_rows,
    expert_ids,
    gate_values,
    gate_proj,
    up_proj,
    down_proj,
    queries,
    latent_cache,
    cache_lengths,
):
    rows_dev, feature_count = hidden_rows.shape
    local_experts = gate_proj.shape[0]
    width = down_proj.shape[2]
    experts_all = local_experts * 4
    capacity = max(2, 3 * rows_dev * expert_ids.shape[1] // (2 * experts_all))
    sent = pack(hidden_rows, expert_ids, gate_values, experts_all)
    along_z = [sent] + [swap(sent, "expert", k) for k in (1, 2, 3)]
    along_z[1:] = [once_done(block, sent, 4 * 10**9) for block in along_z[1:]]
    along_x = [swap(block, "dp", 2) for block in along_z]
    mine_z, mine_x = jnp.stack(along_z), jnp.stack(along_x)
    other_z = swap(mine_z, "dp", 1)
    other_x = swap(mine_x, "dp", 1)

    pieces = [block.reshape(4 * rows_dev, -1) for block in (mine_z, other_z, mine_x, other_x)]
    half = local_experts // 2
    hidden_first, table, rank, across = gate_up_first(
        pieces, gate_proj, up_proj, half, 16 * capacity, experts_all
    )
    first_x = swap(hidden_first, "dp", 2)
    hidden_next, hidden, spread = gate_up_next(
        pieces, gate_proj, up_proj, hidden_first, table, rank, across
    )
    next_x = swap(hidden_next, "dp", 2)
    hidden_c = swap(hidden, "dp", 1)
    attended = attend_after(queries, latent_cache, cache_lengths, hidden_next)
    first_x = once_done(first_x, in_hbm(attended))
    first_far = swap(first_x, "dp", 1)
    begun_first = down_part(0, (hidden, hidden_c, first_x), down_proj)
    next_x = once_done(next_x, begun_first)
    next_far = swap(next_x, "dp", 1)
    begun_next = down_part(half, (hidden, hidden_c, next_x), down_proj)
    partial = down_last(spread, (begun_first, begun_next), (first_far, next_far), down_proj)
    arrived = [partial[0]] + [swap(partial[k], "expert", k) for k in (3, 2, 1)]
    own, to_core, to_x, to_far = collect(arrived)
    far = swap(to_far, "dp", 3)
    blended = place_all((own, swap(to_core, "dp", 1), swap(to_x, "dp", 2), far))
    return blended, attended


def routed_any(hidden_rows, expert_ids, gate_values, gate_proj, up_proj, down_proj):
    rows_dev, feature_count = hidden_rows.shape
    local_experts = gate_proj.shape[0]
    width = down_proj.shape[2]
    owners = lax.axis_size("expert")
    members = lax.axis_size("dp")
    experts_all = local_experts * owners
    table = gate_table(expert_ids, gate_values, experts_all)
    rows = lax.all_gather(hidden_rows, ("expert", "dp"), axis=0, tiled=True)
    table = lax.all_gather(table, ("expert", "dp"), axis=0, tiled=True)
    table = lax.dynamic_slice_in_dim(
        table, lax.axis_index("expert") * local_experts, local_experts, axis=1
    )
    total = jnp.zeros((rows.shape[0], width), F32)
    for e in range(local_experts):
        gate = jnp.dot(rows, gate_proj[e], preferred_element_type=F32)
        up = jnp.dot(rows, up_proj[e], preferred_element_type=F32)
        share = (jax.nn.silu(gate) * up).astype(BF16)
        hidden = lax.all_gather(share, "dp", axis=1, tiled=True)
        made = jnp.dot(hidden, down_proj[e], preferred_element_type=F32).astype(BF16)
        total += table[:, e : e + 1] * made.astype(F32)
    partial = total.astype(BF16).reshape(owners, members, rows_dev, width)
    returned = lax.all_to_all(
        lax.all_to_all(partial, "expert", split_axis=0, concat_axis=0, tiled=True),
        "dp",
        split_axis=1,
        concat_axis=1,
        tiled=True,
    )
    blended = jnp.sum(returned.astype(F32), axis=0).astype(BF16)
    return jnp.transpose(blended, (1, 0, 2)).reshape(rows_dev, members * width)


def local(
    hidden_rows,
    expert_ids,
    gate_values,
    gate_proj,
    up_proj,
    down_proj,
    queries,
    latent_cache,
    cache_lengths,
):
    routing = (hidden_rows, expert_ids, gate_values, gate_proj, up_proj, down_proj)
    attention = (queries, latent_cache, cache_lengths)
    four = lax.axis_size("expert") == 4 and lax.axis_size("dp") == 4
    if four and hidden_rows.shape[0] == 8 and 12 * gate_proj.shape[0] <= 128:
        return routed_four(*routing, *attention)
    return routed_any(*routing), attend(*attention)


def solution(mesh):
    return jax.shard_map(
        local,
        mesh=mesh,
        in_specs=(
            P(("groups", "expert", "dp"), None),
            P(("groups", "expert", "dp"), None),
            P(("groups", "expert", "dp"), None),
            P("expert", None, "dp"),
            P("expert", None, "dp"),
            P("expert", None, "dp"),
            P(("groups", "expert", "dp"), None, None),
            P(("groups", "expert", "dp"), None, None),
            P(("groups", "expert", "dp")),
        ),
        out_specs=(P(("groups", "expert", "dp"), None), P(("groups", "expert", "dp"), None, None)),
        check_vma=False,
    )
```

```python
import jax
import jax.numpy as jnp
from jax import lax
from jax.experimental import pallas as pl
from jax.experimental.pallas import tpu as pltpu
from jax.sharding import PartitionSpec as P

LATENT = 512
F32 = jnp.float32
BF16 = jnp.bfloat16
VMEM = pltpu.VMEM
MIB = 1024 * 1024


softmax_scale = 192.0 ** (-0.5)


def attend_rows(lengths_ref, queries_ref, cache_ref, out_ref):
    for r in range(queries_ref.shape[0]):
        queries = queries_ref[r].T
        cache = cache_ref[r]
        scores = jnp.dot(queries, cache, preferred_element_type=F32) * softmax_scale
        usable = lax.broadcasted_iota(jnp.int32, scores.shape, 1) < lengths_ref[r]
        scores = jnp.where(usable, scores, -1e30)
        weights = jnp.exp(scores - jnp.max(scores, axis=1, keepdims=True))
        weights = weights / jnp.sum(weights, axis=1, keepdims=True)
        out_ref[r] = lax.dot_general(
            weights.astype(BF16),
            cache[:LATENT],
            (((1,), (1,)), ((), ())),
            preferred_element_type=F32,
        ).astype(BF16)


def attend_cost(queries, latent_cache):
    rows, heads, width = queries.shape
    positions = latent_cache.shape[1]
    return pl.CostEstimate(
        flops=2 * rows * heads * positions * (width + LATENT),
        bytes_accessed=2 * rows * (positions * width + heads * (width + LATENT)),
        transcendentals=rows * heads * positions,
    )


def in_hbm(array):
    return pltpu.with_memory_space_constraint(array, pltpu.HBM)


def in_vmem(array):
    return pltpu.with_memory_space_constraint(array, VMEM)


def whole(space=VMEM):
    return pl.BlockSpec(memory_space=space)


def attend(queries, latent_cache, cache_lengths):
    rows, heads, _ = queries.shape
    return pl.pallas_call(
        attend_rows,
        in_specs=[whole(pltpu.SMEM), whole(), whole()],
        out_specs=whole(),
        out_shape=jax.ShapeDtypeStruct((rows, heads, LATENT), BF16),
        compiler_params=pltpu.CompilerParams(vmem_limit_bytes=16 * MIB),
        cost_estimate=attend_cost(queries, latent_cache),
    )(cache_lengths, jnp.swapaxes(queries, 1, 2), jnp.swapaxes(latent_cache, 1, 2))


def attend_after_kernel(lengths_ref, queries_ref, cache_ref, after_ref, out_ref):
    attend_rows(lengths_ref, queries_ref, cache_ref, out_ref)


def attend_after(queries, latent_cache, cache_lengths, after):
    rows, heads, _ = queries.shape
    return pl.pallas_call(
        attend_after_kernel,
        in_specs=[whole(pltpu.SMEM), whole(), whole(), whole(pl.ANY)],
        out_specs=whole(),
        out_shape=jax.ShapeDtypeStruct((rows, heads, LATENT), BF16),
        compiler_params=pltpu.CompilerParams(vmem_limit_bytes=8 * MIB),
        cost_estimate=pl.CostEstimate(
            flops=4 * 10**9, bytes_accessed=0, transcendentals=0
        ),
    )(
        cache_lengths,
        jnp.swapaxes(queries, 1, 2),
        jnp.swapaxes(latent_cache, 1, 2),
        after,
    )


def once_done(value, other, flops=0):
    return pl.pallas_call(
        lambda *refs: None,
        in_specs=[whole(pl.ANY)] * 2,
        out_specs=whole(pl.ANY),
        out_shape=VMEM(value.shape, value.dtype),
        input_output_aliases={0: 0},
        compiler_params=pltpu.CompilerParams(vmem_limit_bytes=MIB),
        cost_estimate=pl.CostEstimate(flops=flops, bytes_accessed=0, transcendentals=0),
    )(value, other)


def gate_table(expert_ids, gate_values, experts_all):
    chosen = expert_ids[:, :, None] == jnp.arange(experts_all, dtype=jnp.int32)[None, None, :]
    return jnp.sum(jnp.where(chosen, gate_values[:, :, None], 0.0), axis=1)


def pack_kernel(experts_all, rows_in, ids_in, gates_in, out_ref, ids_ref, gates_ref, sems):
    rows, feature_count = rows_in.shape
    copies = [
        pltpu.make_async_copy(ids_in, ids_ref, sems.at[0]),
        pltpu.make_async_copy(gates_in, gates_ref, sems.at[1]),
        pltpu.make_async_copy(rows_in, out_ref.at[:, :feature_count], sems.at[2]),
    ]
    for copy in copies:
        copy.start()
    copies[0].wait()
    copies[1].wait()
    lane = lax.broadcasted_iota(jnp.int32, (rows, out_ref.shape[1] - feature_count), 1)
    expert = lax.rem(lane, experts_all)
    table = jnp.zeros(lane.shape, F32)
    for k in range(ids_ref.shape[1]):
        table += jnp.where(ids_ref[:, k : k + 1] == expert, gates_ref[:, k : k + 1], 0.0)
    high = table.astype(BF16).astype(F32)
    middle = (table - high).astype(BF16).astype(F32)
    low = table - high - middle
    coded = jnp.where(
        lane < experts_all,
        high,
        jnp.where(
            lane < 2 * experts_all, middle, jnp.where(lane < 3 * experts_all, low, 0.0)
        ),
    )
    out_ref[:, feature_count:] = coded.astype(BF16)
    copies[2].wait()


def pack(hidden_rows, expert_ids, gate_values, experts_all):
    rows, feature_count = hidden_rows.shape
    return pl.pallas_call(
        lambda *refs: pack_kernel(experts_all, *refs),
        in_specs=[whole(pltpu.HBM)] * 3,
        out_specs=whole(),
        out_shape=VMEM((rows, feature_count + 128), BF16),
        scratch_shapes=[
            VMEM(expert_ids.shape, jnp.int32),
            VMEM(gate_values.shape, F32),
            pltpu.SemaphoreType.DMA((3,)),
        ],
        compiler_params=pltpu.CompilerParams(vmem_limit_bytes=2 * MIB),
        cost_estimate=pl.CostEstimate(
            flops=0, bytes_accessed=4 * rows * feature_count, transcendentals=0
        ),
    )(in_hbm(hidden_rows), in_hbm(expert_ids), in_hbm(gate_values))


def activated(rows, gate_ref, up_ref):
    gate = jnp.dot(rows, gate_ref[...], preferred_element_type=F32)
    up = jnp.dot(rows, up_ref[...], preferred_element_type=F32)
    return (gate / (1.0 + jnp.exp(-gate)) * up).astype(BF16)


def compacted(made, rank_row, slots):
    slot = lax.broadcasted_iota(jnp.int32, (slots, rank_row.shape[1]), 0).astype(F32)
    to_slot = (rank_row == slot).astype(F32).astype(BF16)
    return jnp.dot(to_slot, made, preferred_element_type=F32).astype(BF16)


def gate_up_first_kernel(experts_all, *refs):
    groups = refs[:4]
    gate_ref, up_ref, hidden_ref, table_ref, rank_ref, across_ref = refs[4:]
    experts, depth, _ = gate_ref.shape
    rows_group, total_width = groups[0].shape
    count = 4 * rows_group
    lanes = total_width - depth
    rows = jnp.concatenate([ref[:, :depth] for ref in groups], axis=0)
    coded = jnp.concatenate([ref[:, depth:] for ref in groups], axis=0)
    made = activated(rows, gate_ref.at[0], up_ref.at[0])
    source = lax.broadcasted_iota(jnp.int32, (lanes, lanes), 0)
    target = lax.broadcasted_iota(jnp.int32, (lanes, lanes), 1)
    selector = (
        (lax.rem(source, experts_all) == lax.axis_index("expert") * experts + target)
        & (target < experts)
        & (source < 3 * experts_all)
    )
    table = jnp.dot(coded, selector.astype(F32).astype(BF16), preferred_element_type=F32)
    chosen = (table > 0.0).astype(F32).astype(BF16)
    row = lax.broadcasted_iota(jnp.int32, (count, count), 0)
    column = lax.broadcasted_iota(jnp.int32, (count, count), 1)
    turn = lax.axis_index("dp") * rows_group
    ahead = jnp.bitwise_xor(column, turn) < jnp.bitwise_xor(row, turn)
    rank = jnp.dot(ahead.astype(F32).astype(BF16), chosen, preferred_element_type=F32)
    rank = jnp.where(table > 0.0, rank, -1.0)
    across = rank.T
    table_ref[...], rank_ref[...], across_ref[...] = table, rank, across
    part, slots, _ = hidden_ref.shape
    for e in range(part):
        later = activated(rows, gate_ref.at[e + 1], up_ref.at[e + 1]) if e + 1 < part else None
        hidden_ref[e] = compacted(made, across[e : e + 1], slots)
        made = later


def gate_up_next_kernel(*refs):
    groups = refs[:4]
    gate_ref, up_ref, first_ref, table_ref, rank_ref, across_ref = refs[4:10]
    hidden_ref, all_ref, spread_ref = refs[10:]
    experts, depth, _ = gate_ref.shape
    rows = jnp.concatenate([ref[:, :depth] for ref in groups], axis=0)
    count = rows.shape[0]
    done, slots, _ = first_ref.shape
    made = activated(rows, gate_ref.at[done], up_ref.at[done])
    all_ref[:done] = first_ref[...]
    slot = lax.broadcasted_iota(jnp.int32, (count, count), 1).astype(F32)
    table, rank = table_ref[...], rank_ref[...]
    for e in range(experts):
        value = jnp.where(rank[:, e : e + 1] == slot, table[:, e : e + 1], 0.0)
        high = value.astype(BF16)
        spread_ref[:count, e * count : (e + 1) * count] = high
        spread_ref[count:, e * count : (e + 1) * count] = (value - high.astype(F32)).astype(BF16)
    for e in range(done, experts):
        later = (
            activated(rows, gate_ref.at[e + 1], up_ref.at[e + 1]) if e + 1 < experts else None
        )
        hidden = compacted(made, across_ref[e : e + 1], slots)
        hidden_ref[e - done] = hidden
        all_ref[e] = hidden
        made = later


def half_cost(gate_proj, count):
    size = gate_proj.size // 2
    return pl.CostEstimate(flops=4 * count * size, bytes_accessed=4 * size, transcendentals=0)


def gate_up_first(pieces, gate_proj, up_proj, part, slots, experts_all):
    _, depth, share = gate_proj.shape
    rows_group, total_width = pieces[0].shape
    count = 4 * rows_group
    square = VMEM((count, total_width - depth), F32)
    return pl.pallas_call(
        lambda *refs: gate_up_first_kernel(experts_all, *refs),
        in_specs=[whole()] * 6,
        out_specs=[whole()] * 4,
        out_shape=[
            VMEM((part, slots, share), BF16),
            square,
            square,
            VMEM((total_width - depth, count), F32),
        ],
        compiler_params=pltpu.CompilerParams(vmem_limit_bytes=28 * MIB),
        cost_estimate=half_cost(gate_proj, count),
    )(*pieces, gate_proj, up_proj)


def gate_up_next(pieces, gate_proj, up_proj, first, table, rank, across):
    experts, depth, share = gate_proj.shape
    done, slots, _ = first.shape
    count = 4 * pieces[0].shape[0]
    return pl.pallas_call(
        gate_up_next_kernel,
        in_specs=[whole()] * 10,
        out_specs=[whole()] * 3,
        out_shape=[
            VMEM((experts - done, slots, share), BF16),
            VMEM((experts, slots, share), BF16),
            VMEM((2 * count, experts * count), BF16),
        ],
        compiler_params=pltpu.CompilerParams(vmem_limit_bytes=28 * MIB),
        cost_estimate=half_cost(gate_proj, count),
    )(*pieces, gate_proj, up_proj, first, table, rank, across)


def down_part_kernel(start, h0_ref, h1_ref, h2_ref, down_ref, made_ref):
    place = lax.axis_index("dp")
    share = h0_ref.shape[2]
    for e in range(h2_ref.shape[0]):
        made = jnp.zeros(made_ref.shape[1:], F32)
        for k, ref in enumerate((h0_ref.at[start + e], h1_ref.at[start + e], h2_ref.at[e])):
            owner = jnp.bitwise_xor(place, k)
            weights = down_ref[start + e, pl.ds(pl.multiple_of(owner * share, share), share)]
            made += jnp.dot(ref[...], weights, preferred_element_type=F32)
        made_ref[e] = made


def down_part(start, hidden, down_proj):
    part, slots, share = hidden[2].shape
    width = down_proj.shape[2]
    return pl.pallas_call(
        lambda *refs: down_part_kernel(start, *refs),
        in_specs=[whole()] * 4,
        out_specs=whole(),
        out_shape=VMEM((part, slots, width), F32),
        compiler_params=pltpu.CompilerParams(vmem_limit_bytes=20 * MIB),
        cost_estimate=pl.CostEstimate(
            flops=6 * part * slots * share * width,
            bytes_accessed=4 * part * slots * width,
            transcendentals=0,
        ),
    )(*hidden, down_proj)


def down_last_kernel(
    spread_ref,
    begun_first_ref,
    begun_next_ref,
    h3_first_ref,
    h3_next_ref,
    down_ref,
    o0_ref,
    o1_ref,
    o2_ref,
    o3_ref,
    made_ref,
):
    owner = jnp.bitwise_xor(lax.axis_index("dp"), 3)
    part, slots, share = h3_first_ref.shape
    experts, _, width = down_ref.shape
    count = spread_ref.shape[0] // 2
    rows_z = o0_ref.shape[0]
    tile = 256
    for e in range(experts):
        if slots < count:
            made_ref[e * count + slots : (e + 1) * count] = jnp.zeros(
                (count - slots, width), BF16
            )
        weights = down_ref[e, pl.ds(pl.multiple_of(owner * share, share), share)]
        if e < part:
            begun, far = begun_first_ref[e], h3_first_ref[e]
        else:
            begun, far = begun_next_ref[e - part], h3_next_ref[e - part]
        made = begun + jnp.dot(far, weights, preferred_element_type=F32)
        made_ref[e * count : e * count + slots] = made.astype(BF16)
    spread = spread_ref[...]
    for start in range(0, width, tile):
        both = jnp.dot(spread, made_ref[:, start : start + tile], preferred_element_type=F32)
        done = both[:count] + both[count:]
        rows = rows_z // 4
        for k, ref in enumerate((o0_ref, o1_ref, o2_ref, o3_ref)):
            parts = [
                done[g * rows_z + k * rows : g * rows_z + (k + 1) * rows] for g in range(4)
            ]
            ref[:, start : start + tile] = jnp.concatenate(parts, axis=0).astype(BF16)


def down_last(spread, begun, hidden, down_proj):
    experts, _, width = down_proj.shape
    slots = hidden[0].shape[1]
    count = spread.shape[0] // 2
    return pl.pallas_call(
        down_last_kernel,
        in_specs=[whole()] * 6,
        out_specs=[whole()] * 4,
        out_shape=[VMEM((count // 4, width), BF16)] * 4,
        scratch_shapes=[VMEM((experts * count, width), BF16)],
        compiler_params=pltpu.CompilerParams(vmem_limit_bytes=20 * MIB),
        cost_estimate=pl.CostEstimate(
            flops=4 * experts * count * count * width,
            bytes_accessed=8 * experts * slots * width,
            transcendentals=0,
        ),
    )(spread, *begun, *hidden, down_proj)


def collect_kernel(p0_ref, p1_ref, p2_ref, p3_ref, own_ref, core_ref, x_ref, far_ref):
    total = p0_ref[...].astype(F32)
    for ref in (p1_ref, p2_ref, p3_ref):
        total += ref[...].astype(F32)
    rows = own_ref.shape[0]
    for k, ref in enumerate((own_ref, core_ref, x_ref, far_ref)):
        ref[...] = total[k * rows : (k + 1) * rows].astype(BF16)


def collect(partials):
    rows, width = partials[0].shape
    return pl.pallas_call(
        collect_kernel,
        in_specs=[whole()] * 4,
        out_specs=[whole()] * 4,
        out_shape=[VMEM((rows // 4, width), BF16)] * 4,
        compiler_params=pltpu.CompilerParams(vmem_limit_bytes=2 * MIB),
        cost_estimate=pl.CostEstimate(
            flops=4 * rows * width, bytes_accessed=8 * rows * width, transcendentals=0
        ),
    )(*partials)


def place_kernel(p0_ref, p1_ref, p2_ref, p3_ref, out_ref):
    place = lax.axis_index("dp")
    width = p0_ref.shape[1]
    for k, ref in enumerate((p0_ref, p1_ref, p2_ref, p3_ref)):
        at = pl.multiple_of(jnp.bitwise_xor(place, k) * width, width)
        out_ref[:, pl.ds(at, width)] = ref[...]


def place_all(pieces):
    rows, width = pieces[0].shape
    return pl.pallas_call(
        place_kernel,
        in_specs=[whole()] * 4,
        out_specs=whole(),
        out_shape=jax.ShapeDtypeStruct((rows, 4 * width), BF16),
        compiler_params=pltpu.CompilerParams(vmem_limit_bytes=2 * MIB),
        cost_estimate=pl.CostEstimate(
            flops=0, bytes_accessed=16 * rows * width, transcendentals=0
        ),
    )(*pieces)


def swap(value, axis, bit):
    size = lax.axis_size(axis)
    return lax.ppermute(value, axis, [(i, i ^ bit) for i in range(size)])


def routed_four(
    hidden_rows,
    expert_ids,
    gate_values,
    gate_proj,
    up_proj,
    down_proj,
    queries,
    latent_cache,
    cache_lengths,
):
    rows_dev, feature_count = hidden_rows.shape
    local_experts = gate_proj.shape[0]
    width = down_proj.shape[2]
    experts_all = local_experts * 4
    capacity = max(2, 3 * rows_dev * expert_ids.shape[1] // (2 * experts_all))
    sent = pack(hidden_rows, expert_ids, gate_values, experts_all)
    along_z = [sent] + [swap(sent, "expert", k) for k in (2, 1, 3)]
    along_z[1:] = [once_done(block, sent, 4 * 10**9) for block in along_z[1:]]
    along_x = [swap(block, "dp", 2) for block in along_z]
    mine_z, mine_x = jnp.stack(along_z), jnp.stack(along_x)
    other_z = swap(mine_z, "dp", 1)
    other_x = swap(mine_x, "dp", 1)

    pieces = [block.reshape(4 * rows_dev, -1) for block in (mine_z, other_z, mine_x, other_x)]
    half = local_experts // 2
    hidden_first, table, rank, across = gate_up_first(
        pieces, gate_proj, up_proj, half, 16 * capacity, experts_all
    )
    first_x = swap(hidden_first, "dp", 2)
    hidden_next, hidden, spread = gate_up_next(
        pieces, gate_proj, up_proj, hidden_first, table, rank, across
    )
    next_x = swap(hidden_next, "dp", 2)
    hidden_c = swap(hidden, "dp", 1)
    attended = attend_after(queries, latent_cache, cache_lengths, hidden_next)
    first_x = once_done(first_x, in_hbm(attended))
    first_far = swap(first_x, "dp", 1)
    begun_first = down_part(0, (hidden, hidden_c, first_x), down_proj)
    next_x = once_done(next_x, begun_first)
    next_far = swap(next_x, "dp", 1)
    begun_next = down_part(half, (hidden, hidden_c, next_x), down_proj)
    partial = down_last(spread, (begun_first, begun_next), (first_far, next_far), down_proj)
    arrived = [partial[0]] + [swap(partial[j], "expert", k) for j, k in ((3, 3), (2, 1), (1, 2))]
    own, to_core, to_x, to_far = collect(arrived)
    far = swap(to_far, "dp", 3)
    blended = place_all((own, swap(to_core, "dp", 1), swap(to_x, "dp", 2), far))
    return blended, attended


def routed_any(hidden_rows, expert_ids, gate_values, gate_proj, up_proj, down_proj):
    rows_dev, feature_count = hidden_rows.shape
    local_experts = gate_proj.shape[0]
    width = down_proj.shape[2]
    owners = lax.axis_size("expert")
    members = lax.axis_size("dp")
    experts_all = local_experts * owners
    table = gate_table(expert_ids, gate_values, experts_all)
    rows = lax.all_gather(hidden_rows, ("expert", "dp"), axis=0, tiled=True)
    table = lax.all_gather(table, ("expert", "dp"), axis=0, tiled=True)
    table = lax.dynamic_slice_in_dim(
        table, lax.axis_index("expert") * local_experts, local_experts, axis=1
    )
    total = jnp.zeros((rows.shape[0], width), F32)
    for e in range(local_experts):
        gate = jnp.dot(rows, gate_proj[e], preferred_element_type=F32)
        up = jnp.dot(rows, up_proj[e], preferred_element_type=F32)
        share = (jax.nn.silu(gate) * up).astype(BF16)
        hidden = lax.all_gather(share, "dp", axis=1, tiled=True)
        made = jnp.dot(hidden, down_proj[e], preferred_element_type=F32).astype(BF16)
        total += table[:, e : e + 1] * made.astype(F32)
    partial = total.astype(BF16).reshape(owners, members, rows_dev, width)
    returned = lax.all_to_all(
        lax.all_to_all(partial, "expert", split_axis=0, concat_axis=0, tiled=True),
        "dp",
        split_axis=1,
        concat_axis=1,
        tiled=True,
    )
    blended = jnp.sum(returned.astype(F32), axis=0).astype(BF16)
    return jnp.transpose(blended, (1, 0, 2)).reshape(rows_dev, members * width)


def local(
    hidden_rows,
    expert_ids,
    gate_values,
    gate_proj,
    up_proj,
    down_proj,
    queries,
    latent_cache,
    cache_lengths,
):
    routing = (hidden_rows, expert_ids, gate_values, gate_proj, up_proj, down_proj)
    attention = (queries, latent_cache, cache_lengths)
    four = lax.axis_size("expert") == 4 and lax.axis_size("dp") == 4
    if four and hidden_rows.shape[0] == 8 and 12 * gate_proj.shape[0] <= 128:
        return routed_four(*routing, *attention)
    return routed_any(*routing), attend(*attention)


def solution(mesh):
    return jax.shard_map(
        local,
        mesh=mesh,
        in_specs=(
            P(("groups", "expert", "dp"), None),
            P(("groups", "expert", "dp"), None),
            P(("groups", "expert", "dp"), None),
            P("expert", None, "dp"),
            P("expert", None, "dp"),
            P("expert", None, "dp"),
            P(("groups", "expert", "dp"), None, None),
            P(("groups", "expert", "dp"), None, None),
            P(("groups", "expert", "dp")),
        ),
        out_specs=(P(("groups", "expert", "dp"), None), P(("groups", "expert", "dp"), None, None)),
        check_vma=False,
    )
```

```python
import jax
import jax.numpy as jnp
from jax import lax
from jax.experimental import pallas as pl
from jax.experimental.pallas import tpu as pltpu
from jax.sharding import PartitionSpec as P

LATENT = 512
F32 = jnp.float32
BF16 = jnp.bfloat16
VMEM = pltpu.VMEM
MIB = 1024 * 1024


softmax_scale = 192.0 ** (-0.5)


def attend_rows(lengths_ref, queries_ref, cache_ref, out_ref):
    for r in range(queries_ref.shape[0]):
        queries = queries_ref[r].T
        cache = cache_ref[r]
        scores = jnp.dot(queries, cache, preferred_element_type=F32) * softmax_scale
        usable = lax.broadcasted_iota(jnp.int32, scores.shape, 1) < lengths_ref[r]
        scores = jnp.where(usable, scores, -1e30)
        weights = jnp.exp(scores - jnp.max(scores, axis=1, keepdims=True))
        weights = weights / jnp.sum(weights, axis=1, keepdims=True)
        out_ref[r] = lax.dot_general(
            weights.astype(BF16),
            cache[:LATENT],
            (((1,), (1,)), ((), ())),
            preferred_element_type=F32,
        ).astype(BF16)


def attend_cost(queries, latent_cache):
    rows, heads, width = queries.shape
    positions = latent_cache.shape[1]
    return pl.CostEstimate(
        flops=2 * rows * heads * positions * (width + LATENT),
        bytes_accessed=2 * rows * (positions * width + heads * (width + LATENT)),
        transcendentals=rows * heads * positions,
    )


def in_hbm(array):
    return pltpu.with_memory_space_constraint(array, pltpu.HBM)


def in_vmem(array):
    return pltpu.with_memory_space_constraint(array, VMEM)


def whole(space=VMEM):
    return pl.BlockSpec(memory_space=space)


def attend(queries, latent_cache, cache_lengths):
    rows, heads, _ = queries.shape
    return pl.pallas_call(
        attend_rows,
        in_specs=[whole(pltpu.SMEM), whole(), whole()],
        out_specs=whole(),
        out_shape=jax.ShapeDtypeStruct((rows, heads, LATENT), BF16),
        compiler_params=pltpu.CompilerParams(vmem_limit_bytes=16 * MIB),
        cost_estimate=attend_cost(queries, latent_cache),
    )(cache_lengths, jnp.swapaxes(queries, 1, 2), jnp.swapaxes(latent_cache, 1, 2))


def attend_after_kernel(lengths_ref, queries_ref, cache_ref, after_ref, out_ref):
    attend_rows(lengths_ref, queries_ref, cache_ref, out_ref)


def attend_after(queries, latent_cache, cache_lengths, after):
    rows, heads, _ = queries.shape
    return pl.pallas_call(
        attend_after_kernel,
        in_specs=[whole(pltpu.SMEM), whole(), whole(), whole(pl.ANY)],
        out_specs=whole(),
        out_shape=jax.ShapeDtypeStruct((rows, heads, LATENT), BF16),
        compiler_params=pltpu.CompilerParams(vmem_limit_bytes=8 * MIB),
        cost_estimate=pl.CostEstimate(
            flops=4 * 10**9, bytes_accessed=0, transcendentals=0
        ),
    )(
        cache_lengths,
        jnp.swapaxes(queries, 1, 2),
        jnp.swapaxes(latent_cache, 1, 2),
        after,
    )


def once_done(value, other, flops=0):
    return pl.pallas_call(
        lambda *refs: None,
        in_specs=[whole(pl.ANY)] * 2,
        out_specs=whole(pl.ANY),
        out_shape=VMEM(value.shape, value.dtype),
        input_output_aliases={0: 0},
        compiler_params=pltpu.CompilerParams(vmem_limit_bytes=MIB),
        cost_estimate=pl.CostEstimate(flops=flops, bytes_accessed=0, transcendentals=0),
    )(value, other)


def gate_table(expert_ids, gate_values, experts_all):
    chosen = expert_ids[:, :, None] == jnp.arange(experts_all, dtype=jnp.int32)[None, None, :]
    return jnp.sum(jnp.where(chosen, gate_values[:, :, None], 0.0), axis=1)


def pack_kernel(experts_all, rows_in, ids_in, gates_in, out_ref, ids_ref, gates_ref, sems):
    rows, feature_count = rows_in.shape
    copies = [
        pltpu.make_async_copy(ids_in, ids_ref, sems.at[0]),
        pltpu.make_async_copy(gates_in, gates_ref, sems.at[1]),
        pltpu.make_async_copy(rows_in, out_ref.at[:, :feature_count], sems.at[2]),
    ]
    for copy in copies:
        copy.start()
    copies[0].wait()
    copies[1].wait()
    lane = lax.broadcasted_iota(jnp.int32, (rows, out_ref.shape[1] - feature_count), 1)
    expert = lax.rem(lane, experts_all)
    table = jnp.zeros(lane.shape, F32)
    for k in range(ids_ref.shape[1]):
        table += jnp.where(ids_ref[:, k : k + 1] == expert, gates_ref[:, k : k + 1], 0.0)
    high = table.astype(BF16).astype(F32)
    middle = (table - high).astype(BF16).astype(F32)
    low = table - high - middle
    coded = jnp.where(
        lane < experts_all,
        high,
        jnp.where(
            lane < 2 * experts_all, middle, jnp.where(lane < 3 * experts_all, low, 0.0)
        ),
    )
    out_ref[:, feature_count:] = coded.astype(BF16)
    copies[2].wait()


def pack(hidden_rows, expert_ids, gate_values, experts_all):
    rows, feature_count = hidden_rows.shape
    return pl.pallas_call(
        lambda *refs: pack_kernel(experts_all, *refs),
        in_specs=[whole(pltpu.HBM)] * 3,
        out_specs=whole(),
        out_shape=VMEM((rows, feature_count + 128), BF16),
        scratch_shapes=[
            VMEM(expert_ids.shape, jnp.int32),
            VMEM(gate_values.shape, F32),
            pltpu.SemaphoreType.DMA((3,)),
        ],
        compiler_params=pltpu.CompilerParams(vmem_limit_bytes=2 * MIB),
        cost_estimate=pl.CostEstimate(
            flops=0, bytes_accessed=4 * rows * feature_count, transcendentals=0
        ),
    )(in_hbm(hidden_rows), in_hbm(expert_ids), in_hbm(gate_values))


def activated(rows, gate_ref, up_ref):
    gate = jnp.dot(rows, gate_ref[...], preferred_element_type=F32)
    up = jnp.dot(rows, up_ref[...], preferred_element_type=F32)
    return (gate / (1.0 + jnp.exp(-gate)) * up).astype(BF16)


def compacted(made, rank_row, slots):
    slot = lax.broadcasted_iota(jnp.int32, (slots, rank_row.shape[1]), 0).astype(F32)
    to_slot = (rank_row == slot).astype(F32).astype(BF16)
    return jnp.dot(to_slot, made, preferred_element_type=F32).astype(BF16)


def gate_up_first_kernel(experts_all, *refs):
    groups = refs[:4]
    gate_ref, up_ref, hidden_ref, table_ref, rank_ref, across_ref = refs[4:]
    experts, depth, _ = gate_ref.shape
    rows_group, total_width = groups[0].shape
    count = 4 * rows_group
    lanes = total_width - depth
    rows = jnp.concatenate([ref[:, :depth] for ref in groups], axis=0)
    coded = jnp.concatenate([ref[:, depth:] for ref in groups], axis=0)
    made = activated(rows, gate_ref.at[0], up_ref.at[0])
    source = lax.broadcasted_iota(jnp.int32, (lanes, lanes), 0)
    target = lax.broadcasted_iota(jnp.int32, (lanes, lanes), 1)
    selector = (
        (lax.rem(source, experts_all) == lax.axis_index("expert") * experts + target)
        & (target < experts)
        & (source < 3 * experts_all)
    )
    table = jnp.dot(coded, selector.astype(F32).astype(BF16), preferred_element_type=F32)
    chosen = (table > 0.0).astype(F32).astype(BF16)
    row = lax.broadcasted_iota(jnp.int32, (count, count), 0)
    column = lax.broadcasted_iota(jnp.int32, (count, count), 1)
    turn = lax.axis_index("dp") * rows_group
    ahead = jnp.bitwise_xor(column, turn) < jnp.bitwise_xor(row, turn)
    rank = jnp.dot(ahead.astype(F32).astype(BF16), chosen, preferred_element_type=F32)
    rank = jnp.where(table > 0.0, rank, -1.0)
    across = rank.T
    table_ref[...], rank_ref[...], across_ref[...] = table, rank, across
    part, slots, _ = hidden_ref.shape
    for e in range(part):
        later = activated(rows, gate_ref.at[e + 1], up_ref.at[e + 1]) if e + 1 < part else None
        hidden_ref[e] = compacted(made, across[e : e + 1], slots)
        made = later


def gate_up_next_kernel(*refs):
    groups = refs[:4]
    gate_ref, up_ref, first_ref, table_ref, rank_ref, across_ref = refs[4:10]
    hidden_ref, all_ref, spread_ref = refs[10:]
    experts, depth, _ = gate_ref.shape
    rows = jnp.concatenate([ref[:, :depth] for ref in groups], axis=0)
    count = rows.shape[0]
    done, slots, _ = first_ref.shape
    made = activated(rows, gate_ref.at[done], up_ref.at[done])
    all_ref[:done] = first_ref[...]
    slot = lax.broadcasted_iota(jnp.int32, (count, count), 1).astype(F32)
    table, rank = table_ref[...], rank_ref[...]
    for e in range(experts):
        value = jnp.where(rank[:, e : e + 1] == slot, table[:, e : e + 1], 0.0)
        high = value.astype(BF16)
        spread_ref[:count, e * count : (e + 1) * count] = high
        spread_ref[count:, e * count : (e + 1) * count] = (value - high.astype(F32)).astype(BF16)
    for e in range(done, experts):
        later = (
            activated(rows, gate_ref.at[e + 1], up_ref.at[e + 1]) if e + 1 < experts else None
        )
        hidden = compacted(made, across_ref[e : e + 1], slots)
        hidden_ref[e - done] = hidden
        all_ref[e] = hidden
        made = later


def half_cost(gate_proj, count):
    size = gate_proj.size // 2
    return pl.CostEstimate(flops=4 * count * size, bytes_accessed=4 * size, transcendentals=0)


def gate_up_first(pieces, gate_proj, up_proj, part, slots, experts_all):
    _, depth, share = gate_proj.shape
    rows_group, total_width = pieces[0].shape
    count = 4 * rows_group
    square = VMEM((count, total_width - depth), F32)
    return pl.pallas_call(
        lambda *refs: gate_up_first_kernel(experts_all, *refs),
        in_specs=[whole()] * 6,
        out_specs=[whole()] * 4,
        out_shape=[
            VMEM((part, slots, share), BF16),
            square,
            square,
            VMEM((total_width - depth, count), F32),
        ],
        compiler_params=pltpu.CompilerParams(vmem_limit_bytes=28 * MIB),
        cost_estimate=half_cost(gate_proj, count),
    )(*pieces, gate_proj, up_proj)


def gate_up_next(pieces, gate_proj, up_proj, first, table, rank, across):
    experts, depth, share = gate_proj.shape
    done, slots, _ = first.shape
    count = 4 * pieces[0].shape[0]
    return pl.pallas_call(
        gate_up_next_kernel,
        in_specs=[whole()] * 10,
        out_specs=[whole()] * 3,
        out_shape=[
            VMEM((experts - done, slots, share), BF16),
            VMEM((experts, slots, share), BF16),
            VMEM((2 * count, experts * count), BF16),
        ],
        compiler_params=pltpu.CompilerParams(vmem_limit_bytes=28 * MIB),
        cost_estimate=half_cost(gate_proj, count),
    )(*pieces, gate_proj, up_proj, first, table, rank, across)


def down_part_kernel(start, h0_ref, h1_ref, h2_ref, down_ref, made_ref):
    place = lax.axis_index("dp")
    share = h0_ref.shape[2]
    for e in range(h2_ref.shape[0]):
        made = jnp.zeros(made_ref.shape[1:], F32)
        for k, ref in enumerate((h0_ref.at[start + e], h1_ref.at[start + e], h2_ref.at[e])):
            owner = jnp.bitwise_xor(place, k)
            weights = down_ref[start + e, pl.ds(pl.multiple_of(owner * share, share), share)]
            made += jnp.dot(ref[...], weights, preferred_element_type=F32)
        made_ref[e] = made


def down_part(start, hidden, down_proj):
    part, slots, share = hidden[2].shape
    width = down_proj.shape[2]
    return pl.pallas_call(
        lambda *refs: down_part_kernel(start, *refs),
        in_specs=[whole()] * 4,
        out_specs=whole(),
        out_shape=VMEM((part, slots, width), F32),
        compiler_params=pltpu.CompilerParams(vmem_limit_bytes=20 * MIB),
        cost_estimate=pl.CostEstimate(
            flops=6 * part * slots * share * width,
            bytes_accessed=4 * part * slots * width,
            transcendentals=0,
        ),
    )(*hidden, down_proj)


def down_last_kernel(
    spread_ref,
    begun_first_ref,
    begun_next_ref,
    h3_first_ref,
    h3_next_ref,
    down_ref,
    o0_ref,
    o1_ref,
    o2_ref,
    o3_ref,
    made_ref,
):
    owner = jnp.bitwise_xor(lax.axis_index("dp"), 3)
    part, slots, share = h3_first_ref.shape
    experts, _, width = down_ref.shape
    count = spread_ref.shape[0] // 2
    rows_z = o0_ref.shape[0]
    tile = 256
    for e in range(experts):
        if slots < count:
            made_ref[e * count + slots : (e + 1) * count] = jnp.zeros(
                (count - slots, width), BF16
            )
        weights = down_ref[e, pl.ds(pl.multiple_of(owner * share, share), share)]
        if e < part:
            begun, far = begun_first_ref[e], h3_first_ref[e]
        else:
            begun, far = begun_next_ref[e - part], h3_next_ref[e - part]
        made = begun + jnp.dot(far, weights, preferred_element_type=F32)
        made_ref[e * count : e * count + slots] = made.astype(BF16)
    spread = spread_ref[...]
    for start in range(0, width, tile):
        both = jnp.dot(spread, made_ref[:, start : start + tile], preferred_element_type=F32)
        done = both[:count] + both[count:]
        rows = rows_z // 4
        for k, ref in enumerate((o0_ref, o1_ref, o2_ref, o3_ref)):
            parts = [
                done[g * rows_z + k * rows : g * rows_z + (k + 1) * rows] for g in range(4)
            ]
            ref[:, start : start + tile] = jnp.concatenate(parts, axis=0).astype(BF16)


def down_last(spread, begun, hidden, down_proj):
    experts, _, width = down_proj.shape
    slots = hidden[0].shape[1]
    count = spread.shape[0] // 2
    return pl.pallas_call(
        down_last_kernel,
        in_specs=[whole()] * 6,
        out_specs=[whole()] * 4,
        out_shape=[VMEM((count // 4, width), BF16)] * 4,
        scratch_shapes=[VMEM((experts * count, width), BF16)],
        compiler_params=pltpu.CompilerParams(vmem_limit_bytes=20 * MIB),
        cost_estimate=pl.CostEstimate(
            flops=4 * experts * count * count * width,
            bytes_accessed=8 * experts * slots * width,
            transcendentals=0,
        ),
    )(spread, *begun, *hidden, down_proj)


def collect_kernel(p0_ref, p1_ref, p2_ref, p3_ref, own_ref, core_ref, x_ref, far_ref):
    total = p0_ref[...].astype(F32)
    for ref in (p1_ref, p2_ref, p3_ref):
        total += ref[...].astype(F32)
    rows = own_ref.shape[0]
    for k, ref in enumerate((own_ref, core_ref, x_ref, far_ref)):
        ref[...] = total[k * rows : (k + 1) * rows].astype(BF16)


def collect(partials):
    rows, width = partials[0].shape
    return pl.pallas_call(
        collect_kernel,
        in_specs=[whole()] * 4,
        out_specs=[whole()] * 4,
        out_shape=[VMEM((rows // 4, width), BF16)] * 4,
        compiler_params=pltpu.CompilerParams(vmem_limit_bytes=2 * MIB),
        cost_estimate=pl.CostEstimate(
            flops=4 * rows * width, bytes_accessed=8 * rows * width, transcendentals=0
        ),
    )(*partials)


def place_kernel(p0_ref, p1_ref, p2_ref, p3_ref, out_ref):
    place = lax.axis_index("dp")
    width = p0_ref.shape[1]
    for k, ref in enumerate((p0_ref, p1_ref, p2_ref, p3_ref)):
        at = pl.multiple_of(jnp.bitwise_xor(place, k) * width, width)
        out_ref[:, pl.ds(at, width)] = ref[...]


def place_all(pieces):
    rows, width = pieces[0].shape
    return pl.pallas_call(
        place_kernel,
        in_specs=[whole()] * 4,
        out_specs=whole(),
        out_shape=jax.ShapeDtypeStruct((rows, 4 * width), BF16),
        compiler_params=pltpu.CompilerParams(vmem_limit_bytes=2 * MIB),
        cost_estimate=pl.CostEstimate(
            flops=0, bytes_accessed=16 * rows * width, transcendentals=0
        ),
    )(*pieces)


def swap(value, axis, bit):
    size = lax.axis_size(axis)
    return lax.ppermute(value, axis, [(i, i ^ bit) for i in range(size)])


def routed_four(
    hidden_rows,
    expert_ids,
    gate_values,
    gate_proj,
    up_proj,
    down_proj,
    queries,
    latent_cache,
    cache_lengths,
):
    rows_dev, feature_count = hidden_rows.shape
    local_experts = gate_proj.shape[0]
    width = down_proj.shape[2]
    experts_all = local_experts * 4
    capacity = max(2, 3 * rows_dev * expert_ids.shape[1] // (2 * experts_all))
    sent = pack(hidden_rows, expert_ids, gate_values, experts_all)
    along_z = [sent] + [swap(sent, "expert", k) for k in (2, 1, 3)]
    along_z[1:] = [once_done(block, sent, 4 * 10**9) for block in along_z[1:]]
    along_x = [swap(block, "dp", 2) for block in along_z]
    mine_z, mine_x = jnp.stack(along_z), jnp.stack(along_x)
    other_z = swap(mine_z, "dp", 1)
    early = swap(jnp.stack([along_x[0], along_x[2], along_x[3]]), "dp", 1)
    late = swap(along_x[1], "dp", 1)
    other_x = jnp.stack([early[0], late, early[1], early[2]])

    pieces = [block.reshape(4 * rows_dev, -1) for block in (mine_z, other_z, mine_x, other_x)]
    half = local_experts // 2
    hidden_first, table, rank, across = gate_up_first(
        pieces, gate_proj, up_proj, half, 16 * capacity, experts_all
    )
    first_x = swap(hidden_first, "dp", 2)
    hidden_next, hidden, spread = gate_up_next(
        pieces, gate_proj, up_proj, hidden_first, table, rank, across
    )
    next_x = swap(hidden_next, "dp", 2)
    hidden_c = swap(hidden, "dp", 1)
    attended = attend_after(queries, latent_cache, cache_lengths, hidden_next)
    first_x = once_done(first_x, in_hbm(attended))
    first_far = swap(first_x, "dp", 1)
    begun_first = down_part(0, (hidden, hidden_c, first_x), down_proj)
    next_x = once_done(next_x, begun_first)
    next_far = swap(next_x, "dp", 1)
    begun_next = down_part(half, (hidden, hidden_c, next_x), down_proj)
    partial = down_last(spread, (begun_first, begun_next), (first_far, next_far), down_proj)
    arrived = [partial[0]] + [swap(partial[j], "expert", k) for j, k in ((3, 3), (2, 1), (1, 2))]
    own, to_core, to_x, to_far = collect(arrived)
    far = swap(to_far, "dp", 3)
    blended = place_all((own, swap(to_core, "dp", 1), swap(to_x, "dp", 2), far))
    return blended, attended


def routed_any(hidden_rows, expert_ids, gate_values, gate_proj, up_proj, down_proj):
    rows_dev, feature_count = hidden_rows.shape
    local_experts = gate_proj.shape[0]
    width = down_proj.shape[2]
    owners = lax.axis_size("expert")
    members = lax.axis_size("dp")
    experts_all = local_experts * owners
    table = gate_table(expert_ids, gate_values, experts_all)
    rows = lax.all_gather(hidden_rows, ("expert", "dp"), axis=0, tiled=True)
    table = lax.all_gather(table, ("expert", "dp"), axis=0, tiled=True)
    table = lax.dynamic_slice_in_dim(
        table, lax.axis_index("expert") * local_experts, local_experts, axis=1
    )
    total = jnp.zeros((rows.shape[0], width), F32)
    for e in range(local_experts):
        gate = jnp.dot(rows, gate_proj[e], preferred_element_type=F32)
        up = jnp.dot(rows, up_proj[e], preferred_element_type=F32)
        share = (jax.nn.silu(gate) * up).astype(BF16)
        hidden = lax.all_gather(share, "dp", axis=1, tiled=True)
        made = jnp.dot(hidden, down_proj[e], preferred_element_type=F32).astype(BF16)
        total += table[:, e : e + 1] * made.astype(F32)
    partial = total.astype(BF16).reshape(owners, members, rows_dev, width)
    returned = lax.all_to_all(
        lax.all_to_all(partial, "expert", split_axis=0, concat_axis=0, tiled=True),
        "dp",
        split_axis=1,
        concat_axis=1,
        tiled=True,
    )
    blended = jnp.sum(returned.astype(F32), axis=0).astype(BF16)
    return jnp.transpose(blended, (1, 0, 2)).reshape(rows_dev, members * width)


def local(
    hidden_rows,
    expert_ids,
    gate_values,
    gate_proj,
    up_proj,
    down_proj,
    queries,
    latent_cache,
    cache_lengths,
):
    routing = (hidden_rows, expert_ids, gate_values, gate_proj, up_proj, down_proj)
    attention = (queries, latent_cache, cache_lengths)
    four = lax.axis_size("expert") == 4 and lax.axis_size("dp") == 4
    if four and hidden_rows.shape[0] == 8 and 12 * gate_proj.shape[0] <= 128:
        return routed_four(*routing, *attention)
    return routed_any(*routing), attend(*attention)


def solution(mesh):
    return jax.shard_map(
        local,
        mesh=mesh,
        in_specs=(
            P(("groups", "expert", "dp"), None),
            P(("groups", "expert", "dp"), None),
            P(("groups", "expert", "dp"), None),
            P("expert", None, "dp"),
            P("expert", None, "dp"),
            P("expert", None, "dp"),
            P(("groups", "expert", "dp"), None, None),
            P(("groups", "expert", "dp"), None, None),
            P(("groups", "expert", "dp")),
        ),
        out_specs=(P(("groups", "expert", "dp"), None), P(("groups", "expert", "dp"), None, None)),
        check_vma=False,
    )
```

```python
import jax
import jax.numpy as jnp
from jax import lax
from jax.experimental import pallas as pl
from jax.experimental.pallas import tpu as pltpu
from jax.sharding import PartitionSpec as P

LATENT = 512
F32 = jnp.float32
BF16 = jnp.bfloat16
VMEM = pltpu.VMEM
MIB = 1024 * 1024


softmax_scale = 192.0 ** (-0.5)


def attend_rows(lengths_ref, queries_ref, cache_ref, out_ref):
    for r in range(queries_ref.shape[0]):
        queries = queries_ref[r].T
        cache = cache_ref[r]
        scores = jnp.dot(queries, cache, preferred_element_type=F32) * softmax_scale
        usable = lax.broadcasted_iota(jnp.int32, scores.shape, 1) < lengths_ref[r]
        scores = jnp.where(usable, scores, -1e30)
        weights = jnp.exp(scores - jnp.max(scores, axis=1, keepdims=True))
        weights = weights / jnp.sum(weights, axis=1, keepdims=True)
        out_ref[r] = lax.dot_general(
            weights.astype(BF16),
            cache[:LATENT],
            (((1,), (1,)), ((), ())),
            preferred_element_type=F32,
        ).astype(BF16)


def attend_cost(queries, latent_cache):
    rows, heads, width = queries.shape
    positions = latent_cache.shape[1]
    return pl.CostEstimate(
        flops=2 * rows * heads * positions * (width + LATENT),
        bytes_accessed=2 * rows * (positions * width + heads * (width + LATENT)),
        transcendentals=rows * heads * positions,
    )


def in_hbm(array):
    return pltpu.with_memory_space_constraint(array, pltpu.HBM)


def in_vmem(array):
    return pltpu.with_memory_space_constraint(array, VMEM)


def whole(space=VMEM):
    return pl.BlockSpec(memory_space=space)


def attend(queries, latent_cache, cache_lengths):
    rows, heads, _ = queries.shape
    return pl.pallas_call(
        attend_rows,
        in_specs=[whole(pltpu.SMEM), whole(), whole()],
        out_specs=whole(),
        out_shape=jax.ShapeDtypeStruct((rows, heads, LATENT), BF16),
        compiler_params=pltpu.CompilerParams(vmem_limit_bytes=16 * MIB),
        cost_estimate=attend_cost(queries, latent_cache),
    )(cache_lengths, jnp.swapaxes(queries, 1, 2), jnp.swapaxes(latent_cache, 1, 2))


def attend_after_kernel(lengths_ref, queries_ref, cache_ref, after_ref, out_ref):
    attend_rows(lengths_ref, queries_ref, cache_ref, out_ref)


def attend_after(queries, latent_cache, cache_lengths, after):
    rows, heads, _ = queries.shape
    return pl.pallas_call(
        attend_after_kernel,
        in_specs=[whole(pltpu.SMEM), whole(), whole(), whole(pl.ANY)],
        out_specs=whole(),
        out_shape=jax.ShapeDtypeStruct((rows, heads, LATENT), BF16),
        compiler_params=pltpu.CompilerParams(vmem_limit_bytes=8 * MIB),
        cost_estimate=pl.CostEstimate(
            flops=4 * 10**9, bytes_accessed=0, transcendentals=0
        ),
    )(
        cache_lengths,
        jnp.swapaxes(queries, 1, 2),
        jnp.swapaxes(latent_cache, 1, 2),
        after,
    )


def once_done(value, other, flops=0):
    return pl.pallas_call(
        lambda *refs: None,
        in_specs=[whole(pl.ANY)] * 2,
        out_specs=whole(pl.ANY),
        out_shape=VMEM(value.shape, value.dtype),
        input_output_aliases={0: 0},
        compiler_params=pltpu.CompilerParams(vmem_limit_bytes=MIB),
        cost_estimate=pl.CostEstimate(flops=flops, bytes_accessed=0, transcendentals=0),
    )(value, other)


def gate_table(expert_ids, gate_values, experts_all):
    chosen = expert_ids[:, :, None] == jnp.arange(experts_all, dtype=jnp.int32)[None, None, :]
    return jnp.sum(jnp.where(chosen, gate_values[:, :, None], 0.0), axis=1)


def pack_kernel(experts_all, rows_in, ids_in, gates_in, out_ref, ids_ref, gates_ref, sems):
    rows, feature_count = rows_in.shape
    copies = [
        pltpu.make_async_copy(ids_in, ids_ref, sems.at[0]),
        pltpu.make_async_copy(gates_in, gates_ref, sems.at[1]),
        pltpu.make_async_copy(rows_in, out_ref.at[:, :feature_count], sems.at[2]),
    ]
    for copy in (copies[2], copies[0], copies[1]):
        copy.start()
    copies[0].wait()
    copies[1].wait()
    lane = lax.broadcasted_iota(jnp.int32, (rows, out_ref.shape[1] - feature_count), 1)
    expert = lax.rem(lane, experts_all)
    table = jnp.zeros(lane.shape, F32)
    for k in range(ids_ref.shape[1]):
        table += jnp.where(ids_ref[:, k : k + 1] == expert, gates_ref[:, k : k + 1], 0.0)
    high = table.astype(BF16).astype(F32)
    middle = (table - high).astype(BF16).astype(F32)
    low = table - high - middle
    coded = jnp.where(
        lane < experts_all,
        high,
        jnp.where(
            lane < 2 * experts_all, middle, jnp.where(lane < 3 * experts_all, low, 0.0)
        ),
    )
    out_ref[:, feature_count:] = coded.astype(BF16)
    copies[2].wait()


def pack(hidden_rows, expert_ids, gate_values, experts_all):
    rows, feature_count = hidden_rows.shape
    return pl.pallas_call(
        lambda *refs: pack_kernel(experts_all, *refs),
        in_specs=[whole(pltpu.HBM)] * 3,
        out_specs=whole(),
        out_shape=VMEM((rows, feature_count + 128), BF16),
        scratch_shapes=[
            VMEM(expert_ids.shape, jnp.int32),
            VMEM(gate_values.shape, F32),
            pltpu.SemaphoreType.DMA((3,)),
        ],
        compiler_params=pltpu.CompilerParams(vmem_limit_bytes=2 * MIB),
        cost_estimate=pl.CostEstimate(
            flops=0, bytes_accessed=4 * rows * feature_count, transcendentals=0
        ),
    )(in_hbm(hidden_rows), in_hbm(expert_ids), in_hbm(gate_values))


def activated(rows, gate_ref, up_ref):
    gate = jnp.dot(rows, gate_ref[...], preferred_element_type=F32)
    up = jnp.dot(rows, up_ref[...], preferred_element_type=F32)
    return (gate / (1.0 + jnp.exp(-gate)) * up).astype(BF16)


def compacted(made, rank_row, slots):
    slot = lax.broadcasted_iota(jnp.int32, (slots, rank_row.shape[1]), 0).astype(F32)
    to_slot = (rank_row == slot).astype(F32).astype(BF16)
    return jnp.dot(to_slot, made, preferred_element_type=F32).astype(BF16)


def gate_up_first_kernel(experts_all, *refs):
    groups = refs[:4]
    gate_ref, up_ref, hidden_ref, table_ref, rank_ref, across_ref = refs[4:]
    experts, depth, _ = gate_ref.shape
    rows_group, total_width = groups[0].shape
    count = 4 * rows_group
    lanes = total_width - depth
    rows = jnp.concatenate([ref[:, :depth] for ref in groups], axis=0)
    coded = jnp.concatenate([ref[:, depth:] for ref in groups], axis=0)
    made = activated(rows, gate_ref.at[0], up_ref.at[0])
    source = lax.broadcasted_iota(jnp.int32, (lanes, lanes), 0)
    target = lax.broadcasted_iota(jnp.int32, (lanes, lanes), 1)
    selector = (
        (lax.rem(source, experts_all) == lax.axis_index("expert") * experts + target)
        & (target < experts)
        & (source < 3 * experts_all)
    )
    table = jnp.dot(coded, selector.astype(F32).astype(BF16), preferred_element_type=F32)
    chosen = (table > 0.0).astype(F32).astype(BF16)
    row = lax.broadcasted_iota(jnp.int32, (count, count), 0)
    column = lax.broadcasted_iota(jnp.int32, (count, count), 1)
    turn = lax.axis_index("dp") * rows_group
    ahead = jnp.bitwise_xor(column, turn) < jnp.bitwise_xor(row, turn)
    rank = jnp.dot(ahead.astype(F32).astype(BF16), chosen, preferred_element_type=F32)
    rank = jnp.where(table > 0.0, rank, -1.0)
    across = rank.T
    table_ref[...], rank_ref[...], across_ref[...] = table, rank, across
    part, slots, _ = hidden_ref.shape
    for e in range(part):
        later = activated(rows, gate_ref.at[e + 1], up_ref.at[e + 1]) if e + 1 < part else None
        hidden_ref[e] = compacted(made, across[e : e + 1], slots)
        made = later


def gate_up_next_kernel(*refs):
    groups = refs[:4]
    gate_ref, up_ref, first_ref, table_ref, rank_ref, across_ref = refs[4:10]
    hidden_ref, all_ref, spread_ref = refs[10:]
    experts, depth, _ = gate_ref.shape
    rows = jnp.concatenate([ref[:, :depth] for ref in groups], axis=0)
    count = rows.shape[0]
    done, slots, _ = first_ref.shape
    made = activated(rows, gate_ref.at[done], up_ref.at[done])
    all_ref[:done] = first_ref[...]
    slot = lax.broadcasted_iota(jnp.int32, (count, count), 1).astype(F32)
    table, rank = table_ref[...], rank_ref[...]
    for e in range(experts):
        value = jnp.where(rank[:, e : e + 1] == slot, table[:, e : e + 1], 0.0)
        high = value.astype(BF16)
        spread_ref[:count, e * count : (e + 1) * count] = high
        spread_ref[count:, e * count : (e + 1) * count] = (value - high.astype(F32)).astype(BF16)
    for e in range(done, experts):
        later = (
            activated(rows, gate_ref.at[e + 1], up_ref.at[e + 1]) if e + 1 < experts else None
        )
        hidden = compacted(made, across_ref[e : e + 1], slots)
        hidden_ref[e - done] = hidden
        all_ref[e] = hidden
        made = later


def half_cost(gate_proj, count):
    size = gate_proj.size // 2
    return pl.CostEstimate(flops=4 * count * size, bytes_accessed=4 * size, transcendentals=0)


def gate_up_first(pieces, gate_proj, up_proj, part, slots, experts_all):
    _, depth, share = gate_proj.shape
    rows_group, total_width = pieces[0].shape
    count = 4 * rows_group
    square = VMEM((count, total_width - depth), F32)
    return pl.pallas_call(
        lambda *refs: gate_up_first_kernel(experts_all, *refs),
        in_specs=[whole()] * 6,
        out_specs=[whole()] * 4,
        out_shape=[
            VMEM((part, slots, share), BF16),
            square,
            square,
            VMEM((total_width - depth, count), F32),
        ],
        compiler_params=pltpu.CompilerParams(vmem_limit_bytes=28 * MIB),
        cost_estimate=half_cost(gate_proj, count),
    )(*pieces, gate_proj, up_proj)


def gate_up_next(pieces, gate_proj, up_proj, first, table, rank, across):
    experts, depth, share = gate_proj.shape
    done, slots, _ = first.shape
    count = 4 * pieces[0].shape[0]
    return pl.pallas_call(
        gate_up_next_kernel,
        in_specs=[whole()] * 10,
        out_specs=[whole()] * 3,
        out_shape=[
            VMEM((experts - done, slots, share), BF16),
            VMEM((experts, slots, share), BF16),
            VMEM((2 * count, experts * count), BF16),
        ],
        compiler_params=pltpu.CompilerParams(vmem_limit_bytes=28 * MIB),
        cost_estimate=half_cost(gate_proj, count),
    )(*pieces, gate_proj, up_proj, first, table, rank, across)


def down_part_kernel(start, h0_ref, h1_ref, h2_ref, down_ref, made_ref):
    place = lax.axis_index("dp")
    share = h0_ref.shape[2]
    for e in range(h2_ref.shape[0]):
        made = jnp.zeros(made_ref.shape[1:], F32)
        for k, ref in enumerate((h0_ref.at[start + e], h1_ref.at[start + e], h2_ref.at[e])):
            owner = jnp.bitwise_xor(place, k)
            weights = down_ref[start + e, pl.ds(pl.multiple_of(owner * share, share), share)]
            made += jnp.dot(ref[...], weights, preferred_element_type=F32)
        made_ref[e] = made


def down_part(start, hidden, down_proj):
    part, slots, share = hidden[2].shape
    width = down_proj.shape[2]
    return pl.pallas_call(
        lambda *refs: down_part_kernel(start, *refs),
        in_specs=[whole()] * 4,
        out_specs=whole(),
        out_shape=VMEM((part, slots, width), F32),
        compiler_params=pltpu.CompilerParams(vmem_limit_bytes=20 * MIB),
        cost_estimate=pl.CostEstimate(
            flops=6 * part * slots * share * width,
            bytes_accessed=4 * part * slots * width,
            transcendentals=0,
        ),
    )(*hidden, down_proj)


def finish(e, begun, far, down_ref, made_ref, at, count):
    owner = jnp.bitwise_xor(lax.axis_index("dp"), 3)
    slots, share = far.shape
    weights = down_ref[e, pl.ds(pl.multiple_of(owner * share, share), share)]
    made = begun + jnp.dot(far, weights, preferred_element_type=F32)
    made_ref[at : at + slots] = made.astype(BF16)
    if slots < count:
        made_ref[at + slots : at + count] = jnp.zeros((count - slots, made.shape[1]), BF16)


def down_middle_kernel(
    start,
    h2_ref,
    h0_ref,
    h1_ref,
    begun_first_ref,
    h3_first_ref,
    spread_ref,
    down_ref,
    begun_ref,
    mixed_ref,
    made_ref,
):
    count = mixed_ref.shape[0]
    for e in range(start):
        finish(e, begun_first_ref[e], h3_first_ref[e], down_ref, made_ref, e * count, count)
    down_part_kernel(start, h0_ref, h1_ref, h2_ref, down_ref, begun_ref)
    both = jnp.dot(
        spread_ref[:, : start * count], made_ref[...], preferred_element_type=F32
    )
    mixed_ref[...] = both[:count] + both[count:]


def down_middle(start, hidden, begun_first, far_first, spread, down_proj):
    part, slots, share = hidden[0].shape
    width = down_proj.shape[2]
    count = spread.shape[0] // 2
    return pl.pallas_call(
        lambda *refs: down_middle_kernel(start, *refs),
        in_specs=[whole()] * 7,
        out_specs=[whole()] * 2,
        out_shape=[VMEM((part, slots, width), F32), VMEM((count, width), F32)],
        scratch_shapes=[VMEM((start * count, width), BF16)],
        compiler_params=pltpu.CompilerParams(vmem_limit_bytes=20 * MIB),
        cost_estimate=pl.CostEstimate(
            flops=6 * part * slots * share * width,
            bytes_accessed=4 * part * slots * width,
            transcendentals=0,
        ),
    )(*hidden, begun_first, far_first, spread, down_proj)


def down_last_kernel(
    start,
    spread_ref,
    mixed_ref,
    begun_ref,
    h3_ref,
    down_ref,
    o0_ref,
    o1_ref,
    o2_ref,
    o3_ref,
    made_ref,
):
    count, width = mixed_ref.shape
    rows_z = o0_ref.shape[0]
    rows = rows_z // 4
    tile = 256
    for e in range(begun_ref.shape[0]):
        finish(start + e, begun_ref[e], h3_ref[e], down_ref, made_ref, e * count, count)
    spread = spread_ref[:, start * count :]
    for at in range(0, width, tile):
        both = jnp.dot(spread, made_ref[:, at : at + tile], preferred_element_type=F32)
        done = mixed_ref[:, at : at + tile] + both[:count] + both[count:]
        for k, ref in enumerate((o0_ref, o1_ref, o2_ref, o3_ref)):
            parts = [
                done[g * rows_z + k * rows : g * rows_z + (k + 1) * rows] for g in range(4)
            ]
            ref[:, at : at + tile] = jnp.concatenate(parts, axis=0).astype(BF16)


def down_last(start, spread, mixed, begun, far, down_proj):
    part, slots, share = far.shape
    count, width = mixed.shape
    return pl.pallas_call(
        lambda *refs: down_last_kernel(start, *refs),
        in_specs=[whole()] * 5,
        out_specs=[whole()] * 4,
        out_shape=[VMEM((count // 4, width), BF16)] * 4,
        scratch_shapes=[VMEM((part * count, width), BF16)],
        compiler_params=pltpu.CompilerParams(vmem_limit_bytes=20 * MIB),
        cost_estimate=pl.CostEstimate(
            flops=4 * part * count * count * width,
            bytes_accessed=8 * part * slots * width,
            transcendentals=0,
        ),
    )(spread, mixed, begun, far, down_proj)


def collect_kernel(p0_ref, p1_ref, p2_ref, p3_ref, own_ref, core_ref, x_ref, far_ref):
    total = p0_ref[...].astype(F32)
    for ref in (p1_ref, p2_ref, p3_ref):
        total += ref[...].astype(F32)
    rows = own_ref.shape[0]
    for k, ref in enumerate((own_ref, core_ref, x_ref, far_ref)):
        ref[...] = total[k * rows : (k + 1) * rows].astype(BF16)


def collect(partials):
    rows, width = partials[0].shape
    return pl.pallas_call(
        collect_kernel,
        in_specs=[whole()] * 4,
        out_specs=[whole()] * 4,
        out_shape=[VMEM((rows // 4, width), BF16)] * 4,
        compiler_params=pltpu.CompilerParams(vmem_limit_bytes=2 * MIB),
        cost_estimate=pl.CostEstimate(
            flops=4 * rows * width, bytes_accessed=8 * rows * width, transcendentals=0
        ),
    )(*partials)


def place_kernel(p0_ref, p1_ref, p2_ref, p3_ref, out_ref):
    place = lax.axis_index("dp")
    width = p0_ref.shape[1]
    for k, ref in enumerate((p0_ref, p1_ref, p2_ref, p3_ref)):
        at = pl.multiple_of(jnp.bitwise_xor(place, k) * width, width)
        out_ref[:, pl.ds(at, width)] = ref[...]


def place_all(pieces):
    rows, width = pieces[0].shape
    return pl.pallas_call(
        place_kernel,
        in_specs=[whole()] * 4,
        out_specs=whole(),
        out_shape=jax.ShapeDtypeStruct((rows, 4 * width), BF16),
        compiler_params=pltpu.CompilerParams(vmem_limit_bytes=2 * MIB),
        cost_estimate=pl.CostEstimate(
            flops=0, bytes_accessed=16 * rows * width, transcendentals=0
        ),
    )(*pieces)


def swap(value, axis, bit):
    size = lax.axis_size(axis)
    return lax.ppermute(value, axis, [(i, i ^ bit) for i in range(size)])


def routed_four(
    hidden_rows,
    expert_ids,
    gate_values,
    gate_proj,
    up_proj,
    down_proj,
    queries,
    latent_cache,
    cache_lengths,
):
    rows_dev, feature_count = hidden_rows.shape
    local_experts = gate_proj.shape[0]
    width = down_proj.shape[2]
    experts_all = local_experts * 4
    capacity = max(2, 3 * rows_dev * expert_ids.shape[1] // (2 * experts_all))
    sent = pack(hidden_rows, expert_ids, gate_values, experts_all)
    along_z = [sent] + [swap(sent, "expert", k) for k in (2, 1, 3)]
    along_z[1:] = [once_done(block, sent, 4 * 10**9) for block in along_z[1:]]
    along_x = [swap(block, "dp", 2) for block in along_z]
    mine_z, mine_x = jnp.stack(along_z), jnp.stack(along_x)
    other_z = swap(mine_z, "dp", 1)
    early = swap(jnp.stack([along_x[0], along_x[2], along_x[3]]), "dp", 1)
    late = swap(along_x[1], "dp", 1)
    other_x = jnp.stack([early[0], late, early[1], early[2]])

    pieces = [block.reshape(4 * rows_dev, -1) for block in (mine_z, other_z, mine_x, other_x)]
    half = local_experts // 2
    hidden_first, table, rank, across = gate_up_first(
        pieces, gate_proj, up_proj, half, 16 * capacity, experts_all
    )
    first_x = swap(hidden_first, "dp", 2)
    hidden_next, hidden, spread = gate_up_next(
        pieces, gate_proj, up_proj, hidden_first, table, rank, across
    )
    next_x = swap(hidden_next, "dp", 2)
    hidden_c = swap(hidden, "dp", 1)
    attended = attend_after(queries, latent_cache, cache_lengths, hidden_next)
    first_x = once_done(first_x, in_hbm(attended))
    first_far = swap(first_x, "dp", 1)
    begun_first = down_part(0, (hidden, hidden_c, first_x), down_proj)
    next_x = once_done(next_x, begun_first)
    next_far = swap(next_x, "dp", 1)
    begun_next, mixed = down_middle(
        half, (next_x, hidden, hidden_c), begun_first, first_far, spread, down_proj
    )
    partial = down_last(half, spread, mixed, begun_next, next_far, down_proj)
    arrived = [partial[0]] + [swap(partial[j], "expert", k) for j, k in ((1, 2), (3, 3), (2, 1))]
    own, to_core, to_x, to_far = collect(arrived)
    far = swap(to_far, "dp", 3)
    blended = place_all((own, swap(to_core, "dp", 1), swap(to_x, "dp", 2), far))
    return blended, attended


def routed_any(hidden_rows, expert_ids, gate_values, gate_proj, up_proj, down_proj):
    rows_dev, feature_count = hidden_rows.shape
    local_experts = gate_proj.shape[0]
    width = down_proj.shape[2]
    owners = lax.axis_size("expert")
    members = lax.axis_size("dp")
    experts_all = local_experts * owners
    table = gate_table(expert_ids, gate_values, experts_all)
    rows = lax.all_gather(hidden_rows, ("expert", "dp"), axis=0, tiled=True)
    table = lax.all_gather(table, ("expert", "dp"), axis=0, tiled=True)
    table = lax.dynamic_slice_in_dim(
        table, lax.axis_index("expert") * local_experts, local_experts, axis=1
    )
    total = jnp.zeros((rows.shape[0], width), F32)
    for e in range(local_experts):
        gate = jnp.dot(rows, gate_proj[e], preferred_element_type=F32)
        up = jnp.dot(rows, up_proj[e], preferred_element_type=F32)
        share = (jax.nn.silu(gate) * up).astype(BF16)
        hidden = lax.all_gather(share, "dp", axis=1, tiled=True)
        made = jnp.dot(hidden, down_proj[e], preferred_element_type=F32).astype(BF16)
        total += table[:, e : e + 1] * made.astype(F32)
    partial = total.astype(BF16).reshape(owners, members, rows_dev, width)
    returned = lax.all_to_all(
        lax.all_to_all(partial, "expert", split_axis=0, concat_axis=0, tiled=True),
        "dp",
        split_axis=1,
        concat_axis=1,
        tiled=True,
    )
    blended = jnp.sum(returned.astype(F32), axis=0).astype(BF16)
    return jnp.transpose(blended, (1, 0, 2)).reshape(rows_dev, members * width)


def local(
    hidden_rows,
    expert_ids,
    gate_values,
    gate_proj,
    up_proj,
    down_proj,
    queries,
    latent_cache,
    cache_lengths,
):
    routing = (hidden_rows, expert_ids, gate_values, gate_proj, up_proj, down_proj)
    attention = (queries, latent_cache, cache_lengths)
    four = lax.axis_size("expert") == 4 and lax.axis_size("dp") == 4
    if four and hidden_rows.shape[0] == 8 and 12 * gate_proj.shape[0] <= 128:
        return routed_four(*routing, *attention)
    return routed_any(*routing), attend(*attention)


def solution(mesh):
    return jax.shard_map(
        local,
        mesh=mesh,
        in_specs=(
            P(("groups", "expert", "dp"), None),
            P(("groups", "expert", "dp"), None),
            P(("groups", "expert", "dp"), None),
            P("expert", None, "dp"),
            P("expert", None, "dp"),
            P("expert", None, "dp"),
            P(("groups", "expert", "dp"), None, None),
            P(("groups", "expert", "dp"), None, None),
            P(("groups", "expert", "dp")),
        ),
        out_specs=(P(("groups", "expert", "dp"), None), P(("groups", "expert", "dp"), None, None)),
        check_vma=False,
    )
```
